256 devices in a mesh: dp: 8 (over x, core), seq: 32 (over y, z).
Axes of the slice: x: 4, y: 4, z: 8, core: 2. Of those that a mesh axis runs over, the one named last changes fastest.
Arguments:
- nodes: bfloat16 [8, 4096, 1024], P('dp', 'seq'), may hold values from -40 to 40
- w_qkv: bfloat16 [1024, 3072], replicated, may hold values from -1 to 1, as said below
- incoming_adjoint: bfloat16 [8, 4096, 1024], P('dp', 'seq'), may hold values from -6 to 6
- block_cols: int32 [8, 32, 4], P('dp'), may hold values from 0 to 31, as said below
- block_counts: int32 [8, 32], P('dp'), may hold values from 1 to 4, as said below
Outputs:
- mixture_output: bfloat16 [8, 4096, 1024], P('dp', 'seq')
- grad_nodes: bfloat16 [8, 4096, 1024], P('dp', 'seq')
- weight_grad: float32 [3072, 1024], P('dp', 'seq')
The draws below stay inside these ranges and needn't reach their ends.
Inputs may be any that keep to these rules, and one draw needn't show every extreme that they name: `block_cols`: slot 0 of row block r names r itself; the 4 slots of a row block name distinct column blocks. `block_counts`: slots at or beyond the count are ignored; in every subgraph some row block uses all 4 slots. `w_qkv`: projection weights.
All inputs are finite; a program needn't handle non-finite values.
Results may differ from the reference program's by a relative error of at most 0.033.
Values may be sent and summed in bfloat16 or wider, within the bound.
A program may use at most 64 MiB of HBM per device.

```python
import math
import jax
import jax.numpy as jnp
from jax import lax

HIDDEN_SPAN = 1024
LENS_TALLY = 32
LENS_FEATURES = 32
TILE_SPAN = 128
PLACE_CEILING = 4
PATCH_VERTICES = 4096
PATCH_TALLY = 8


def block_pattern(key):
    seed_alpha, seed_beta, seed_gamma, seed_delta = jax.random.split(jax.random.fold_in(key, 5), 4)
    tile_tally = PATCH_VERTICES // TILE_SPAN
    stride_progression = jnp.broadcast_to(jnp.arange(1, tile_tally, dtype=jnp.int32), (PATCH_TALLY, tile_tally, tile_tally - 1))
    shuffled = jax.random.permutation(seed_alpha, stride_progression, axis=2, independent=True)
    line_positions = jnp.broadcast_to(jnp.arange(tile_tally, dtype=jnp.int32)[None, :, None], (PATCH_TALLY, tile_tally, 1))
    col_table = jnp.concatenate([line_positions, (line_positions + shuffled[:, :, :PLACE_CEILING - 1]) % tile_tally], axis=2)
    ceiling_bound = jax.random.randint(seed_beta, (PATCH_TALLY, 1), 2, PLACE_CEILING + 1)
    target_tallies = jnp.minimum(jax.random.randint(seed_gamma, (PATCH_TALLY, tile_tally), 1, PLACE_CEILING + 1), ceiling_bound)
    packed_line = jax.random.randint(seed_delta, (PATCH_TALLY, 1), 0, tile_tally)
    target_tallies = jnp.where(jnp.arange(tile_tally, dtype=jnp.int32)[None, :] == packed_line, PLACE_CEILING, target_tallies)
    return (col_table.astype(jnp.int32), target_tallies.astype(jnp.int32))


def draw_block_cols(key, part):
    col_table, target_tallies = block_pattern(key)
    return col_table


def draw_block_counts(key, part):
    col_table, target_tallies = block_pattern(key)
    return target_tallies


def draw_nodes(key, part):
    key = jax.random.fold_in(key, 11)
    seed_alpha = jax.random.fold_in(key, 0)
    uncovered_outcome = jnp.clip(jax.random.normal(seed_alpha, (PATCH_TALLY, PATCH_VERTICES, HIDDEN_SPAN), jnp.float32), -6.0, 6.0)
    return uncovered_outcome.astype(jnp.bfloat16)


def draw_w_qkv(key, part):
    key = jax.random.fold_in(key, 23)
    seed_alpha = jax.random.fold_in(key, 0)
    uncovered_outcome = jnp.clip(jax.random.normal(seed_alpha, (HIDDEN_SPAN, 3 * HIDDEN_SPAN), jnp.float32), -6.0, 6.0) * HIDDEN_SPAN ** (-0.5)
    return jnp.clip(uncovered_outcome, -1.0, 1.0).astype(jnp.bfloat16)


def levels(rng, shape, cuts, smallest, largest):
    def one(axis_at, shards_of):
        draws = jax.random.uniform(jax.random.fold_in(jax.random.fold_in(rng, 6), axis_at), (shards_of,), jnp.float32, smallest / len(cuts), largest / len(cuts))
        return jnp.repeat(jnp.exp(draws), shape[axis_at] // shards_of).reshape((-1,) + (1,) * (len(shape) - axis_at - 1))

    level = one(*cuts[0])
    for cut in cuts[1:]:
        level = level * one(*cut)
    return level


def bell_draw(stream_key, dims, width, most, cuts=(), kind=jnp.bfloat16):
    array = width * jax.random.normal(stream_key, dims, jnp.float32)
    if cuts:
        array = array * levels(stream_key, dims, cuts, -0.22, 0.18)
    return jnp.clip(array, -most, most).astype(kind)


def setup_inputs(seed: int = 0) -> dict:
    key_list = jax.random.split(jax.random.key(seed), 6)
    return {
        "nodes": draw_nodes(jax.random.fold_in(key_list[5], 71), 0),
        "w_qkv": draw_w_qkv(jax.random.fold_in(key_list[5], 71), 0),
        "incoming_adjoint": bell_draw(key_list[2], (PATCH_TALLY, PATCH_VERTICES, HIDDEN_SPAN), 1.0, 6.0, ((0, 8), (1, 32))),
        "block_cols": draw_block_cols(jax.random.fold_in(key_list[5], 71), 0),
        "block_counts": draw_block_counts(jax.random.fold_in(key_list[5], 71), 0),
    }


def attend(queries, key_rows, value_rows, adjoint_vertices, col_table, target_tallies):
    tile_tally = PATCH_VERTICES // TILE_SPAN
    score_scale = 1.0 / math.sqrt(LENS_FEATURES)
    q_blocks = queries.reshape(tile_tally, TILE_SPAN, LENS_FEATURES).astype(jnp.float32)
    key_blocks = key_rows.reshape(tile_tally, TILE_SPAN, LENS_FEATURES)
    value_blocks = value_rows.reshape(tile_tally, TILE_SPAN, LENS_FEATURES)
    keys_now = key_blocks[col_table].reshape(tile_tally, PLACE_CEILING * TILE_SPAN, LENS_FEATURES).astype(jnp.float32)
    values_now = value_blocks[col_table].reshape(tile_tally, PLACE_CEILING * TILE_SPAN, LENS_FEATURES).astype(jnp.float32)
    slot_live = jnp.repeat(jnp.arange(PLACE_CEILING, dtype=jnp.int32)[None, :] < target_tallies[:, None], TILE_SPAN, axis=1)[:, None, :]
    scores = jnp.einsum('rqd,rkd->rqk', q_blocks, keys_now) * score_scale
    scores = jnp.where(slot_live, scores, -jnp.inf)
    weights = jnp.exp(scores - lax.optimization_barrier(jnp.max(scores, axis=-1, keepdims=True)))
    probability = weights / lax.optimization_barrier(jnp.sum(weights, axis=-1, keepdims=True))
    prob_bf = probability.astype(jnp.bfloat16)
    tile_output = jnp.einsum('rqk,rkd->rqd', prob_bf.astype(jnp.float32), values_now).astype(jnp.bfloat16)
    cot_blocks = adjoint_vertices.reshape(tile_tally, TILE_SPAN, LENS_FEATURES).astype(jnp.float32)
    row_delta = lax.optimization_barrier(jnp.sum(cot_blocks * tile_output.astype(jnp.float32), axis=-1, keepdims=True))
    value_part = jnp.einsum('rqk,rqd->rkd', prob_bf.astype(jnp.float32), cot_blocks)
    grad_prob = jnp.einsum('rqd,rkd->rqk', cot_blocks, values_now)
    grad_score = (probability * (grad_prob - row_delta) * score_scale).astype(jnp.bfloat16)
    deriv_request = jnp.einsum('rqk,rkd->rqd', grad_score.astype(jnp.float32), keys_now).astype(jnp.bfloat16)
    key_part = jnp.einsum('rqk,rqd->rkd', grad_score.astype(jnp.float32), q_blocks)
    flat_cols = col_table.reshape(-1).astype(jnp.int32)
    empty = jnp.zeros((tile_tally, TILE_SPAN, LENS_FEATURES), jnp.float32)
    lookup_totals = empty.at[flat_cols].add(key_part.reshape(tile_tally * PLACE_CEILING, TILE_SPAN, LENS_FEATURES))
    payload_totals = empty.at[flat_cols].add(value_part.reshape(tile_tally * PLACE_CEILING, TILE_SPAN, LENS_FEATURES))
    return (tile_output.reshape(PATCH_VERTICES, LENS_FEATURES), deriv_request.reshape(PATCH_VERTICES, LENS_FEATURES), lookup_totals.astype(jnp.bfloat16).reshape(PATCH_VERTICES, LENS_FEATURES), payload_totals.astype(jnp.bfloat16).reshape(PATCH_VERTICES, LENS_FEATURES))

def reference(nodes, w_qkv, incoming_adjoint, block_cols, block_counts):

    def one_graph(carry, inputs_now):
        features, adjoint_vertices, col_table, target_tallies = inputs_now
        mapped_vectors = jnp.dot(features, w_qkv, preferred_element_type=jnp.float32).astype(jnp.bfloat16)
        lensewise = mapped_vectors.reshape(PATCH_VERTICES, 3, LENS_TALLY, LENS_FEATURES).transpose(2, 1, 0, 3)
        adjoint_lenses = adjoint_vertices.reshape(PATCH_VERTICES, LENS_TALLY, LENS_FEATURES).transpose(1, 0, 2)

        def head_work(pieces):
            stacked, cot_one = pieces
            return attend(stacked[0], stacked[1], stacked[2], cot_one, col_table, target_tallies)
        lens_output, deriv_asking, deriv_lookup, deriv_payload = lax.map(head_work, (lensewise, adjoint_lenses))
        mixture_output = lens_output.transpose(1, 0, 2).reshape(PATCH_VERTICES, HIDDEN_SPAN)
        flattened_derivs = jnp.stack([deriv_asking, deriv_lookup, deriv_payload], axis=0).transpose(2, 0, 1, 3).reshape(PATCH_VERTICES, 3 * HIDDEN_SPAN)
        grad_nodes = lax.dot_general(flattened_derivs, w_qkv, (((1,), (1,)), ((), ())), preferred_element_type=jnp.float32).astype(jnp.bfloat16)
        carry = carry + lax.dot_general(flattened_derivs, features, (((0,), (0,)), ((), ())), preferred_element_type=jnp.float32)
        return (carry, (mixture_output, grad_nodes))
    start_grad = jnp.zeros((3 * HIDDEN_SPAN, HIDDEN_SPAN), jnp.float32)
    weight_grad, (mixture_output, grad_nodes) = lax.scan(one_graph, start_grad, (nodes, incoming_adjoint, block_cols, block_counts))
    return (mixture_output, grad_nodes, weight_grad)
```

```python
import functools
import math

import jax
import jax.numpy as jnp
from jax import lax
from jax.experimental import pallas as pl
from jax.experimental.pallas import tpu as pltpu
from jax.sharding import PartitionSpec as P

MESH = pl.DeviceIdType.MESH
BLK = 128
FEAT = 32
SLOTS = 4
F32 = jnp.float32
BF16 = jnp.bfloat16
VMEM_LIMIT = 48 * 1024 * 1024


def lane_ids(shape):
    return lax.broadcasted_iota(jnp.int32, shape, len(shape) - 1)


def swap_quarters(tiles):
    lane = lane_ids(tiles[0].shape)
    low = lane < 64
    even = (lane // 32) % 2 == 0
    a0, a1, a2, a3 = tiles
    b0 = jnp.where(low, a0, pltpu.roll(a2, 64, 1))
    b2 = jnp.where(low, pltpu.roll(a0, 64, 1), a2)
    b1 = jnp.where(low, a1, pltpu.roll(a3, 64, 1))
    b3 = jnp.where(low, pltpu.roll(a1, 64, 1), a3)
    return (
        jnp.where(even, b0, pltpu.roll(b1, 32, 1)),
        jnp.where(even, pltpu.roll(b0, 96, 1), b1),
        jnp.where(even, b2, pltpu.roll(b3, 32, 1)),
        jnp.where(even, pltpu.roll(b2, 96, 1), b3),
    )


def greet(me_d, me_s, nd, ns):
    barrier = pltpu.get_barrier_semaphore()

    def seq_hello(k, c):
        pl.semaphore_signal(
            barrier, inc=1, device_id=(me_d, lax.rem(me_s + k, ns)), device_id_type=MESH
        )
        return c

    def dp_hello(k, c):
        pl.semaphore_signal(
            barrier, inc=1, device_id=(lax.rem(me_d + k, nd), me_s), device_id_type=MESH
        )
        return c

    lax.fori_loop(1, ns, seq_hello, 0)
    lax.fori_loop(1, nd, dp_hello, 0)
    return barrier


def peer_at(me_s, i, j, ng, sign):
    group = lax.rem(me_s // 4 + sign * i + ng, ng)
    return 4 * group + lax.rem(me_s % 4 + sign * j + 4, 4)


def spread_kernel(
    nd, ns, x_ref, w_ref, do_ref, recv_ref, xt_all, w_vm, send_buf, xt_vm,
    w_sem, send_sem, recv_sem, xs_sem, xr_sem, own_sem,
):
    me_d, me_s = lax.axis_index("dp"), lax.axis_index("seq")
    ng = ns // 4
    my_group = me_s // 4

    def w_copy(i, m):
        g = lax.rem(my_group + i, ng)
        return pltpu.make_async_copy(
            w_ref.at[:, pl.ds(pl.multiple_of((m * ng + g) * BLK, BLK), BLK)],
            w_vm.at[i, :, pl.ds(m * BLK, BLK)],
            w_sem.at[i, m],
        )

    def w_start(i, c):
        for m in range(3):
            w_copy(i, m).start()
        return c

    lax.fori_loop(0, ng, w_start, 0)
    barrier = greet(me_d, me_s, nd, ns)
    xt_vm[...] = jnp.transpose(x_ref[...].astype(F32)).astype(BF16)

    def xt_slot(d):
        return xt_all.at[:, pl.ds(pl.multiple_of(d * BLK, BLK), BLK)]

    def xt_copy(k):
        return pltpu.make_async_remote_copy(
            src_ref=xt_vm,
            dst_ref=xt_slot(me_d),
            send_sem=xs_sem.at[k],
            recv_sem=xr_sem.at[k],
            device_id=(lax.rem(me_d + k, nd), me_s),
            device_id_type=MESH,
        )

    def head_copy(i, j):
        peer = peer_at(me_s, i, j, ng, 1)
        return pltpu.make_async_remote_copy(
            src_ref=send_buf.at[peer],
            dst_ref=recv_ref.at[me_s],
            send_sem=send_sem.at[i, j],
            recv_sem=recv_sem.at[i, j],
            device_id=(me_d, peer),
            device_id_type=MESH,
        )

    own_head = pltpu.make_async_copy(send_buf.at[me_s], recv_ref.at[me_s], own_sem.at[0])
    own_xt = pltpu.make_async_copy(xt_vm, xt_slot(me_d), own_sem.at[1])

    def project(i, c):
        g = lax.rem(my_group + i, ng)
        for m in range(3):
            w_copy(i, m).wait()
        qkv = jnp.dot(x_ref[...], w_vm[i], preferred_element_type=F32).astype(BF16)
        cot = do_ref[:, pl.ds(pl.multiple_of(g * BLK, BLK), BLK)]
        packed = swap_quarters(
            (qkv[:, :BLK], qkv[:, BLK : 2 * BLK], qkv[:, 2 * BLK :], cot)
        )
        for j in range(4):
            send_buf[4 * g + j] = packed[j]

        @pl.when(i == 0)
        def _():
            pl.semaphore_wait(barrier, ns + nd - 2)
            own_head.start()
            own_xt.start()

            def xt_start(k, c):
                xt_copy(k).start()
                return c

            lax.fori_loop(1, nd, xt_start, 0)

        @pl.when(i > 0)
        def _():
            head_copy(i, 0).start()

        for j in range(1, 4):
            head_copy(i, j).start()
        return c

    lax.fori_loop(0, ng, project, 0)
    own_head.wait()
    own_xt.wait()

    def finish(i, c):
        @pl.when(i > 0)
        def _():
            head_copy(i, 0).wait()

        for j in range(1, 4):
            head_copy(i, j).wait()
        return c

    lax.fori_loop(0, ng, finish, 0)

    def xt_wait(k, c):
        xt_copy(k).wait()
        return c

    lax.fori_loop(1, nd, xt_wait, 0)


def attend_kernel(nb, cols_ref, counts_ref, a_ref, out_ref, kvt, acc):
    scale = 1.0 / math.sqrt(FEAT)
    to_exp2 = scale * math.log2(math.e)
    lane = lane_ids((BLK, BLK))

    def prepare(b, c):
        kvt[b] = jnp.transpose(a_ref[b].astype(F32))[FEAT : 3 * FEAT].astype(BF16)
        acc[b] = jnp.zeros((BLK, BLK), F32)
        return c

    lax.fori_loop(0, nb, prepare, 0)

    def row_block(r, c):
        mine = a_ref[r]
        zero = jnp.zeros_like(mine)
        quarter = lane // FEAT
        left = jnp.concatenate(
            [
                jnp.where(quarter == 1, pltpu.roll(mine, 32, 1), zero),
                jnp.where(quarter == 2, pltpu.roll(mine, 96, 1), zero),
            ],
            axis=0,
        )
        right = jnp.concatenate(
            [
                jnp.where(quarter == 3, mine, zero),
                jnp.where(quarter == 2, pltpu.roll(mine, 64, 1), zero),
            ],
            axis=0,
        )
        count = counts_ref[r]
        named = [cols_ref[r * SLOTS + s] for s in range(SLOTS)]
        keys = jnp.concatenate([a_ref[n] for n in named], axis=0)
        both = lax.dot_general(
            keys, left, (((1,), (1,)), ((), ())), preferred_element_type=F32
        )
        scores = [
            jnp.where(s < count, both[s * BLK : (s + 1) * BLK, :BLK], -jnp.inf)
            for s in range(SLOTS)
        ]
        scores = jnp.concatenate(scores, axis=0)
        grad_prob = both[:, BLK:]
        top = jnp.max(scores, axis=0, keepdims=True)
        weights = jnp.exp2((scores - top) * to_exp2)
        prob = weights * (1.0 / jnp.sum(weights, axis=0, keepdims=True))
        delta = jnp.sum(prob * grad_prob, axis=0, keepdims=True)
        grad_score = prob * (grad_prob - delta) * scale
        pair = jnp.concatenate([prob.astype(BF16), grad_score.astype(BF16)], axis=1)
        key_side = jnp.dot(pair, right, preferred_element_type=F32)
        for s in range(SLOTS):
            acc[named[s]] += key_side[s * BLK : (s + 1) * BLK]
        turned = jnp.concatenate([kvt[n] for n in named], axis=1)
        row_side = jnp.dot(turned, pair, preferred_element_type=F32)
        row_side = jnp.concatenate(
            [row_side[FEAT:, :BLK], row_side[:FEAT, BLK:], jnp.zeros((2 * FEAT, BLK), F32)],
            axis=0,
        )
        acc[r] += jnp.transpose(row_side)
        return c

    lax.fori_loop(0, nb, row_block, 0)

    def emit(b, c):
        out_ref[b] = acc[b].astype(BF16)
        return c

    lax.fori_loop(0, nb, emit, 0)


def return_kernel(
    nd, ns, ny, nz, tpd, ret_ref, w_ref, xt_ref, mix_ref, gn_ref, wg_ref,
    ret_in, w_vm, xt_vm, dq, wg_in, part, rs_y, mid, rs_z,
    load_sem, send_sem, recv_sem, own_sem, ts_sem, tr_sem, to_sem,
    ys_sem, yr_sem, zs_sem, zr_sem,
):
    me_d, me_s = lax.axis_index("dp"), lax.axis_index("seq")
    me_y, me_z = me_s // nz, me_s % nz
    ng = ns // 4
    hidden = ng * BLK
    load_w = pltpu.make_async_copy(w_ref, w_vm, load_sem.at[0])
    load_xt = pltpu.make_async_copy(xt_ref, xt_vm, load_sem.at[1])
    own = pltpu.make_async_copy(ret_ref.at[me_s], ret_in.at[me_s], own_sem.at[0])
    own.start()
    load_xt.start()
    load_w.start()
    barrier = greet(me_d, me_s, nd, ns)

    def back_copy(i, j):
        peer = peer_at(me_s, i, j, ng, 1)
        return pltpu.make_async_remote_copy(
            src_ref=ret_ref.at[peer],
            dst_ref=ret_in.at[me_s],
            send_sem=send_sem.at[i, j],
            recv_sem=recv_sem.at[i, j],
            device_id=(me_d, peer),
            device_id_type=MESH,
        )

    pl.semaphore_wait(barrier, ns + nd - 2)

    def back_start(i, c):
        @pl.when(i > 0)
        def _():
            back_copy(i, 0).start()

        for j in range(1, 4):
            back_copy(i, j).start()
        return c

    lax.fori_loop(0, ng, back_start, 0)

    def tile_rows(d):
        return pl.ds(pl.multiple_of(d * BLK, BLK), BLK)

    def lanes(t):
        return pl.ds(pl.multiple_of(t * BLK, BLK), BLK)

    def tile_own(t):
        return pltpu.make_async_copy(
            dq.at[:, lanes(t)], wg_in.at[t % tpd, tile_rows(me_d)], to_sem.at[t % tpd]
        )

    def tile_copy(t):
        return pltpu.make_async_remote_copy(
            src_ref=dq.at[:, lanes(t)],
            dst_ref=wg_in.at[t % tpd, tile_rows(me_d)],
            send_sem=ts_sem.at[t],
            recv_sem=tr_sem.at[me_d, t % tpd],
            device_id=(t // tpd, me_s),
            device_id_type=MESH,
        )

    def gather(i, c):
        g = lax.rem(me_s // 4 - i + ng, ng)

        @pl.when(i == 0)
        def _():
            own.wait()

        @pl.when(i > 0)
        def _():
            back_copy(i, 0).wait_recv()

        for j in range(1, 4):
            back_copy(i, j).wait_recv()
        mix, d_q, d_k, d_v = swap_quarters(tuple(ret_in[4 * g + j] for j in range(4)))
        mix_ref[:, lanes(g)] = mix
        for m, tile in enumerate((d_q, d_k, d_v)):
            t = m * ng + g
            dq[:, lanes(t)] = tile

            @pl.when(t // tpd == me_d)
            def _():
                tile_own(t).start()

            @pl.when(t // tpd != me_d)
            def _():
                tile_copy(t).start()

        return c

    lax.fori_loop(0, ng, gather, 0)
    load_xt.wait()

    def y_copy(t, k):
        to = lax.rem(me_y + k, ny)
        return pltpu.make_async_remote_copy(
            src_ref=part.at[t, pl.ds(pl.multiple_of(to * nz * FEAT, FEAT), nz * FEAT)],
            dst_ref=rs_y.at[t, k - 1],
            send_sem=ys_sem.at[t, k],
            recv_sem=yr_sem.at[t, k],
            device_id=(me_d, to * nz + me_z),
            device_id_type=MESH,
        )

    def z_copy(t, k):
        to = lax.rem(me_z + k, nz)
        return pltpu.make_async_remote_copy(
            src_ref=mid.at[t, pl.ds(pl.multiple_of(to * FEAT, FEAT), FEAT)],
            dst_ref=rs_z.at[t, k - 1],
            send_sem=zs_sem.at[t, k],
            recv_sem=zr_sem.at[t, k],
            device_id=(me_d, me_y * nz + to),
            device_id_type=MESH,
        )

    def tile_done(t, k):
        src = lax.rem(me_d + k, nd)
        return pltpu.make_async_remote_copy(
            src_ref=dq.at[:, lanes(0)],
            dst_ref=wg_in.at[t, tile_rows(src)],
            send_sem=ts_sem.at[0],
            recv_sem=tr_sem.at[src, t],
            device_id=(src, me_s),
            device_id_type=MESH,
        )

    for t in range(tpd):
        tile_own(me_d * tpd + t).wait()

        def arrived(k, c):
            tile_done(t, k).wait_recv()
            return c

        lax.fori_loop(1, nd, arrived, 0)
        part[t] = jnp.dot(xt_vm[...], wg_in[t], preferred_element_type=F32).astype(BF16)
        for k in range(1, ny):
            y_copy(t, k).start()

    load_w.wait()

    def node_cols(n, c):
        cols = pl.ds(pl.multiple_of(n * 2 * BLK, 2 * BLK), 2 * BLK)
        gn_ref[:, cols] = lax.dot_general(
            dq[...], w_vm[cols, :], (((1,), (1,)), ((), ())), preferred_element_type=F32
        ).astype(BF16)
        return c

    lax.fori_loop(0, hidden // (2 * BLK), node_cols, 0)

    for t in range(tpd):
        total = part[t, pl.ds(pl.multiple_of(me_y * nz * FEAT, FEAT), nz * FEAT)].astype(F32)
        for k in range(1, ny):
            y_copy(t, k).wait_recv()
            total += rs_y[t, k - 1].astype(F32)
        mid[t] = total.astype(BF16)
        for k in range(1, nz):
            z_copy(t, k).start()

    for t in range(tpd):
        total = mid[t, pl.ds(pl.multiple_of(me_z * FEAT, FEAT), FEAT)].astype(F32)
        for k in range(1, nz):
            z_copy(t, k).wait_recv()
            total += rs_z[t, k - 1].astype(F32)
        wg_ref[:, pl.ds(t * BLK, BLK)] = total

    def back_sent(i, c):
        @pl.when(i > 0)
        def _():
            back_copy(i, 0).wait_send()

        for j in range(1, 4):
            back_copy(i, j).wait_send()
        return c

    lax.fori_loop(0, ng, back_sent, 0)

    def tile_sent(t, c):
        @pl.when(t // tpd != me_d)
        def _():
            tile_copy(t).wait_send()

        return c

    lax.fori_loop(0, 3 * ng, tile_sent, 0)
    for t in range(tpd):
        for k in range(1, ny):
            y_copy(t, k).wait_send()
        for k in range(1, nz):
            z_copy(t, k).wait_send()


def per_device(nd, ns, nodes, w_qkv, incoming_adjoint, block_cols, block_counts):
    rows, hidden = nodes.shape[1:]
    ny, nz = 4, ns // 4
    ng = ns // 4
    tpd = 3 * ng // nd
    any_spec = pl.BlockSpec(memory_space=pl.ANY)
    vm_spec = pl.BlockSpec(memory_space=pltpu.VMEM)
    sm_spec = pl.BlockSpec(memory_space=pltpu.SMEM)
    dma = pltpu.SemaphoreType.DMA
    packed, xt_all = pl.pallas_call(
        functools.partial(spread_kernel, nd, ns),
        out_shape=(
            jax.ShapeDtypeStruct((ns, BLK, BLK), BF16),
            jax.ShapeDtypeStruct((hidden, nd * BLK), BF16),
        ),
        in_specs=[vm_spec, any_spec, vm_spec],
        out_specs=(any_spec, any_spec),
        scratch_shapes=[
            pltpu.VMEM((ng, hidden, 3 * BLK), BF16),
            pltpu.VMEM((ns, BLK, BLK), BF16),
            pltpu.VMEM((hidden, BLK), BF16),
            dma((ng, 3)),
            dma((ng, 4)),
            dma((ng, 4)),
            dma((nd,)),
            dma((nd,)),
            dma((2,)),
        ],
        compiler_params=pltpu.CompilerParams(
            collective_id=1, has_side_effects=True, vmem_limit_bytes=VMEM_LIMIT
        ),
        name="spread",
    )(nodes[0], w_qkv, incoming_adjoint[0])
    returned = pl.pallas_call(
        functools.partial(attend_kernel, ns),
        out_shape=jax.ShapeDtypeStruct((ns, BLK, BLK), BF16),
        in_specs=[sm_spec, sm_spec, vm_spec],
        out_specs=vm_spec,
        scratch_shapes=[
            pltpu.VMEM((ns, 2 * FEAT, BLK), BF16),
            pltpu.VMEM((ns, BLK, BLK), F32),
        ],
        compiler_params=pltpu.CompilerParams(vmem_limit_bytes=VMEM_LIMIT),
        name="attend",
    )(block_cols[0].reshape(-1), block_counts[0], packed)
    mixture, grad_nodes, weight_grad = pl.pallas_call(
        functools.partial(return_kernel, nd, ns, ny, nz, tpd),
        out_shape=(
            jax.ShapeDtypeStruct((rows, hidden), BF16),
            jax.ShapeDtypeStruct((rows, hidden), BF16),
            jax.ShapeDtypeStruct((FEAT, tpd * BLK), F32),
        ),
        in_specs=[any_spec, any_spec, any_spec],
        out_specs=(vm_spec, vm_spec, vm_spec),
        scratch_shapes=[
            pltpu.VMEM((ns, BLK, BLK), BF16),
            pltpu.VMEM((hidden, 3 * hidden), BF16),
            pltpu.VMEM((hidden, nd * BLK), BF16),
            pltpu.VMEM((rows, 3 * hidden), BF16),
            pltpu.VMEM((tpd, nd * BLK, BLK), BF16),
            pltpu.VMEM((tpd, hidden, BLK), BF16),
            pltpu.VMEM((tpd, ny - 1, nz * FEAT, BLK), BF16),
            pltpu.VMEM((tpd, nz * FEAT, BLK), BF16),
            pltpu.VMEM((tpd, nz - 1, FEAT, BLK), BF16),
            dma((2,)),
            dma((ng, 4)),
            dma((ng, 4)),
            dma((1,)),
            dma((3 * ng,)),
            dma((nd, tpd)),
            dma((tpd,)),
            dma((tpd, ny)),
            dma((tpd, ny)),
            dma((tpd, nz)),
            dma((tpd, nz)),
        ],
        compiler_params=pltpu.CompilerParams(
            collective_id=2, has_side_effects=True, vmem_limit_bytes=VMEM_LIMIT
        ),
        name="give_back",
    )(returned, w_qkv, xt_all)
    return (mixture[None], grad_nodes[None], jnp.transpose(weight_grad))


def solution(mesh):
    nd, ns = mesh.shape["dp"], mesh.shape["seq"]
    in_specs = (P("dp", "seq", None), P(), P("dp", "seq", None), P("dp", None, None), P("dp", None))
    out_specs = (P("dp", "seq", None), P("dp", "seq", None), P("dp", "seq"))
    return jax.shard_map(
        functools.partial(per_device, nd, ns),
        mesh=mesh,
        in_specs=in_specs,
        out_specs=out_specs,
        check_vma=False,
    )
```

```python
import functools
import math

import jax
import jax.numpy as jnp
from jax import lax
from jax.experimental import pallas as pl
from jax.experimental.pallas import tpu as pltpu
from jax.sharding import PartitionSpec as P

MESH = pl.DeviceIdType.MESH
BLK = 128
FEAT = 32
SLOTS = 4
F32 = jnp.float32
BF16 = jnp.bfloat16
VMEM_LIMIT = 62 * 1024 * 1024


def lane_ids(shape):
    return lax.broadcasted_iota(jnp.int32, shape, len(shape) - 1)


def swap_quarters(tiles):
    lane = lane_ids(tiles[0].shape)
    low = lane < 64
    even = (lane // 32) % 2 == 0
    a0, a1, a2, a3 = tiles
    b0 = jnp.where(low, a0, pltpu.roll(a2, 64, 1))
    b2 = jnp.where(low, pltpu.roll(a0, 64, 1), a2)
    b1 = jnp.where(low, a1, pltpu.roll(a3, 64, 1))
    b3 = jnp.where(low, pltpu.roll(a1, 64, 1), a3)
    return (
        jnp.where(even, b0, pltpu.roll(b1, 32, 1)),
        jnp.where(even, pltpu.roll(b0, 96, 1), b1),
        jnp.where(even, b2, pltpu.roll(b3, 32, 1)),
        jnp.where(even, pltpu.roll(b2, 96, 1), b3),
    )


def greet(me_d, me_s, nd, ns):
    barrier = pltpu.get_barrier_semaphore()

    def seq_hello(k, c):
        pl.semaphore_signal(
            barrier, inc=1, device_id=(me_d, lax.rem(me_s + k, ns)), device_id_type=MESH
        )
        return c

    def dp_hello(k, c):
        pl.semaphore_signal(
            barrier, inc=1, device_id=(lax.rem(me_d + k, nd), me_s), device_id_type=MESH
        )
        return c

    lax.fori_loop(1, ns, seq_hello, 0)
    lax.fori_loop(1, nd, dp_hello, 0)
    return barrier


def peer_at(me_s, i, j, ng, sign):
    group = lax.rem(me_s // 4 + sign * i + ng, ng)
    return 4 * group + lax.rem(me_s % 4 + sign * j + 4, 4)


def spread_kernel(
    nd, ns, x_in, w_ref, do_in, recv_ref, xt_all, x_ref, do_ref, w_vm, send_buf, xt_vm,
    w_sem, send_sem, recv_sem, xs_sem, xr_sem, own_sem,
):
    me_d, me_s = lax.axis_index("dp"), lax.axis_index("seq")
    ng = ns // 4
    my_group = me_s // 4

    def w_copy(i, m):
        g = lax.rem(my_group + i, ng)
        return pltpu.make_async_copy(
            w_ref.at[:, pl.ds(pl.multiple_of((m * ng + g) * BLK, BLK), BLK)],
            w_vm.at[i, :, pl.ds(m * BLK, BLK)],
            w_sem.at[i, m],
        )

    def w_start(i, c):
        for m in range(3):
            w_copy(i, m).start()
        return c

    load_x = pltpu.make_async_copy(x_in.at[0], x_ref, own_sem.at[2])
    load_do = pltpu.make_async_copy(do_in.at[0], do_ref, own_sem.at[3])
    load_x.start()
    load_do.start()
    lax.fori_loop(0, ng, w_start, 0)
    barrier = greet(me_d, me_s, nd, ns)
    load_x.wait()
    load_do.wait()
    xt_vm[...] = jnp.transpose(x_ref[...].astype(F32)).astype(BF16)

    def xt_slot(d):
        return xt_all.at[:, pl.ds(pl.multiple_of(d * BLK, BLK), BLK)]

    def xt_copy(k):
        return pltpu.make_async_remote_copy(
            src_ref=xt_vm,
            dst_ref=xt_slot(me_d),
            send_sem=xs_sem.at[k],
            recv_sem=xr_sem.at[k],
            device_id=(lax.rem(me_d + k, nd), me_s),
            device_id_type=MESH,
        )

    def head_copy(i, j):
        peer = peer_at(me_s, i, j, ng, 1)
        return pltpu.make_async_remote_copy(
            src_ref=send_buf.at[peer],
            dst_ref=recv_ref.at[me_s],
            send_sem=send_sem.at[i, j],
            recv_sem=recv_sem.at[i, j],
            device_id=(me_d, peer),
            device_id_type=MESH,
        )

    own_head = pltpu.make_async_copy(send_buf.at[me_s], recv_ref.at[me_s], own_sem.at[0])
    own_xt = pltpu.make_async_copy(xt_vm, xt_slot(me_d), own_sem.at[1])

    def project(i, c):
        g = lax.rem(my_group + i, ng)
        for m in range(3):
            w_copy(i, m).wait()
        qkv = jnp.dot(x_ref[...], w_vm[i], preferred_element_type=F32).astype(BF16)
        cot = do_ref[:, pl.ds(pl.multiple_of(g * BLK, BLK), BLK)]
        packed = swap_quarters(
            (qkv[:, :BLK], qkv[:, BLK : 2 * BLK], qkv[:, 2 * BLK :], cot)
        )
        for j in range(4):
            send_buf[4 * g + j] = packed[j]

        @pl.when(i == 0)
        def _():
            pl.semaphore_wait(barrier, ns + nd - 2)
            own_head.start()
            own_xt.start()

            def xt_start(k, c):
                xt_copy(k).start()
                return c

            lax.fori_loop(1, nd, xt_start, 0)

        @pl.when(i > 0)
        def _():
            head_copy(i, 0).start()

        for j in range(1, 4):
            head_copy(i, j).start()
        return c

    lax.fori_loop(0, ng, project, 0)
    own_head.wait()
    own_xt.wait()

    def finish(i, c):
        @pl.when(i > 0)
        def _():
            head_copy(i, 0).wait()

        for j in range(1, 4):
            head_copy(i, j).wait()
        return c

    lax.fori_loop(0, ng, finish, 0)

    def xt_wait(k, c):
        xt_copy(k).wait()
        return c

    lax.fori_loop(1, nd, xt_wait, 0)


def attend_kernel(
    nb, cols_ref, counts_ref, a_ref, out_ref, turned_kv, left, right, col_acc, row_out,
    raw_even, raw_odd, top_even, top_odd, pair_even, pair_odd,
):
    scale = 1.0 / math.sqrt(FEAT)
    to_exp2 = scale * math.log2(math.e)
    raw, top, pair = (raw_even, raw_odd), (top_even, top_odd), (pair_even, pair_odd)
    quarter = lane_ids((BLK, BLK)) // FEAT

    def prepare(b, c):
        mine = a_ref[b]
        zero = jnp.zeros_like(mine)
        turned = jnp.transpose(mine.astype(F32)).astype(BF16)
        empty = jnp.zeros((FEAT, BLK), BF16)
        turned_kv[b] = turned[FEAT : 3 * FEAT]
        left[b, :BLK] = jnp.where(quarter == 1, pltpu.roll(mine, 32, 1), zero)
        left[b, BLK:] = jnp.where(quarter == 2, pltpu.roll(mine, 96, 1), zero)
        right[b, :FEAT, :BLK] = empty
        right[b, :FEAT, BLK:] = turned[:FEAT]
        right[b, FEAT:, :BLK] = turned[3 * FEAT :]
        right[b, FEAT:, BLK:] = empty
        col_acc[b] = jnp.zeros((2 * FEAT, BLK), F32)
        return c

    lax.fori_loop(0, nb, prepare, 0, unroll=2)

    def score_stage(r, p):
        count = counts_ref[0, r]
        keys = jnp.concatenate([a_ref[cols_ref[0, s, r]] for s in range(SLOTS)], axis=0)
        both = lax.dot_general(
            keys, left[r], (((1,), (1,)), ((), ())), preferred_element_type=F32
        )
        best = None
        for s in range(SLOTS):
            block = both[s * BLK : (s + 1) * BLK]
            scores = block[:, :BLK]
            if s:
                scores = jnp.where(s < count, scores, -jnp.inf)
            raw[p][s, :, :BLK] = scores
            raw[p][s, :, BLK:] = block[:, BLK:]
            peak = jnp.max(scores, axis=0, keepdims=True)
            best = peak if best is None else jnp.maximum(best, peak)
        top[p][...] = best * to_exp2

    def soft_stage(p):
        peak = top[p][...]
        total = mixed = None
        for s in range(SLOTS):
            weights = jnp.exp2(raw[p][s, :, :BLK] * to_exp2 - peak)
            t = jnp.sum(weights, axis=0, keepdims=True)
            m = jnp.sum(weights * raw[p][s, :, BLK:], axis=0, keepdims=True)
            total = t if total is None else total + t
            mixed = m if mixed is None else mixed + m
            raw[p][s, :, :BLK] = weights
        inverse = 1.0 / total
        delta = mixed * inverse
        for s in range(SLOTS):
            prob = raw[p][s, :, :BLK] * inverse
            rows = slice(s * BLK, (s + 1) * BLK)
            pair[p][rows, :BLK] = prob.astype(BF16)
            pair[p][rows, BLK:] = (prob * (raw[p][s, :, BLK:] - delta)).astype(BF16)

    def grad_stage(r, p):
        named = [cols_ref[0, s, r] for s in range(SLOTS)]
        both = pair[p][...]
        turned = jnp.concatenate([turned_kv[n] for n in named], axis=1)
        row_side = jnp.dot(turned, both, preferred_element_type=F32)
        row_out[r, :FEAT] = row_side[FEAT:, :BLK]
        row_out[r, FEAT:] = row_side[:FEAT, BLK:]
        key_side = lax.dot_general(
            right[r], both, (((1,), (1,)), ((), ())), preferred_element_type=F32
        )
        for s in range(SLOTS):
            col_acc[named[s]] += key_side[:, s * BLK : (s + 1) * BLK]

    score_stage(0, 0)
    score_stage(1, 1)
    soft_stage(0)

    def steps(i, c):
        for u in range(2):
            r, p = 1 + 2 * i + u, (1 + u) % 2
            score_stage(r + 1, 1 - p)
            soft_stage(p)
            grad_stage(r - 1, 1 - p)
        return c

    lax.fori_loop(0, (nb - 2) // 2, steps, 0)
    soft_stage(1)
    grad_stage(nb - 2, 0)
    grad_stage(nb - 1, 1)
    part = lax.broadcasted_iota(jnp.int32, (BLK, BLK), 0) // FEAT
    factor = jnp.where((part == 1) | (part == 2), scale, 1.0).astype(F32)

    def emit(b, c):
        whole = jnp.concatenate([row_out[b], col_acc[b]], axis=0) * factor
        out_ref[b] = jnp.transpose(whole).astype(BF16)
        return c

    lax.fori_loop(0, nb, emit, 0, unroll=2)


def return_kernel(
    nd, ns, ny, nz, tpd, ret_ref, w_ref, xt_ref, mix_ref, gn_ref, wg_ref,
    ret_in, w_vm, xt_vm, dq, wg_in, part, rs_y, mid, rs_z,
    load_sem, send_sem, recv_sem, own_sem, ts_sem, tr_sem, to_sem,
    ys_sem, yr_sem, zs_sem, zr_sem,
):
    me_d, me_s = lax.axis_index("dp"), lax.axis_index("seq")
    me_y, me_z = me_s // nz, me_s % nz
    ng = ns // 4
    hidden = ng * BLK
    load_w = pltpu.make_async_copy(w_ref, w_vm, load_sem.at[0])
    load_xt = pltpu.make_async_copy(xt_ref, xt_vm, load_sem.at[1])
    own = pltpu.make_async_copy(ret_ref.at[me_s], ret_in.at[me_s], own_sem.at[0])
    own.start()
    load_xt.start()
    load_w.start()
    barrier = greet(me_d, me_s, nd, ns)

    def back_copy(i, j):
        peer = peer_at(me_s, i, j, ng, 1)
        return pltpu.make_async_remote_copy(
            src_ref=ret_ref.at[peer],
            dst_ref=ret_in.at[me_s],
            send_sem=send_sem.at[i, j],
            recv_sem=recv_sem.at[i, j],
            device_id=(me_d, peer),
            device_id_type=MESH,
        )

    pl.semaphore_wait(barrier, ns + nd - 2)

    def back_start(i, c):
        @pl.when(i > 0)
        def _():
            back_copy(i, 0).start()

        for j in range(1, 4):
            back_copy(i, j).start()
        return c

    lax.fori_loop(0, ng, back_start, 0)

    def tile_rows(d):
        return pl.ds(pl.multiple_of(d * BLK, BLK), BLK)

    def lanes(t):
        return pl.ds(pl.multiple_of(t * BLK, BLK), BLK)

    def tile_own(t):
        return pltpu.make_async_copy(
            dq.at[:, lanes(t)], wg_in.at[t % tpd, tile_rows(me_d)], to_sem.at[t % tpd]
        )

    def tile_copy(t):
        return pltpu.make_async_remote_copy(
            src_ref=dq.at[:, lanes(t)],
            dst_ref=wg_in.at[t % tpd, tile_rows(me_d)],
            send_sem=ts_sem.at[t],
            recv_sem=tr_sem.at[me_d, t % tpd],
            device_id=(t // tpd, me_s),
            device_id_type=MESH,
        )

    def gather(i, c):
        g = lax.rem(me_s // 4 - i + ng, ng)

        @pl.when(i == 0)
        def _():
            own.wait()

        @pl.when(i > 0)
        def _():
            back_copy(i, 0).wait_recv()

        for j in range(1, 4):
            back_copy(i, j).wait_recv()
        mix, d_q, d_k, d_v = swap_quarters(tuple(ret_in[4 * g + j] for j in range(4)))
        mix_ref[:, lanes(g)] = mix
        for m, tile in enumerate((d_q, d_k, d_v)):
            t = m * ng + g
            dq[:, lanes(t)] = tile

            @pl.when(t // tpd == me_d)
            def _():
                tile_own(t).start()

            @pl.when(t // tpd != me_d)
            def _():
                tile_copy(t).start()

        return c

    lax.fori_loop(0, ng, gather, 0)
    load_xt.wait()

    def y_copy(t, k):
        to = lax.rem(me_y + k, ny)
        return pltpu.make_async_remote_copy(
            src_ref=part.at[t, pl.ds(pl.multiple_of(to * nz * FEAT, FEAT), nz * FEAT)],
            dst_ref=rs_y.at[t, k - 1],
            send_sem=ys_sem.at[t, k],
            recv_sem=yr_sem.at[t, k],
            device_id=(me_d, to * nz + me_z),
            device_id_type=MESH,
        )

    def z_copy(t, k):
        to = lax.rem(me_z + k, nz)
        return pltpu.make_async_remote_copy(
            src_ref=mid.at[t, pl.ds(pl.multiple_of(to * FEAT, FEAT), FEAT)],
            dst_ref=rs_z.at[t, k - 1],
            send_sem=zs_sem.at[t, k],
            recv_sem=zr_sem.at[t, k],
            device_id=(me_d, me_y * nz + to),
            device_id_type=MESH,
        )

    def tile_done(t, k):
        src = lax.rem(me_d + k, nd)
        return pltpu.make_async_remote_copy(
            src_ref=dq.at[:, lanes(0)],
            dst_ref=wg_in.at[t, tile_rows(src)],
            send_sem=ts_sem.at[0],
            recv_sem=tr_sem.at[src, t],
            device_id=(src, me_s),
            device_id_type=MESH,
        )

    for t in range(tpd):
        tile_own(me_d * tpd + t).wait()

        def arrived(k, c):
            tile_done(t, k).wait_recv()
            return c

        lax.fori_loop(1, nd, arrived, 0)
        part[t] = jnp.dot(xt_vm[...], wg_in[t], preferred_element_type=F32).astype(BF16)
        for k in range(1, ny):
            y_copy(t, k).start()

    load_w.wait()

    def node_cols(n, c):
        cols = pl.ds(pl.multiple_of(n * 2 * BLK, 2 * BLK), 2 * BLK)
        gn_ref[:, cols] = lax.dot_general(
            dq[...], w_vm[cols, :], (((1,), (1,)), ((), ())), preferred_element_type=F32
        ).astype(BF16)
        return c

    lax.fori_loop(0, hidden // (2 * BLK), node_cols, 0)

    for t in range(tpd):
        total = part[t, pl.ds(pl.multiple_of(me_y * nz * FEAT, FEAT), nz * FEAT)].astype(F32)
        for k in range(1, ny):
            y_copy(t, k).wait_recv()
            total += rs_y[t, k - 1].astype(F32)
        mid[t] = total.astype(BF16)
        for k in range(1, nz):
            z_copy(t, k).start()

    for t in range(tpd):
        total = mid[t, pl.ds(pl.multiple_of(me_z * FEAT, FEAT), FEAT)].astype(F32)
        for k in range(1, nz):
            z_copy(t, k).wait_recv()
            total += rs_z[t, k - 1].astype(F32)
        wg_ref[:, pl.ds(t * BLK, BLK)] = total

    def back_sent(i, c):
        @pl.when(i > 0)
        def _():
            back_copy(i, 0).wait_send()

        for j in range(1, 4):
            back_copy(i, j).wait_send()
        return c

    lax.fori_loop(0, ng, back_sent, 0)

    def tile_sent(t, c):
        @pl.when(t // tpd != me_d)
        def _():
            tile_copy(t).wait_send()

        return c

    lax.fori_loop(0, 3 * ng, tile_sent, 0)
    for t in range(tpd):
        for k in range(1, ny):
            y_copy(t, k).wait_send()
        for k in range(1, nz):
            z_copy(t, k).wait_send()


def per_device(nd, ns, nodes, w_qkv, incoming_adjoint, block_cols, block_counts):
    rows, hidden = nodes.shape[1:]
    ny, nz = 4, ns // 4
    ng = ns // 4
    tpd = 3 * ng // nd
    any_spec = pl.BlockSpec(memory_space=pl.ANY)
    vm_spec = pl.BlockSpec(memory_space=pltpu.VMEM)
    sm_spec = pl.BlockSpec(memory_space=pltpu.SMEM)
    dma = pltpu.SemaphoreType.DMA
    packed, xt_all = pl.pallas_call(
        functools.partial(spread_kernel, nd, ns),
        out_shape=(
            jax.ShapeDtypeStruct((ns, BLK, BLK), BF16),
            jax.ShapeDtypeStruct((hidden, nd * BLK), BF16),
        ),
        in_specs=[any_spec, any_spec, any_spec],
        out_specs=(any_spec, any_spec),
        scratch_shapes=[
            pltpu.VMEM((rows, hidden), BF16),
            pltpu.VMEM((rows, hidden), BF16),
            pltpu.VMEM((ng, hidden, 3 * BLK), BF16),
            pltpu.VMEM((ns, BLK, BLK), BF16),
            pltpu.VMEM((hidden, BLK), BF16),
            dma((ng, 3)),
            dma((ng, 4)),
            dma((ng, 4)),
            dma((nd,)),
            dma((nd,)),
            dma((4,)),
        ],
        compiler_params=pltpu.CompilerParams(
            collective_id=1, has_side_effects=True, vmem_limit_bytes=VMEM_LIMIT
        ),
        name="spread",
    )(nodes, w_qkv, incoming_adjoint)
    returned = pl.pallas_call(
        functools.partial(attend_kernel, ns),
        out_shape=jax.ShapeDtypeStruct((ns, BLK, BLK), BF16),
        in_specs=[sm_spec, sm_spec, vm_spec],
        out_specs=vm_spec,
        scratch_shapes=[
            pltpu.VMEM((ns, 2 * FEAT, BLK), BF16),
            pltpu.VMEM((ns, 2 * BLK, BLK), BF16),
            pltpu.VMEM((ns, 2 * FEAT, 2 * BLK), BF16),
            pltpu.VMEM((ns, 2 * FEAT, BLK), F32),
            pltpu.VMEM((ns, 2 * FEAT, BLK), F32),
            pltpu.VMEM((SLOTS, BLK, 2 * BLK), F32),
            pltpu.VMEM((SLOTS, BLK, 2 * BLK), F32),
            pltpu.VMEM((1, BLK), F32),
            pltpu.VMEM((1, BLK), F32),
            pltpu.VMEM((SLOTS * BLK, 2 * BLK), BF16),
            pltpu.VMEM((SLOTS * BLK, 2 * BLK), BF16),
        ],
        compiler_params=pltpu.CompilerParams(vmem_limit_bytes=VMEM_LIMIT),
        name="attend",
    )(jnp.swapaxes(block_cols, 1, 2), block_counts, packed)
    mixture, grad_nodes, weight_grad = pl.pallas_call(
        functools.partial(return_kernel, nd, ns, ny, nz, tpd),
        out_shape=(
            jax.ShapeDtypeStruct((rows, hidden), BF16),
            jax.ShapeDtypeStruct((rows, hidden), BF16),
            jax.ShapeDtypeStruct((FEAT, tpd * BLK), F32),
        ),
        in_specs=[any_spec, any_spec, any_spec],
        out_specs=(vm_spec, vm_spec, vm_spec),
        scratch_shapes=[
            pltpu.VMEM((ns, BLK, BLK), BF16),
            pltpu.VMEM((hidden, 3 * hidden), BF16),
            pltpu.VMEM((hidden, nd * BLK), BF16),
            pltpu.VMEM((rows, 3 * hidden), BF16),
            pltpu.VMEM((tpd, nd * BLK, BLK), BF16),
            pltpu.VMEM((tpd, hidden, BLK), BF16),
            pltpu.VMEM((tpd, ny - 1, nz * FEAT, BLK), BF16),
            pltpu.VMEM((tpd, nz * FEAT, BLK), BF16),
            pltpu.VMEM((tpd, nz - 1, FEAT, BLK), BF16),
            dma((2,)),
            dma((ng, 4)),
            dma((ng, 4)),
            dma((1,)),
            dma((3 * ng,)),
            dma((nd, tpd)),
            dma((tpd,)),
            dma((tpd, ny)),
            dma((tpd, ny)),
            dma((tpd, nz)),
            dma((tpd, nz)),
        ],
        compiler_params=pltpu.CompilerParams(
            collective_id=2, has_side_effects=True, vmem_limit_bytes=VMEM_LIMIT
        ),
        name="give_back",
    )(returned, w_qkv, xt_all)
    return (mixture[None], grad_nodes[None], jnp.transpose(weight_grad))


def solution(mesh):
    nd, ns = mesh.shape["dp"], mesh.shape["seq"]
    in_specs = (P("dp", "seq", None), P(), P("dp", "seq", None), P("dp", None, None), P("dp", None))
    out_specs = (P("dp", "seq", None), P("dp", "seq", None), P("dp", "seq"))
    return jax.shard_map(
        functools.partial(per_device, nd, ns),
        mesh=mesh,
        in_specs=in_specs,
        out_specs=out_specs,
        check_vma=False,
    )
```

```python
import functools
import math

import jax
import jax.numpy as jnp
from jax import lax
from jax.experimental import pallas as pl
from jax.experimental.pallas import tpu as pltpu
from jax.sharding import PartitionSpec as P

MESH = pl.DeviceIdType.MESH
BLK = 128
FEAT = 32
SLOTS = 4
F32 = jnp.float32
BF16 = jnp.bfloat16
VMEM_LIMIT = 62 * 1024 * 1024


def lane_ids(shape):
    return lax.broadcasted_iota(jnp.int32, shape, len(shape) - 1)


def swap_quarters(tiles):
    lane = lane_ids(tiles[0].shape)
    low = lane < 64
    even = (lane // 32) % 2 == 0
    a0, a1, a2, a3 = tiles
    b0 = jnp.where(low, a0, pltpu.roll(a2, 64, 1))
    b2 = jnp.where(low, pltpu.roll(a0, 64, 1), a2)
    b1 = jnp.where(low, a1, pltpu.roll(a3, 64, 1))
    b3 = jnp.where(low, pltpu.roll(a1, 64, 1), a3)
    return (
        jnp.where(even, b0, pltpu.roll(b1, 32, 1)),
        jnp.where(even, pltpu.roll(b0, 96, 1), b1),
        jnp.where(even, b2, pltpu.roll(b3, 32, 1)),
        jnp.where(even, pltpu.roll(b2, 96, 1), b3),
    )


def greet(me_d, me_s, nd, ns):
    barrier = pltpu.get_barrier_semaphore()

    def seq_hello(k, c):
        pl.semaphore_signal(
            barrier, inc=1, device_id=(me_d, lax.rem(me_s + k, ns)), device_id_type=MESH
        )
        return c

    def dp_hello(k, c):
        pl.semaphore_signal(
            barrier, inc=1, device_id=(lax.rem(me_d + k, nd), me_s), device_id_type=MESH
        )
        return c

    lax.fori_loop(1, ns, seq_hello, 0)
    lax.fori_loop(1, nd, dp_hello, 0)
    return barrier


def peer_at(me_s, i, j, ng, sign):
    group = lax.rem(me_s // 4 + sign * i + ng, ng)
    return 4 * group + lax.rem(me_s % 4 + sign * j + 4, 4)


def whole_kernel(
    nd, ns, ny, nz, tpd,
    x_in, w_in, cot_in, cols_ref, cols_vec, counts_ref,
    mix_ref, gn_ref, wg_ref,
    x_vm, cot_vm, w_vm, head_out, head_in, xt_own, xt_all,
    turned_kv, left, right, chain, row_out, col_out, row_in, col_in,
    raw_even, raw_odd, top_even, top_odd, pair_even, pair_odd,
    table_vm, table, dq, wg_in, part, relay, fold, mid, last_in,
    w_sem, load_sem, head_s, head_r, xt_s, xt_r, row_s, row_r, col_s, col_r,
    own_sem, tile_s, tile_r, tile_o, relay_s, relay_r, fold_s, fold_r, last_s, last_r,
):
    me_d, me_s = lax.axis_index("dp"), lax.axis_index("seq")
    me_y, me_z = me_s // nz, me_s % nz
    ng = ns // 4
    my_group = me_s // 4
    hidden = ng * BLK
    nb = ns
    scale = 1.0 / math.sqrt(FEAT)
    to_exp2 = scale * math.log2(math.e)

    def lanes(t):
        return pl.ds(pl.multiple_of(t * BLK, BLK), BLK)

    def sent_group(i):
        return lax.rem(my_group + i, ng)

    def got_group(i):
        return lax.rem(my_group - i + ng, ng)

    def row_at(k):
        return peer_at(me_s, k // 4, k % 4, ng, 1)

    def remote(src, dst, send_sem, recv_sem, d, s):
        return pltpu.make_async_remote_copy(
            src_ref=src, dst_ref=dst, send_sem=send_sem, recv_sem=recv_sem,
            device_id=(d, s), device_id_type=MESH,
        )

    load_x = pltpu.make_async_copy(x_in.at[0], x_vm, load_sem.at[0])
    load_cot = pltpu.make_async_copy(cot_in.at[0], cot_vm, load_sem.at[1])
    load_x.start()

    def w_copy(i, m):
        g = sent_group(i)
        return pltpu.make_async_copy(
            w_in.at[:, lanes(m * ng + g)],
            w_vm.at[g, :, pl.ds(m * BLK, BLK)],
            w_sem.at[i, m],
        )

    def w_start(i, c):
        for m in range(3):
            w_copy(i, m).start()
        return c

    w_start(0, 0)
    load_cot.start()
    lax.fori_loop(1, ng, w_start, 0)
    barrier = greet(me_d, me_s, nd, ns)
    load_x.wait()
    load_cot.wait()

    def head_copy(i, j):
        peer = peer_at(me_s, i, j, ng, 1)
        return remote(
            head_out.at[peer], head_in.at[me_s], head_s.at[i, j], head_r.at[i, j], me_d, peer
        )

    own_head = pltpu.make_async_copy(head_out.at[me_s], head_in.at[me_s], own_sem.at[0])

    def project(i, c):
        g = sent_group(i)
        for m in range(3):
            w_copy(i, m).wait()
        qkv = jnp.dot(x_vm[...], w_vm[g], preferred_element_type=F32).astype(BF16)
        packed = swap_quarters(
            (qkv[:, :BLK], qkv[:, BLK : 2 * BLK], qkv[:, 2 * BLK :], cot_vm[:, lanes(g)])
        )
        for j in range(4):
            head_out[4 * g + j] = packed[j]

        @pl.when(i == 0)
        def _():
            pl.semaphore_wait(barrier, ns + nd - 2)
            own_head.start()

        @pl.when(i > 0)
        def _():
            head_copy(i, 0).start()

        for j in range(1, 4):
            head_copy(i, j).start()
        return c

    lax.fori_loop(0, ng, project, 0)

    xt_own[...] = jnp.transpose(x_vm[...].astype(F32)).astype(BF16)
    xt_keep = pltpu.make_async_copy(xt_own, xt_all.at[:, lanes(me_d)], own_sem.at[1])
    xt_keep.start()

    def xt_copy(k):
        return remote(
            xt_own, xt_all.at[:, lanes(me_d)], xt_s.at[k], xt_r.at[k],
            lax.rem(me_d + k, nd), me_s,
        )

    def xt_start(k, c):
        xt_copy(k).start()
        return c

    lax.fori_loop(1, nd, xt_start, 0)

    named_now = cols_vec[...]
    row_ids = lane_ids((SLOTS, nb))
    place = 4 * lax.rem(row_ids // 4 - my_group + ng, ng) + lax.rem(
        row_ids % 4 - me_s % 4 + 4, 4
    )
    col_ids = lane_ids((1, nb))

    def link(k, carry):
        before, final = carry
        r = row_at(k)
        for s in range(SLOTS):
            name = cols_ref[0, s, r]
            before = jnp.where((named_now == name) & (place > k), 4 * k + s, before)
            final = jnp.where(col_ids == name, 4 * k + s, final)
        return before, final

    before, final = lax.fori_loop(
        0, nb, link,
        (jnp.full((SLOTS, nb), SLOTS * nb, jnp.int32), jnp.zeros((1, nb), jnp.int32)),
    )
    table_vm[...] = jnp.zeros_like(table_vm)
    table_vm[:SLOTS, :nb] = before
    table_vm[SLOTS : SLOTS + 1, :nb] = final
    table_copy = pltpu.make_async_copy(table_vm, table, own_sem.at[2])
    table_copy.start()
    chain[SLOTS * nb] = jnp.zeros((2 * FEAT, BLK), F32)

    raw, top, pair = (raw_even, raw_odd), (top_even, top_odd), (pair_even, pair_odd)
    quarter = lane_ids((BLK, BLK)) // FEAT

    def prepare(b):
        mine = head_in[b]
        zero = jnp.zeros_like(mine)
        turned = jnp.transpose(mine.astype(F32)).astype(BF16)
        empty = jnp.zeros((FEAT, BLK), BF16)
        turned_kv[b] = turned[FEAT : 3 * FEAT]
        left[b, :BLK] = jnp.where(quarter == 1, pltpu.roll(mine, 32, 1), zero)
        left[b, BLK:] = jnp.where(quarter == 2, pltpu.roll(mine, 96, 1), zero)
        right[b, :FEAT, :BLK] = empty
        right[b, :FEAT, BLK:] = turned[:FEAT]
        right[b, FEAT:, :BLK] = turned[3 * FEAT :]
        right[b, FEAT:, BLK:] = empty

    def arrive(i, c):
        for j in range(4):
            if j == 0:

                @pl.when(i == 0)
                def _():
                    own_head.wait()

                @pl.when(i > 0)
                def _():
                    head_copy(i, 0).wait_recv()

            else:
                head_copy(i, j).wait_recv()
            prepare(4 * got_group(i) + lax.rem(me_s % 4 - j + 4, 4))
        return c

    lax.fori_loop(0, ng, arrive, 0)
    table_copy.wait()

    def score_stage(k, p):
        r = row_at(k)
        count = counts_ref[0, r]
        keys = jnp.concatenate([head_in[cols_ref[0, s, r]] for s in range(SLOTS)], axis=0)
        both = lax.dot_general(
            keys, left[r], (((1,), (1,)), ((), ())), preferred_element_type=F32
        )
        best = None
        for s in range(SLOTS):
            block = both[s * BLK : (s + 1) * BLK]
            scores = block[:, :BLK]
            if s:
                scores = jnp.where(s < count, scores, -jnp.inf)
            raw[p][s, :, :BLK] = scores
            raw[p][s, :, BLK:] = block[:, BLK:]
            peak = jnp.max(scores, axis=0, keepdims=True)
            best = peak if best is None else jnp.maximum(best, peak)
        top[p][...] = best * to_exp2

    def soft_stage(p):
        peak = top[p][...]
        total = mixed = None
        for s in range(SLOTS):
            weights = jnp.exp2(raw[p][s, :, :BLK] * to_exp2 - peak)
            t = jnp.sum(weights, axis=0, keepdims=True)
            m = jnp.sum(weights * raw[p][s, :, BLK:], axis=0, keepdims=True)
            total = t if total is None else total + t
            mixed = m if mixed is None else mixed + m
            raw[p][s, :, :BLK] = weights
        inverse = 1.0 / total
        delta = mixed * inverse
        for s in range(SLOTS):
            prob = raw[p][s, :, :BLK] * inverse
            rows = slice(s * BLK, (s + 1) * BLK)
            pair[p][rows, :BLK] = prob.astype(BF16)
            pair[p][rows, BLK:] = (prob * (raw[p][s, :, BLK:] - delta)).astype(BF16)

    def grad_stage(k, p):
        r = row_at(k)
        named = [cols_ref[0, s, r] for s in range(SLOTS)]
        both = pair[p][...]
        turned = jnp.concatenate([turned_kv[n] for n in named], axis=1)
        row_side = jnp.dot(turned, both, preferred_element_type=F32)
        row_out[r, :FEAT] = row_side[FEAT:, :BLK].astype(BF16)
        row_out[r, FEAT:] = (row_side[:FEAT, BLK:] * scale).astype(BF16)
        key_side = lax.dot_general(
            right[r], both, (((1,), (1,)), ((), ())), preferred_element_type=F32
        )
        for s in range(SLOTS):
            chain[4 * k + s] = key_side[:, s * BLK : (s + 1) * BLK] + chain[table[s, r]]

    def row_copy(i, j):
        peer = peer_at(me_s, i, j, ng, 1)
        return remote(
            row_out.at[peer], row_in.at[me_s], row_s.at[i, j], row_r.at[i, j], me_d, peer
        )

    def col_copy(i, j):
        peer = peer_at(me_s, i, j, ng, 1)
        return remote(
            col_out.at[peer], col_in.at[me_s], col_s.at[i, j], col_r.at[i, j], me_d, peer
        )

    own_row = pltpu.make_async_copy(row_out.at[me_s], row_in.at[me_s], own_sem.at[3])
    own_col = pltpu.make_async_copy(col_out.at[me_s], col_in.at[me_s], own_sem.at[4])
    score_stage(0, 0)
    score_stage(1, 1)
    soft_stage(0)

    def steps(i, c):
        @pl.when(i > 1)
        def _():
            row_copy((i - 1) // 2, 2 * ((i - 1) % 2)).start()

        @pl.when(i > 0)
        def _():
            row_copy((i - 1) // 2, 2 * ((i - 1) % 2) + 1).start()

        for u in range(2):
            k, p = 1 + 2 * i + u, (1 + u) % 2
            score_stage(k + 1, 1 - p)
            soft_stage(p)
            grad_stage(k - 1, 1 - p)
        return c

    lax.fori_loop(0, (nb - 2) // 2, steps, 0)
    own_row.start()
    row_copy(ng - 1, 0).start()
    row_copy(ng - 1, 1).start()
    soft_stage(1)
    grad_stage(nb - 2, 0)
    grad_stage(nb - 1, 1)
    row_copy(ng - 1, 2).start()
    row_copy(ng - 1, 3).start()

    def col_send(i, c):
        for j in range(4):
            peer = peer_at(me_s, i, j, ng, 1)
            total = chain[table[SLOTS, peer]]
            col_out[peer, :FEAT] = (total[:FEAT] * scale).astype(BF16)
            col_out[peer, FEAT:] = total[FEAT:].astype(BF16)
            if j == 0:

                @pl.when(i == 0)
                def _():
                    own_col.start()

                @pl.when(i > 0)
                def _():
                    col_copy(i, 0).start()

            else:
                col_copy(i, j).start()
        return c

    lax.fori_loop(0, ng, col_send, 0)

    def tile_own(g, m):
        t = m * ng + g
        return pltpu.make_async_copy(
            dq.at[g, pl.ds(m * BLK, BLK)], wg_in.at[t % tpd, :, lanes(me_d)],
            tile_o.at[t % tpd],
        )

    def tile_copy(g, m):
        t = m * ng + g
        return remote(
            dq.at[g, pl.ds(m * BLK, BLK)], wg_in.at[t % tpd, :, lanes(me_d)],
            tile_s.at[g, m], tile_r.at[me_d, t % tpd], t // tpd, me_s,
        )

    def tile_send(g, m):
        t = m * ng + g

        @pl.when(t // tpd == me_d)
        def _():
            tile_own(g, m).start()

        @pl.when(t // tpd != me_d)
        def _():
            tile_copy(g, m).start()

    def await_group(i, own, copy):
        @pl.when(i == 0)
        def _():
            own.wait()

        @pl.when(i > 0)
        def _():
            copy(i, 0).wait_recv()

        for j in range(1, 4):
            copy(i, j).wait_recv()

    def take_rows(i, c):
        g = got_group(i)
        await_group(i, own_row, row_copy)
        mix = jnp.concatenate([row_in[4 * g + j, :FEAT] for j in range(4)], axis=0)
        mix_ref[:, lanes(g)] = jnp.transpose(mix.astype(F32)).astype(BF16)
        for j in range(4):
            dq[g, j * FEAT : (j + 1) * FEAT] = row_in[4 * g + j, FEAT:]
        tile_send(g, 0)
        return c

    def take_cols(i, c):
        g = got_group(i)
        await_group(i, own_col, col_copy)
        for j in range(4):
            dq[g, BLK + j * FEAT : BLK + (j + 1) * FEAT] = col_in[4 * g + j, :FEAT]
            dq[g, 2 * BLK + j * FEAT : 2 * BLK + (j + 1) * FEAT] = col_in[4 * g + j, FEAT:]
        tile_send(g, 1)
        tile_send(g, 2)
        return c

    lax.fori_loop(0, ng, take_rows, 0)
    lax.fori_loop(0, ng, take_cols, 0)
    xt_keep.wait()

    def xt_wait(k, c):
        xt_copy(k).wait()
        return c

    lax.fori_loop(1, nd, xt_wait, 0)

    chunk = nz * FEAT
    half = chunk // 2
    up, down = lax.rem(me_y + 1, ny), lax.rem(me_y + ny - 1, ny)
    across = lax.rem(me_y + 2, ny)

    def rows_of(y, which):
        return pl.ds(pl.multiple_of(y * chunk + which * half, half), half)

    def relay_copy(t, way):
        return remote(
            part.at[t, rows_of(across, way)], relay.at[t, way],
            relay_s.at[t, way], relay_r.at[t, way], me_d, (up, down)[way] * nz + me_z,
        )

    def fold_copy(t, way, which):
        return remote(
            part.at[t, rows_of((up, down)[way], which)], fold.at[t, way, which],
            fold_s.at[t, way, which], fold_r.at[t, way, which],
            me_d, (up, down)[way] * nz + me_z,
        )

    def last_copy(t, k):
        to = lax.rem(me_z + k, nz)
        return remote(
            mid.at[t, pl.ds(pl.multiple_of(to * FEAT, FEAT), FEAT)], last_in.at[t, k - 1],
            last_s.at[t, k], last_r.at[t, k], me_d, me_y * nz + to,
        )

    def tile_done(t, k):
        src = lax.rem(me_d + k, nd)
        return remote(
            dq.at[0, pl.ds(0, BLK)], wg_in.at[t, :, lanes(src)],
            tile_s.at[0, 0], tile_r.at[src, t], src, me_s,
        )

    for t in range(tpd):
        pltpu.make_async_copy(
            dq.at[0, pl.ds(0, BLK)], wg_in.at[t, :, lanes(me_d)], tile_o.at[t]
        ).wait()

        def arrived(k, c):
            tile_done(t, k).wait_recv()
            return c

        lax.fori_loop(1, nd, arrived, 0)
        part[t] = lax.dot_general(
            xt_all[...], wg_in[t], (((1,), (1,)), ((), ())), preferred_element_type=F32
        ).astype(BF16)
        for way in range(2):
            relay_copy(t, way).start()
            fold_copy(t, way, 1 - way).start()

    def node_cols(n, c):
        width = 2 * BLK
        cols = pl.ds(pl.multiple_of(n * width, width), width)
        total = jnp.zeros((width, BLK), F32)
        for g in range(ng):
            total += jnp.dot(w_vm[g, cols], dq[g], preferred_element_type=F32)
        gn_ref[:, cols] = jnp.transpose(total).astype(BF16)
        return c

    steps_gn = hidden // (2 * BLK)
    lax.fori_loop(0, steps_gn // 2, node_cols, 0)
    for t in range(tpd):
        for way in range(2):
            relay_copy(t, way).wait_recv()
            rows = rows_of((up, down)[way], way)
            part[t, rows] = (
                part[t, rows].astype(F32) + relay[t, way].astype(F32)
            ).astype(BF16)
            fold_copy(t, way, way).start()
    lax.fori_loop(steps_gn // 2, steps_gn, node_cols, 0)
    for t in range(tpd):
        for which in range(2):
            total = part[t, rows_of(me_y, which)].astype(F32)
            for way in range(2):
                fold_copy(t, way, which).wait_recv()
                total += fold[t, way, which].astype(F32)
            mid[t, which * half : (which + 1) * half] = total.astype(BF16)
        for k in range(1, nz):
            last_copy(t, k).start()
    for t in range(tpd):
        total = mid[t, pl.ds(pl.multiple_of(me_z * FEAT, FEAT), FEAT)].astype(F32)
        for k in range(1, nz):
            last_copy(t, k).wait_recv()
            total += last_in[t, k - 1].astype(F32)
        wg_ref[:, t * BLK : (t + 1) * BLK] = total

    def sent(i, c):
        for copy in (head_copy, row_copy, col_copy):

            @pl.when(i > 0)
            def _():
                copy(i, 0).wait_send()

            for j in range(1, 4):
                copy(i, j).wait_send()
        for m in range(3):

            @pl.when((m * ng + i) // tpd != me_d)
            def _():
                tile_copy(i, m).wait_send()

        return c

    lax.fori_loop(0, ng, sent, 0)
    for t in range(tpd):
        for way in range(2):
            relay_copy(t, way).wait_send()
            for which in range(2):
                fold_copy(t, way, which).wait_send()
        for k in range(1, nz):
            last_copy(t, k).wait_send()


def per_device(nd, ns, nodes, w_qkv, incoming_adjoint, block_cols, block_counts):
    rows, hidden = nodes.shape[1:]
    ny, nz = 4, ns // 4
    ng = ns // 4
    tpd = 3 * ng // nd
    chunk = nz * FEAT
    hbm = pl.BlockSpec(memory_space=pltpu.HBM)
    vm_spec = pl.BlockSpec(memory_space=pltpu.VMEM)
    sm_spec = pl.BlockSpec(memory_space=pltpu.SMEM)
    dma = pltpu.SemaphoreType.DMA
    slots_first = jnp.swapaxes(block_cols, 1, 2)
    mixture, grad_nodes, weight_grad = pl.pallas_call(
        functools.partial(whole_kernel, nd, ns, ny, nz, tpd),
        out_shape=(
            jax.ShapeDtypeStruct((rows, hidden), BF16),
            jax.ShapeDtypeStruct((rows, hidden), BF16),
            jax.ShapeDtypeStruct((FEAT, tpd * BLK), F32),
        ),
        in_specs=[hbm, hbm, hbm, sm_spec, vm_spec, sm_spec],
        out_specs=(vm_spec, vm_spec, vm_spec),
        scratch_shapes=[
            pltpu.VMEM((rows, hidden), BF16),
            pltpu.VMEM((rows, hidden), BF16),
            pltpu.VMEM((ng, hidden, 3 * BLK), BF16),
            pltpu.VMEM((ns, BLK, BLK), BF16),
            pltpu.VMEM((ns, BLK, BLK), BF16),
            pltpu.VMEM((hidden, BLK), BF16),
            pltpu.VMEM((hidden, nd * BLK), BF16),
            pltpu.VMEM((ns, 2 * FEAT, BLK), BF16),
            pltpu.VMEM((ns, 2 * BLK, BLK), BF16),
            pltpu.VMEM((ns, 2 * FEAT, 2 * BLK), BF16),
            pltpu.VMEM((SLOTS * ns + 1, 2 * FEAT, BLK), F32),
            pltpu.VMEM((ns, 2 * FEAT, BLK), BF16),
            pltpu.VMEM((ns, 2 * FEAT, BLK), BF16),
            pltpu.VMEM((ns, 2 * FEAT, BLK), BF16),
            pltpu.VMEM((ns, 2 * FEAT, BLK), BF16),
            pltpu.VMEM((SLOTS, BLK, 2 * BLK), F32),
            pltpu.VMEM((SLOTS, BLK, 2 * BLK), F32),
            pltpu.VMEM((1, BLK), F32),
            pltpu.VMEM((1, BLK), F32),
            pltpu.VMEM((SLOTS * BLK, 2 * BLK), BF16),
            pltpu.VMEM((SLOTS * BLK, 2 * BLK), BF16),
            pltpu.VMEM((8, BLK), jnp.int32),
            pltpu.SMEM((8, BLK), jnp.int32),
            pltpu.VMEM((ng, 3 * BLK, BLK), BF16),
            pltpu.VMEM((tpd, BLK, nd * BLK), BF16),
            pltpu.VMEM((tpd, hidden, BLK), BF16),
            pltpu.VMEM((tpd, 2, chunk // 2, BLK), BF16),
            pltpu.VMEM((tpd, 2, 2, chunk // 2, BLK), BF16),
            pltpu.VMEM((tpd, chunk, BLK), BF16),
            pltpu.VMEM((tpd, nz - 1, FEAT, BLK), BF16),
            dma((ng, 3)),
            dma((2,)),
            dma((ng, 4)),
            dma((ng, 4)),
            dma((nd,)),
            dma((nd,)),
            dma((ng, 4)),
            dma((ng, 4)),
            dma((ng, 4)),
            dma((ng, 4)),
            dma((5,)),
            dma((ng, 3)),
            dma((nd, tpd)),
            dma((tpd,)),
            dma((tpd, 2)),
            dma((tpd, 2)),
            dma((tpd, 2, 2)),
            dma((tpd, 2, 2)),
            dma((tpd, nz)),
            dma((tpd, nz)),
        ],
        compiler_params=pltpu.CompilerParams(
            collective_id=1, has_side_effects=True, vmem_limit_bytes=VMEM_LIMIT
        ),
        name="whole",
    )(nodes, w_qkv, incoming_adjoint, slots_first, slots_first[0], block_counts)
    return (mixture[None], grad_nodes[None], jnp.transpose(weight_grad))


def solution(mesh):
    nd, ns = mesh.shape["dp"], mesh.shape["seq"]
    in_specs = (P("dp", "seq", None), P(), P("dp", "seq", None), P("dp", None, None), P("dp", None))
    out_specs = (P("dp", "seq", None), P("dp", "seq", None), P("dp", "seq"))
    return jax.shard_map(
        functools.partial(per_device, nd, ns),
        mesh=mesh,
        in_specs=in_specs,
        out_specs=out_specs,
        check_vma=False,
    )
```

```python
import functools
import math

import jax
import jax.numpy as jnp
from jax import lax
from jax.experimental import pallas as pl
from jax.experimental.pallas import tpu as pltpu
from jax.sharding import PartitionSpec as P

MESH = pl.DeviceIdType.MESH
BLK = 128
FEAT = 32
SLOTS = 4
F32 = jnp.float32
BF16 = jnp.bfloat16
VMEM_LIMIT = 62 * 1024 * 1024


def lane_ids(shape):
    return lax.broadcasted_iota(jnp.int32, shape, len(shape) - 1)


def peer_at(me_s, i, j, ng, sign):
    group = lax.rem(me_s // 4 + sign * i + ng, ng)
    return 4 * group + lax.rem(me_s % 4 + sign * j + 4, 4)


def flip(tile):
    return jnp.transpose(tile.astype(F32)).astype(BF16)


def whole_kernel(
    nd, ns, ny, nz,
    x_in, w_in, cot_in, cols_ref, cols_vec, counts_ref,
    mix_out, gn_out, wg_ref,
    x_vm, cot_vm, cot_t, w_vm, head_out, head_in, natural, xt_own, xt_all,
    left, right, chain, row_out, col_out, row_in, col_in,
    raw_even, raw_odd, top_even, top_odd, pair_even, pair_odd,
    table_vm, table, dq, wg_in, part, y_in, mid, last_in, mix_vm, gn_acc, gn_vm,
    w_sem, load_sem, cot_s, cot_r, head_s, head_r, xt_s, xt_r, share_s, share_r,
    row_s, row_r, col_s, col_r, own_sem, tile_s, tile_r, tile_o,
    ys_sem, yr_sem, last_s, last_r, last_o, out_sem,
):
    me_d, me_s = lax.axis_index("dp"), lax.axis_index("seq")
    me_y, me_z = me_s // nz, me_s % nz
    ng = ns // 4
    my_group = me_s // 4
    hidden = ng * BLK
    nb = ns
    scale = 1.0 / math.sqrt(FEAT)
    to_exp2 = scale * math.log2(math.e)

    def lanes(t):
        return pl.ds(pl.multiple_of(t * BLK, BLK), BLK)

    def sent_group(i):
        return lax.rem(my_group + i, ng)

    def got_group(i):
        return lax.rem(my_group - i + ng, ng)

    def row_at(k):
        return peer_at(me_s, k // 4, k % 4, ng, 1)

    def remote(src, dst, send_sem, recv_sem, d, s):
        return pltpu.make_async_remote_copy(
            src_ref=src, dst_ref=dst, send_sem=send_sem, recv_sem=recv_sem,
            device_id=(d, s), device_id_type=MESH,
        )

    def owner(m):
        return (m * ng + me_d) // 3, (m * ng + me_d) % 3

    def source(u):
        return lax.rem(3 * me_d + u, ng)

    barrier = pltpu.get_barrier_semaphore()

    def hello(d, s):
        pl.semaphore_signal(barrier, inc=1, device_id=(d, s), device_id_type=MESH)

    def seq_hello(k, c):
        hello(me_d, lax.rem(me_s + k, ns))
        return c

    def dp_hello(k, c):
        hello(lax.rem(me_d + k, nd), me_s)
        return c

    lax.fori_loop(1, ns, seq_hello, 0)
    lax.fori_loop(1, nd, dp_hello, 0)
    greeted = ns + nd - 2
    for u in range(3):

        @pl.when(source(u) != me_d)
        def _():
            def z_hello(z, c):
                hello(source(u), me_y * nz + z)
                return c

            lax.fori_loop(0, nz, z_hello, 0)

        greeted += nz * (owner(u)[0] != me_d).astype(jnp.int32)

    load_x = pltpu.make_async_copy(x_in.at[0], x_vm, load_sem.at[0])
    load_cot = pltpu.make_async_copy(cot_in.at[0], cot_vm, load_sem.at[1])
    load_cot.start()
    load_x.start()

    def w_copy(i, m):
        g = sent_group(i)
        return pltpu.make_async_copy(
            w_in.at[:, lanes(m * ng + g)], w_vm.at[m, :, lanes(g)], w_sem.at[i, m]
        )

    def w_start(i, c):
        for m in range(3):
            w_copy(i, m).start()
        return c

    lax.fori_loop(0, ng, w_start, 0)
    load_cot.wait()

    def cot_flip(g, c):
        cot_t[lanes(g)] = flip(cot_vm[:, lanes(g)])
        return c

    lax.fori_loop(0, ng, cot_flip, 0)

    def cot_rows(s):
        return cot_t.at[pl.ds(pl.multiple_of(s * FEAT, FEAT), FEAT)]

    def cot_copy(i, j):
        peer = peer_at(me_s, i, j, ng, 1)
        return remote(
            cot_rows(peer), head_in.at[me_s, pl.ds(3 * FEAT, FEAT)],
            cot_s.at[i, j], cot_r.at[i, j], me_d, peer,
        )

    def head_copy(i, j):
        peer = peer_at(me_s, i, j, ng, 1)
        return remote(
            head_out.at[peer], head_in.at[me_s, pl.ds(0, 3 * FEAT)],
            head_s.at[i, j], head_r.at[i, j], me_d, peer,
        )

    own_cot = pltpu.make_async_copy(
        cot_rows(me_s), head_in.at[me_s, pl.ds(3 * FEAT, FEAT)], own_sem.at[5]
    )
    own_head = pltpu.make_async_copy(
        head_out.at[me_s], head_in.at[me_s, pl.ds(0, 3 * FEAT)], own_sem.at[0]
    )

    def start_group(i, own, copy):
        @pl.when(i == 0)
        def _():
            own.start()

        @pl.when(i > 0)
        def _():
            copy(i, 0).start()

        for j in range(1, 4):
            copy(i, j).start()

    def await_group(i, own, copy):
        @pl.when(i == 0)
        def _():
            own.wait()

        @pl.when(i > 0)
        def _():
            copy(i, 0).wait_recv()

        for j in range(1, 4):
            copy(i, j).wait_recv()

    pl.semaphore_wait(barrier, greeted)

    def cot_send(i, c):
        start_group(i, own_cot, cot_copy)
        return c

    lax.fori_loop(0, ng, cot_send, 0)
    load_x.wait()

    def project(i, c):
        g = sent_group(i)
        for m in range(3):
            w_copy(i, m).wait()
            flat = jnp.dot(x_vm[...], w_vm[m, :, lanes(g)], preferred_element_type=F32)
            turned = jnp.transpose(flat).astype(BF16)
            for j in range(4):
                head_out[4 * g + j, m * FEAT : (m + 1) * FEAT] = turned[
                    j * FEAT : (j + 1) * FEAT
                ]
        start_group(i, own_head, head_copy)
        return c

    lax.fori_loop(0, ng, project, 0)

    xt_own[...] = flip(x_vm[...])
    xt_keep = pltpu.make_async_copy(xt_own, xt_all.at[:, lanes(me_d)], own_sem.at[1])
    xt_keep.start()
    sibling = me_d + 1 - 2 * (me_d % 2)

    def xt_copy(k):
        return remote(
            xt_own, xt_all.at[:, lanes(me_d)], xt_s.at[k], xt_r.at[k],
            lax.rem(me_d + 2 * k, nd), me_s,
        )

    def share_copy(k):
        here = lanes(lax.rem(me_d - 2 * k + nd, nd))
        return remote(
            xt_all.at[:, here] if k else xt_own, xt_all.at[:, here],
            share_s.at[k], share_r.at[k], sibling, me_s,
        )

    for k in range(1, nd // 2):
        xt_copy(k).start()
    share_copy(0).start()

    named_now = cols_vec[...]
    row_ids = lane_ids((SLOTS, nb))
    place = 4 * lax.rem(row_ids // 4 - my_group + ng, ng) + lax.rem(
        row_ids % 4 - me_s % 4 + 4, 4
    )
    col_ids = lane_ids((1, nb))

    def link(k, carry):
        before, final = carry
        r = row_at(k)
        for s in range(SLOTS):
            name = cols_ref[0, s, r]
            before = jnp.where((named_now == name) & (place > k), 4 * k + s, before)
            final = jnp.where(col_ids == name, 4 * k + s, final)
        return before, final

    before, final = lax.fori_loop(
        0, nb, link,
        (jnp.full((SLOTS, nb), SLOTS * nb, jnp.int32), jnp.zeros((1, nb), jnp.int32)),
    )
    table_vm[...] = jnp.zeros_like(table_vm)
    table_vm[:SLOTS, :nb] = before
    table_vm[SLOTS : SLOTS + 1, :nb] = final
    table_copy = pltpu.make_async_copy(table_vm, table, own_sem.at[2])
    table_copy.start()
    chain[SLOTS * nb] = jnp.zeros((2 * FEAT, BLK), F32)

    def blank(b, c):
        left[b] = jnp.zeros((BLK, 2 * BLK), BF16)
        right[b] = jnp.zeros((2 * FEAT, 2 * BLK), BF16)
        return c

    lax.fori_loop(0, nb, blank, 0)

    raw, top, pair = (raw_even, raw_odd), (top_even, top_odd), (pair_even, pair_odd)

    def arrive(i, c):
        await_group(i, own_cot, cot_copy)
        await_group(i, own_head, head_copy)
        for j in range(4):
            b = 4 * got_group(i) + lax.rem(me_s % 4 - j + 4, 4)
            turned = head_in[b]
            queries, cot = turned[:FEAT], turned[3 * FEAT :]
            natural[b] = flip(turned)
            left[b, FEAT : 2 * FEAT, :BLK] = queries
            left[b, 2 * FEAT : 3 * FEAT, BLK:] = cot
            right[b, :FEAT, BLK:] = queries
            right[b, FEAT:, :BLK] = cot
        return c

    lax.fori_loop(0, ng, arrive, 0)
    table_copy.wait()
    for k in range(1, nd // 2):
        xt_copy(k).wait_recv()
        share_copy(k).start()

    def score_stage(k, p):
        r = row_at(k)
        count = counts_ref[0, r]
        keys = jnp.concatenate([natural[cols_ref[0, s, r]] for s in range(SLOTS)], axis=0)
        both = jnp.dot(keys, left[r], preferred_element_type=F32)
        best = None
        for s in range(SLOTS):
            block = both[s * BLK : (s + 1) * BLK]
            scores = block[:, :BLK]
            if s:
                scores = jnp.where(s < count, scores, -jnp.inf)
            raw[p][s, :, :BLK] = scores
            raw[p][s, :, BLK:] = block[:, BLK:]
            peak = jnp.max(scores, axis=0, keepdims=True)
            best = peak if best is None else jnp.maximum(best, peak)
        top[p][...] = best * to_exp2

    def soft_stage(p):
        peak = top[p][...]
        total = mixed = None
        for s in range(SLOTS):
            weights = jnp.exp2(raw[p][s, :, :BLK] * to_exp2 - peak)
            t = jnp.sum(weights, axis=0, keepdims=True)
            m = jnp.sum(weights * raw[p][s, :, BLK:], axis=0, keepdims=True)
            total = t if total is None else total + t
            mixed = m if mixed is None else mixed + m
            raw[p][s, :, :BLK] = weights
        inverse = 1.0 / total
        delta = mixed * inverse
        for s in range(SLOTS):
            prob = raw[p][s, :, :BLK] * inverse
            rows = slice(s * BLK, (s + 1) * BLK)
            pair[p][rows, :BLK] = prob.astype(BF16)
            pair[p][rows, BLK:] = (prob * (raw[p][s, :, BLK:] - delta)).astype(BF16)

    def grad_stage(k, p):
        r = row_at(k)
        named = [cols_ref[0, s, r] for s in range(SLOTS)]
        both = pair[p][...]
        turned = jnp.concatenate([head_in[n, FEAT : 3 * FEAT] for n in named], axis=1)
        row_side = jnp.dot(turned, both, preferred_element_type=F32)
        row_out[r, :FEAT] = row_side[FEAT:, :BLK].astype(BF16)
        row_out[r, FEAT:] = (row_side[:FEAT, BLK:] * scale).astype(BF16)
        key_side = lax.dot_general(
            right[r], both, (((1,), (1,)), ((), ())), preferred_element_type=F32
        )
        for s in range(SLOTS):
            chain[4 * k + s] = key_side[:, s * BLK : (s + 1) * BLK] + chain[table[s, r]]

    def row_copy(i, j):
        peer = peer_at(me_s, i, j, ng, 1)
        return remote(
            row_out.at[peer], row_in.at[me_s], row_s.at[i, j], row_r.at[i, j], me_d, peer
        )

    def col_copy(i, j):
        peer = peer_at(me_s, i, j, ng, 1)
        return remote(
            col_out.at[peer], col_in.at[me_s], col_s.at[i, j], col_r.at[i, j], me_d, peer
        )

    own_row = pltpu.make_async_copy(row_out.at[me_s], row_in.at[me_s], own_sem.at[3])
    own_col = pltpu.make_async_copy(col_out.at[me_s], col_in.at[me_s], own_sem.at[4])
    score_stage(0, 0)
    score_stage(1, 1)
    soft_stage(0)

    def steps(i, c):
        @pl.when(i > 1)
        def _():
            row_copy((i - 1) // 2, 2 * ((i - 1) % 2)).start()

        @pl.when(i > 0)
        def _():
            row_copy((i - 1) // 2, 2 * ((i - 1) % 2) + 1).start()

        for u in range(2):
            k, p = 1 + 2 * i + u, (1 + u) % 2
            score_stage(k + 1, 1 - p)
            soft_stage(p)
            grad_stage(k - 1, 1 - p)
        return c

    lax.fori_loop(0, (nb - 2) // 2, steps, 0)
    own_row.start()
    row_copy(ng - 1, 0).start()
    row_copy(ng - 1, 1).start()
    soft_stage(1)
    grad_stage(nb - 2, 0)
    grad_stage(nb - 1, 1)
    row_copy(ng - 1, 2).start()
    row_copy(ng - 1, 3).start()

    def col_send(i, c):
        for j in range(4):
            peer = peer_at(me_s, i, j, ng, 1)
            total = chain[table[SLOTS, peer]]
            col_out[peer, :FEAT] = (total[:FEAT] * scale).astype(BF16)
            col_out[peer, FEAT:] = total[FEAT:].astype(BF16)
        start_group(i, own_col, col_copy)
        return c

    lax.fori_loop(0, ng, col_send, 0)

    def tile_own(m):
        return pltpu.make_async_copy(
            dq.at[m, lanes(me_d)], wg_in.at[m, :, lanes(me_d)], tile_o.at[m]
        )

    def tile_copy(m, g):
        return remote(
            dq.at[m, lanes(g)], wg_in.at[m, :, lanes(me_d)],
            tile_s.at[m, g], tile_r.at[m, me_d], g, me_s,
        )

    def tile_send(m, g):
        @pl.when(g == me_d)
        def _():
            tile_own(m).start()

        @pl.when(g != me_d)
        def _():
            tile_copy(m, g).start()

    def tile_rows(g, j):
        return pl.ds(pl.multiple_of(g * BLK + j * FEAT, FEAT), FEAT)

    def take_rows(i, c):
        g = got_group(i)
        await_group(i, own_row, row_copy)
        for j in range(4):
            dq[0, tile_rows(g, j)] = row_in[4 * g + j, FEAT:]
        tile_send(0, g)
        mix = jnp.concatenate([row_in[4 * g + j, :FEAT] for j in range(4)], axis=0)
        mix_vm[:, lanes(g)] = flip(mix)
        return c

    def take_cols(i, c):
        g = got_group(i)
        await_group(i, own_col, col_copy)
        for j in range(4):
            dq[1, tile_rows(g, j)] = col_in[4 * g + j, :FEAT]
            dq[2, tile_rows(g, j)] = col_in[4 * g + j, FEAT:]
        tile_send(1, g)
        tile_send(2, g)
        return c

    chunk = nz * FEAT

    def chunk_rows(y):
        return pl.ds(pl.multiple_of(y * chunk, chunk), chunk)

    def y_copy(m, k):
        to = lax.rem(me_y + k, ny)
        return remote(
            part.at[m, chunk_rows(to)], y_in.at[m, k - 1],
            ys_sem.at[m, k], yr_sem.at[m, k], me_d, to * nz + me_z,
        )

    def z_rows(z):
        return pl.ds(pl.multiple_of(z * FEAT, FEAT), FEAT)

    def last_copy(m, k):
        to = lax.rem(me_z + k, nz)
        d, u = owner(m)
        return remote(
            mid.at[m, z_rows(to)], last_in.at[u, k],
            last_s.at[m, k], last_r.at[u, k], d, me_y * nz + to,
        )

    def last_own(m):
        u = owner(m)[1]
        return pltpu.make_async_copy(mid.at[m, z_rows(me_z)], last_in.at[u, 0], last_o.at[u])

    def contract(m):
        tile_own(m).wait()

        def arrived(k, c):
            src = lax.rem(me_d + k, nd)
            remote(
                dq.at[m, lanes(0)], wg_in.at[m, :, lanes(src)],
                tile_s.at[m, 0], tile_r.at[m, src], src, me_s,
            ).wait_recv()
            return c

        lax.fori_loop(1, nd, arrived, 0)
        part[m] = lax.dot_general(
            xt_all[...], wg_in[m], (((1,), (1,)), ((), ())), preferred_element_type=F32
        ).astype(BF16)
        for k in range(1, ny):
            y_copy(m, k).start()

    def sum_y(m):
        total = part[m, chunk_rows(me_y)].astype(F32)
        for k in range(1, ny):
            y_copy(m, k).wait_recv()
            total += y_in[m, k - 1].astype(F32)
        mid[m] = total.astype(BF16)

        @pl.when(owner(m)[0] == me_d)
        def _():
            last_own(m).start()

        @pl.when(owner(m)[0] != me_d)
        def _():
            last_copy(m, 0).start()

        for k in range(1, nz):
            last_copy(m, k).start()

    width = 2 * BLK

    def node_part(n, m):
        rows = pl.ds(pl.multiple_of(n * width, width), width)
        return rows, jnp.dot(w_vm[m, rows], dq[m], preferred_element_type=F32)

    def nodes_early(n, c):
        rows, value = node_part(n, 0)
        gn_acc[rows] = value
        return c

    def nodes_late(n, c):
        rows, keys = node_part(n, 1)
        total = gn_acc[rows] + keys + node_part(n, 2)[1]
        gn_vm[:, rows] = jnp.transpose(total).astype(BF16)
        return c

    lax.fori_loop(0, ng, take_rows, 0)
    mix_done = pltpu.make_async_copy(mix_vm, mix_out, out_sem.at[0])
    mix_done.start()
    xt_keep.wait()
    for k in range(nd // 2):
        share_copy(k).wait_recv()
    contract(0)
    lax.fori_loop(0, hidden // width, nodes_early, 0)
    lax.fori_loop(0, ng // 4, take_cols, 0)
    sum_y(0)
    lax.fori_loop(ng // 4, ng, take_cols, 0)
    contract(1)
    contract(2)
    lax.fori_loop(0, hidden // width // 2, nodes_late, 0)
    sum_y(1)
    sum_y(2)
    lax.fori_loop(hidden // width // 2, hidden // width, nodes_late, 0)
    gn_done = pltpu.make_async_copy(gn_vm, gn_out, out_sem.at[1])
    gn_done.start()
    for u in range(3):

        @pl.when(source(u) == me_d)
        def _():
            pltpu.make_async_copy(mid.at[0, z_rows(0)], last_in.at[u, 0], last_o.at[u]).wait()

        for k in range(nz):
            arrival = remote(
                mid.at[0, z_rows(0)], last_in.at[u, k], last_s.at[0, 0], last_r.at[u, k],
                source(u), me_s,
            )
            if k:
                arrival.wait_recv()
            else:

                @pl.when(source(u) != me_d)
                def _():
                    arrival.wait_recv()

        total = last_in[u, 0].astype(F32)
        for k in range(1, nz):
            total += last_in[u, k].astype(F32)
        wg_ref[:, u * BLK : (u + 1) * BLK] = total

    def sent(i, c):
        for copy in (cot_copy, head_copy, row_copy, col_copy):

            @pl.when(i > 0)
            def _():
                copy(i, 0).wait_send()

            for j in range(1, 4):
                copy(i, j).wait_send()
        for m in range(3):

            @pl.when(i != me_d)
            def _():
                tile_copy(m, i).wait_send()

        return c

    lax.fori_loop(0, ng, sent, 0)
    for k in range(1, nd // 2):
        xt_copy(k).wait_send()
    for k in range(nd // 2):
        share_copy(k).wait_send()
    for m in range(3):
        for k in range(1, ny):
            y_copy(m, k).wait_send()

        @pl.when(owner(m)[0] != me_d)
        def _():
            last_copy(m, 0).wait_send()

        for k in range(1, nz):
            last_copy(m, k).wait_send()
    mix_done.wait()
    gn_done.wait()


def settle_kernel(mix_in, gn_in, wg_in, mix_out, gn_out, wg_out, sem):
    copies = [
        pltpu.make_async_copy(src, dst, sem.at[n])
        for n, (src, dst) in enumerate(((mix_in, mix_out), (gn_in, gn_out), (wg_in, wg_out)))
    ]
    for copy in copies:
        copy.start()
    for copy in copies:
        copy.wait()


def per_device(nd, ns, nodes, w_qkv, incoming_adjoint, block_cols, block_counts):
    rows, hidden = nodes.shape[1:]
    ny, nz = 4, ns // 4
    ng = ns // 4
    chunk = nz * FEAT
    any_spec = pl.BlockSpec(memory_space=pl.ANY)
    vm_spec = pl.BlockSpec(memory_space=pltpu.VMEM)
    sm_spec = pl.BlockSpec(memory_space=pltpu.SMEM)
    dma = pltpu.SemaphoreType.DMA
    slots_first = jnp.swapaxes(block_cols, 1, 2)
    out_shape = (
        jax.ShapeDtypeStruct((rows, hidden), BF16),
        jax.ShapeDtypeStruct((rows, hidden), BF16),
        jax.ShapeDtypeStruct((FEAT, 3 * BLK), F32),
    )
    results = pl.pallas_call(
        functools.partial(whole_kernel, nd, ns, ny, nz),
        out_shape=out_shape,
        in_specs=[any_spec, any_spec, any_spec, sm_spec, vm_spec, sm_spec],
        out_specs=(any_spec, any_spec, vm_spec),
        scratch_shapes=[
            pltpu.VMEM((rows, hidden), BF16),
            pltpu.VMEM((rows, hidden), BF16),
            pltpu.VMEM((hidden, BLK), BF16),
            pltpu.VMEM((3, hidden, hidden), BF16),
            pltpu.VMEM((ns, 3 * FEAT, BLK), BF16),
            pltpu.VMEM((ns, BLK, BLK), BF16),
            pltpu.VMEM((ns, BLK, BLK), BF16),
            pltpu.VMEM((hidden, BLK), BF16),
            pltpu.VMEM((hidden, nd * BLK), BF16),
            pltpu.VMEM((ns, BLK, 2 * BLK), BF16),
            pltpu.VMEM((ns, 2 * FEAT, 2 * BLK), BF16),
            pltpu.VMEM((SLOTS * ns + 1, 2 * FEAT, BLK), F32),
            pltpu.VMEM((ns, 2 * FEAT, BLK), BF16),
            pltpu.VMEM((ns, 2 * FEAT, BLK), BF16),
            pltpu.VMEM((ns, 2 * FEAT, BLK), BF16),
            pltpu.VMEM((ns, 2 * FEAT, BLK), BF16),
            pltpu.VMEM((SLOTS, BLK, 2 * BLK), F32),
            pltpu.VMEM((SLOTS, BLK, 2 * BLK), F32),
            pltpu.VMEM((1, BLK), F32),
            pltpu.VMEM((1, BLK), F32),
            pltpu.VMEM((SLOTS * BLK, 2 * BLK), BF16),
            pltpu.VMEM((SLOTS * BLK, 2 * BLK), BF16),
            pltpu.VMEM((8, BLK), jnp.int32),
            pltpu.SMEM((8, BLK), jnp.int32),
            pltpu.VMEM((3, hidden, BLK), BF16),
            pltpu.VMEM((3, BLK, nd * BLK), BF16),
            pltpu.VMEM((3, hidden, BLK), BF16),
            pltpu.VMEM((3, ny - 1, chunk, BLK), BF16),
            pltpu.VMEM((3, chunk, BLK), BF16),
            pltpu.VMEM((3, nz, FEAT, BLK), BF16),
            pltpu.VMEM((rows, hidden), BF16),
            pltpu.VMEM((hidden, BLK), F32),
            pltpu.VMEM((rows, hidden), BF16),
            dma((ng, 3)),
            dma((2,)),
            dma((ng, 4)),
            dma((ng, 4)),
            dma((ng, 4)),
            dma((ng, 4)),
            dma((nd // 2,)),
            dma((nd // 2,)),
            dma((nd // 2,)),
            dma((nd // 2,)),
            dma((ng, 4)),
            dma((ng, 4)),
            dma((ng, 4)),
            dma((ng, 4)),
            dma((6,)),
            dma((3, ng)),
            dma((3, nd)),
            dma((3,)),
            dma((3, ny)),
            dma((3, ny)),
            dma((3, nz)),
            dma((3, nz)),
            dma((3,)),
            dma((2,)),
        ],
        compiler_params=pltpu.CompilerParams(
            collective_id=1, has_side_effects=True, vmem_limit_bytes=VMEM_LIMIT
        ),
        name="whole",
    )(nodes, w_qkv, incoming_adjoint, slots_first, slots_first[0], block_counts)
    mixture, grad_nodes, weight_grad = pl.pallas_call(
        settle_kernel,
        out_shape=out_shape,
        in_specs=[any_spec] * 3,
        out_specs=(any_spec,) * 3,
        scratch_shapes=[dma((3,))],
        compiler_params=pltpu.CompilerParams(vmem_limit_bytes=VMEM_LIMIT),
        name="settle",
    )(*results)
    return (mixture[None], grad_nodes[None], jnp.transpose(weight_grad))


def solution(mesh):
    nd, ns = mesh.shape["dp"], mesh.shape["seq"]
    in_specs = (P("dp", "seq", None), P(), P("dp", "seq", None), P("dp", None, None), P("dp", None))
    out_specs = (P("dp", "seq", None), P("dp", "seq", None), P("dp", "seq"))
    return jax.shard_map(
        functools.partial(per_device, nd, ns),
        mesh=mesh,
        in_specs=in_specs,
        out_specs=out_specs,
        check_vma=False,
    )
```

```python
import functools
import math

import jax
import jax.numpy as jnp
from jax import lax
from jax.experimental import pallas as pl
from jax.experimental.pallas import tpu as pltpu
from jax.sharding import PartitionSpec as P

MESH = pl.DeviceIdType.MESH
BLK = 128
FEAT = 32
SLOTS = 4
F32 = jnp.float32
BF16 = jnp.bfloat16
VMEM_LIMIT = 62 * 1024 * 1024


def lane_ids(shape):
    return lax.broadcasted_iota(jnp.int32, shape, len(shape) - 1)


def swap_quarters(tiles):
    lane = lane_ids(tiles[0].shape)
    low = lane < 64
    even = (lane // 32) % 2 == 0
    a0, a1, a2, a3 = tiles
    b0 = jnp.where(low, a0, pltpu.roll(a2, 64, 1))
    b2 = jnp.where(low, pltpu.roll(a0, 64, 1), a2)
    b1 = jnp.where(low, a1, pltpu.roll(a3, 64, 1))
    b3 = jnp.where(low, pltpu.roll(a1, 64, 1), a3)
    return (
        jnp.where(even, b0, pltpu.roll(b1, 32, 1)),
        jnp.where(even, pltpu.roll(b0, 96, 1), b1),
        jnp.where(even, b2, pltpu.roll(b3, 32, 1)),
        jnp.where(even, pltpu.roll(b2, 96, 1), b3),
    )


def greet(me_d, me_s, nd, ns):
    barrier = pltpu.get_barrier_semaphore()

    def seq_hello(k, c):
        pl.semaphore_signal(
            barrier, inc=1, device_id=(me_d, lax.rem(me_s + k, ns)), device_id_type=MESH
        )
        return c

    def dp_hello(k, c):
        pl.semaphore_signal(
            barrier, inc=1, device_id=(lax.rem(me_d + k, nd), me_s), device_id_type=MESH
        )
        return c

    lax.fori_loop(1, ns, seq_hello, 0)
    lax.fori_loop(1, nd, dp_hello, 0)
    return barrier


def peer_at(me_s, i, j, ng, sign):
    group = lax.rem(me_s // 4 + sign * i + ng, ng)
    return 4 * group + lax.rem(me_s % 4 + sign * j + 4, 4)


def whole_kernel(
    nd, ns, ny, nz, tpd,
    x_in, w_in, cot_in, cols_in, counts_in,
    mix_out, gn_out, wg_out,
    cols_ref, cols_vec, counts_ref, mix_ref, gn_ref, wg_ref, x_vm, cot_vm, w_vm, head_out, head_in, xt_own, xt_all,
    turned_kv, left, right, chain, row_out, col_out, row_in, col_in,
    raw_even, raw_odd, top_even, top_odd, pair_even, pair_odd,
    table_vm, table, dq, wg_in, part, relay, fold, mid, last_in,
    w_sem, load_sem, head_s, head_r, xt_s, xt_r, row_s, row_r, col_s, col_r,
    own_sem, tile_s, tile_r, tile_o, relay_s, relay_r, fold_s, fold_r, last_s, last_r, late_s, late_r, share_s, share_r, out_sem,
):
    me_d, me_s = lax.axis_index("dp"), lax.axis_index("seq")
    me_y, me_z = me_s // nz, me_s % nz
    ng = ns // 4
    my_group = me_s // 4
    hidden = ng * BLK
    nb = ns
    scale = 1.0 / math.sqrt(FEAT)
    to_exp2 = scale * math.log2(math.e)

    def lanes(t):
        return pl.ds(pl.multiple_of(t * BLK, BLK), BLK)

    def sent_group(i):
        return lax.rem(my_group + i, ng)

    def got_group(i):
        return lax.rem(my_group - i + ng, ng)

    def row_at(k):
        return peer_at(me_s, k // 4, k % 4, ng, 1)

    def remote(src, dst, send_sem, recv_sem, d, s):
        return pltpu.make_async_remote_copy(
            src_ref=src, dst_ref=dst, send_sem=send_sem, recv_sem=recv_sem,
            device_id=(d, s), device_id_type=MESH,
        )

    barrier = greet(me_d, me_s, nd, ns)
    load_x = pltpu.make_async_copy(x_in.at[0], x_vm, load_sem.at[0])
    load_cot = pltpu.make_async_copy(cot_in.at[0], cot_vm, load_sem.at[1])
    load_x.start()

    def w_copy(i, m):
        g = sent_group(i)
        return pltpu.make_async_copy(
            w_in.at[:, lanes(m * ng + g)],
            w_vm.at[g, :, pl.ds(m * BLK, BLK)],
            w_sem.at[i, m],
        )

    def w_start(i, c):
        for m in range(3):
            w_copy(i, m).start()
        return c

    small_loads = [
        pltpu.make_async_copy(src, dst, load_sem.at[2 + n])
        for n, (src, dst) in enumerate(
            ((cols_in, cols_ref), (cols_in.at[0], cols_vec), (counts_in, counts_ref))
        )
    ]
    w_start(0, 0)
    load_cot.start()
    lax.fori_loop(1, ng, w_start, 0)
    for load in small_loads:
        load.start()
    load_x.wait()
    load_cot.wait()

    def head_copy(i, j):
        peer = peer_at(me_s, i, j, ng, 1)
        return remote(
            head_out.at[peer], head_in.at[me_s], head_s.at[i, j], head_r.at[i, j], me_d, peer
        )

    own_head = pltpu.make_async_copy(head_out.at[me_s], head_in.at[me_s], own_sem.at[0])

    def project(i, c):
        g = sent_group(i)
        for m in range(3):
            w_copy(i, m).wait()
        qkv = jnp.dot(x_vm[...], w_vm[g], preferred_element_type=F32).astype(BF16)
        packed = swap_quarters(
            (qkv[:, :BLK], qkv[:, BLK : 2 * BLK], qkv[:, 2 * BLK :], cot_vm[:, lanes(g)])
        )
        for j in range(4):
            head_out[4 * g + j] = packed[j]

        @pl.when(i == 0)
        def _():
            pl.semaphore_wait(barrier, ns + nd - 2)
            own_head.start()

        @pl.when(i > 0)
        def _():
            head_copy(i, 0).start()

        for j in range(1, 4):
            head_copy(i, j).start()
        return c

    lax.fori_loop(0, ng, project, 0)

    xt_own[...] = jnp.transpose(x_vm[...].astype(F32)).astype(BF16)
    xt_keep = pltpu.make_async_copy(xt_own, xt_all.at[:, lanes(me_d)], own_sem.at[1])
    xt_keep.start()

    sibling = me_d + 1 - 2 * (me_d % 2)

    def xt_copy(k):
        return remote(
            xt_own, xt_all.at[:, lanes(me_d)], xt_s.at[k], xt_r.at[k],
            lax.rem(me_d + 2 * k, nd), me_s,
        )

    def share_copy(k):
        here = lanes(lax.rem(me_d - 2 * k + nd, nd))
        return remote(
            xt_all.at[:, here] if k else xt_own, xt_all.at[:, here],
            share_s.at[k], share_r.at[k], sibling, me_s,
        )

    for k in range(1, nd // 2):
        xt_copy(k).start()
    share_copy(0).start()

    for load in small_loads:
        load.wait()
    named_now = cols_vec[...]
    row_ids = lane_ids((SLOTS, nb))
    place = 4 * lax.rem(row_ids // 4 - my_group + ng, ng) + lax.rem(
        row_ids % 4 - me_s % 4 + 4, 4
    )
    col_ids = lane_ids((1, nb))

    def link(k, carry):
        before, final = carry
        r = row_at(k)
        for s in range(SLOTS):
            name = cols_ref[0, s, r]
            before = jnp.where((named_now == name) & (place > k), 4 * k + s, before)
            final = jnp.where(col_ids == name, 4 * k + s, final)
        return before, final

    before, final = lax.fori_loop(
        0, nb, link,
        (jnp.full((SLOTS, nb), SLOTS * nb, jnp.int32), jnp.zeros((1, nb), jnp.int32)),
    )
    table_vm[...] = jnp.zeros_like(table_vm)
    table_vm[:SLOTS, :nb] = before
    table_vm[SLOTS : SLOTS + 1, :nb] = final
    table_copy = pltpu.make_async_copy(table_vm, table, own_sem.at[2])
    table_copy.start()
    chain[SLOTS * nb] = jnp.zeros((2 * FEAT, BLK), F32)

    raw, top, pair = (raw_even, raw_odd), (top_even, top_odd), (pair_even, pair_odd)
    quarter = lane_ids((BLK, BLK)) // FEAT

    def prepare(b):
        mine = head_in[b]
        zero = jnp.zeros_like(mine)
        turned = jnp.transpose(mine.astype(F32)).astype(BF16)
        empty = jnp.zeros((FEAT, BLK), BF16)
        turned_kv[b] = turned[FEAT : 3 * FEAT]
        left[b, :BLK] = jnp.where(quarter == 1, pltpu.roll(mine, 32, 1), zero)
        left[b, BLK:] = jnp.where(quarter == 2, pltpu.roll(mine, 96, 1), zero)
        right[b, :FEAT, :BLK] = empty
        right[b, :FEAT, BLK:] = turned[:FEAT]
        right[b, FEAT:, :BLK] = turned[3 * FEAT :]
        right[b, FEAT:, BLK:] = empty

    def arrive(i, c):
        for j in range(4):
            if j == 0:

                @pl.when(i == 0)
                def _():
                    own_head.wait()

                @pl.when(i > 0)
                def _():
                    head_copy(i, 0).wait_recv()

            else:
                head_copy(i, j).wait_recv()
            prepare(4 * got_group(i) + lax.rem(me_s % 4 - j + 4, 4))
        return c

    lax.fori_loop(0, ng - 1, arrive, 0)
    for k in range(1, nd // 2):
        xt_copy(k).wait_recv()
        share_copy(k).start()
    lax.fori_loop(ng - 1, ng, arrive, 0)
    table_copy.wait()

    def score_stage(k, p):
        r = row_at(k)
        count = counts_ref[0, r]
        keys = jnp.concatenate([head_in[cols_ref[0, s, r]] for s in range(SLOTS)], axis=0)
        both = lax.dot_general(
            keys, left[r], (((1,), (1,)), ((), ())), preferred_element_type=F32
        )
        best = None
        for s in range(SLOTS):
            block = both[s * BLK : (s + 1) * BLK]
            scores = block[:, :BLK]
            if s:
                scores = jnp.where(s < count, scores, -jnp.inf)
            raw[p][s, :, :BLK] = scores
            raw[p][s, :, BLK:] = block[:, BLK:]
            peak = jnp.max(scores, axis=0, keepdims=True)
            best = peak if best is None else jnp.maximum(best, peak)
        top[p][...] = best * to_exp2

    def soft_stage(p):
        peak = top[p][...]
        total = mixed = None
        for s in range(SLOTS):
            weights = jnp.exp2(raw[p][s, :, :BLK] * to_exp2 - peak)
            t = jnp.sum(weights, axis=0, keepdims=True)
            m = jnp.sum(weights * raw[p][s, :, BLK:], axis=0, keepdims=True)
            total = t if total is None else total + t
            mixed = m if mixed is None else mixed + m
            raw[p][s, :, :BLK] = weights
        inverse = 1.0 / total
        delta = mixed * inverse
        for s in range(SLOTS):
            prob = raw[p][s, :, :BLK] * inverse
            rows = slice(s * BLK, (s + 1) * BLK)
            pair[p][rows, :BLK] = prob.astype(BF16)
            pair[p][rows, BLK:] = (prob * (raw[p][s, :, BLK:] - delta)).astype(BF16)

    def grad_stage(k, p):
        r = row_at(k)
        named = [cols_ref[0, s, r] for s in range(SLOTS)]
        both = pair[p][...]
        turned = jnp.concatenate([turned_kv[n] for n in named], axis=1)
        row_side = jnp.dot(turned, both, preferred_element_type=F32)
        row_out[r, :FEAT] = row_side[FEAT:, :BLK].astype(BF16)
        row_out[r, FEAT:] = (row_side[:FEAT, BLK:] * scale).astype(BF16)
        key_side = lax.dot_general(
            right[r], both, (((1,), (1,)), ((), ())), preferred_element_type=F32
        )
        for s in range(SLOTS):
            chain[4 * k + s] = key_side[:, s * BLK : (s + 1) * BLK] + chain[table[s, r]]

    early = ng // 2

    def piece_copy(lo, hi, send_sem, recv_sem):
        def copy(i, j):
            peer = peer_at(me_s, i, j, ng, 1)
            part_of = pl.ds(lo, hi - lo)
            return remote(
                row_out.at[peer, part_of], row_in.at[me_s, part_of],
                send_sem.at[i, j], recv_sem.at[i, j], me_d, peer,
            )

        return copy

    row_copy = piece_copy(0, 2 * FEAT, row_s, row_r)
    query_copy = piece_copy(FEAT, 2 * FEAT, row_s, row_r)
    late_copy = piece_copy(0, FEAT, late_s, late_r)

    def col_copy(i, j):
        peer = peer_at(me_s, i, j, ng, 1)
        return remote(
            col_out.at[peer], col_in.at[me_s], col_s.at[i, j], col_r.at[i, j], me_d, peer
        )

    own_row = pltpu.make_async_copy(row_out.at[me_s], row_in.at[me_s], own_sem.at[3])
    own_col = pltpu.make_async_copy(col_out.at[me_s], col_in.at[me_s], own_sem.at[4])
    score_stage(0, 0)
    score_stage(1, 1)
    soft_stage(0)

    def steps(copy, i, c):
        @pl.when(i > 1)
        def _():
            copy((i - 1) // 2, 2 * ((i - 1) % 2)).start()

        @pl.when(i > 0)
        def _():
            copy((i - 1) // 2, 2 * ((i - 1) % 2) + 1).start()

        for u in range(2):
            k, p = 1 + 2 * i + u, (1 + u) % 2
            score_stage(k + 1, 1 - p)
            soft_stage(p)
            grad_stage(k - 1, 1 - p)
        return c

    turn = 2 * early + 1
    lax.fori_loop(0, turn, functools.partial(steps, row_copy), 0)
    lax.fori_loop(turn, (nb - 2) // 2, functools.partial(steps, query_copy), 0)
    own_row.start()
    query_copy(ng - 1, 0).start()
    query_copy(ng - 1, 1).start()
    soft_stage(1)
    grad_stage(nb - 2, 0)
    grad_stage(nb - 1, 1)
    query_copy(ng - 1, 2).start()
    query_copy(ng - 1, 3).start()

    def col_send(i, c):
        for j in range(4):
            peer = peer_at(me_s, i, j, ng, 1)
            total = chain[table[SLOTS, peer]]
            col_out[peer, :FEAT] = (total[:FEAT] * scale).astype(BF16)
            col_out[peer, FEAT:] = total[FEAT:].astype(BF16)
            if j == 0:

                @pl.when(i == 0)
                def _():
                    own_col.start()

                @pl.when(i > 0)
                def _():
                    col_copy(i, 0).start()

            else:
                col_copy(i, j).start()
        return c

    lax.fori_loop(0, ng, col_send, 0)

    def late_send(i, c):
        for j in range(4):
            late_copy(i, j).start()
        return c

    lax.fori_loop(early, ng, late_send, 0)

    def tile_own(g, m):
        t = m * ng + g
        return pltpu.make_async_copy(
            dq.at[g, pl.ds(m * BLK, BLK)], wg_in.at[t % tpd, :, lanes(me_d)],
            tile_o.at[t % tpd],
        )

    def tile_copy(g, m):
        t = m * ng + g
        return remote(
            dq.at[g, pl.ds(m * BLK, BLK)], wg_in.at[t % tpd, :, lanes(me_d)],
            tile_s.at[g, m], tile_r.at[me_d, t % tpd], t // tpd, me_s,
        )

    def tile_send(g, m):
        t = m * ng + g

        @pl.when(t // tpd == me_d)
        def _():
            tile_own(g, m).start()

        @pl.when(t // tpd != me_d)
        def _():
            tile_copy(g, m).start()

    def await_group(i, own, copy):
        @pl.when(i == 0)
        def _():
            own.wait()

        @pl.when(i > 0)
        def _():
            copy(i, 0).wait_recv()

        for j in range(1, 4):
            copy(i, j).wait_recv()

    def take_queries(g):
        for j in range(4):
            dq[g, j * FEAT : (j + 1) * FEAT] = row_in[4 * g + j, FEAT:]
        tile_send(g, 0)

    def take_mix(g):
        mix = jnp.concatenate([row_in[4 * g + j, :FEAT] for j in range(4)], axis=0)
        mix_ref[:, lanes(g)] = jnp.transpose(mix.astype(F32)).astype(BF16)

    def take_early(i, c):
        await_group(i, own_row, row_copy)
        take_queries(got_group(i))
        take_mix(got_group(i))
        return c

    def take_later(i, c):
        for j in range(4):
            query_copy(i, j).wait_recv()
        take_queries(got_group(i))
        return c

    def take_late(i, c):
        for j in range(4):
            late_copy(i, j).wait_recv()
        take_mix(got_group(i))
        return c

    def take_cols(i, c):
        g = got_group(i)
        await_group(i, own_col, col_copy)
        for j in range(4):
            dq[g, BLK + j * FEAT : BLK + (j + 1) * FEAT] = col_in[4 * g + j, :FEAT]
            dq[g, 2 * BLK + j * FEAT : 2 * BLK + (j + 1) * FEAT] = col_in[4 * g + j, FEAT:]
        tile_send(g, 1)
        tile_send(g, 2)
        return c

    lax.fori_loop(0, early, take_early, 0)
    lax.fori_loop(early, ng, take_later, 0)
    lax.fori_loop(0, ng, take_cols, 0)
    xt_keep.wait()
    for k in range(nd // 2):
        share_copy(k).wait_recv()

    chunk = nz * FEAT
    half = chunk // 2
    up, down = lax.rem(me_y + 1, ny), lax.rem(me_y + ny - 1, ny)
    across = lax.rem(me_y + 2, ny)

    def rows_of(y, which):
        return pl.ds(pl.multiple_of(y * chunk + which * half, half), half)

    def relay_copy(t, way):
        return remote(
            part.at[t, rows_of(across, way)], relay.at[t, way],
            relay_s.at[t, way], relay_r.at[t, way], me_d, (up, down)[way] * nz + me_z,
        )

    def fold_copy(t, way, which):
        return remote(
            part.at[t, rows_of((up, down)[way], which)], fold.at[t, way, which],
            fold_s.at[t, way, which], fold_r.at[t, way, which],
            me_d, (up, down)[way] * nz + me_z,
        )

    def last_copy(t, k):
        to = lax.rem(me_z + k, nz)
        return remote(
            mid.at[t, pl.ds(pl.multiple_of(to * FEAT, FEAT), FEAT)], last_in.at[t, k - 1],
            last_s.at[t, k], last_r.at[t, k], me_d, me_y * nz + to,
        )

    def tile_done(t, k):
        src = lax.rem(me_d + k, nd)
        return remote(
            dq.at[0, pl.ds(0, BLK)], wg_in.at[t, :, lanes(src)],
            tile_s.at[0, 0], tile_r.at[src, t], src, me_s,
        )

    for t in range(tpd):
        pltpu.make_async_copy(
            dq.at[0, pl.ds(0, BLK)], wg_in.at[t, :, lanes(me_d)], tile_o.at[t]
        ).wait()

        def arrived(k, c):
            tile_done(t, k).wait_recv()
            return c

        lax.fori_loop(1, nd, arrived, 0)
        part[t] = lax.dot_general(
            xt_all[...], wg_in[t], (((1,), (1,)), ((), ())), preferred_element_type=F32
        ).astype(BF16)
        for way in range(2):
            relay_copy(t, way).start()
            fold_copy(t, way, 1 - way).start()

    def node_cols(n, c):
        width = 2 * BLK
        cols = pl.ds(pl.multiple_of(n * width, width), width)
        total = jnp.zeros((width, BLK), F32)
        for g in range(ng):
            total += jnp.dot(w_vm[g, cols], dq[g], preferred_element_type=F32)
        gn_ref[:, cols] = jnp.transpose(total).astype(BF16)
        return c

    steps_gn = hidden // (2 * BLK)
    lax.fori_loop(0, steps_gn // 2, node_cols, 0)
    for t in range(tpd):
        for way in range(2):
            relay_copy(t, way).wait_recv()
            rows = rows_of((up, down)[way], way)
            part[t, rows] = (
                part[t, rows].astype(F32) + relay[t, way].astype(F32)
            ).astype(BF16)
            fold_copy(t, way, way).start()
    lax.fori_loop(early, ng, take_late, 0)
    mix_done = pltpu.make_async_copy(mix_ref, mix_out, out_sem.at[0])
    mix_done.start()
    lax.fori_loop(steps_gn // 2, steps_gn, node_cols, 0)
    gn_done = pltpu.make_async_copy(gn_ref, gn_out, out_sem.at[1])
    gn_done.start()
    for t in range(tpd):
        for which in range(2):
            total = part[t, rows_of(me_y, which)].astype(F32)
            for way in range(2):
                fold_copy(t, way, which).wait_recv()
                total += fold[t, way, which].astype(F32)
            mid[t, which * half : (which + 1) * half] = total.astype(BF16)
        for k in sorted(range(1, nz), key=lambda k: -min(k, nz - k)):
            last_copy(t, k).start()
    for t in range(tpd):
        total = mid[t, pl.ds(pl.multiple_of(me_z * FEAT, FEAT), FEAT)].astype(F32)
        for k in range(1, nz):
            last_copy(t, k).wait_recv()
            total += last_in[t, k - 1].astype(F32)
        wg_ref[:, t * BLK : (t + 1) * BLK] = total
    wg_done = pltpu.make_async_copy(wg_ref, wg_out, out_sem.at[2])
    wg_done.start()

    def sent(i, c):
        for copy in (head_copy, col_copy):

            @pl.when(i > 0)
            def _():
                copy(i, 0).wait_send()

            for j in range(1, 4):
                copy(i, j).wait_send()

        @pl.when((i > 0) & (i < early))
        def _():
            row_copy(i, 0).wait_send()

        @pl.when(i < early)
        def _():
            for j in range(1, 4):
                row_copy(i, j).wait_send()

        @pl.when(i >= early)
        def _():
            for j in range(4):
                query_copy(i, j).wait_send()
                late_copy(i, j).wait_send()

        for m in range(3):

            @pl.when((m * ng + i) // tpd != me_d)
            def _():
                tile_copy(i, m).wait_send()

        return c

    lax.fori_loop(0, ng, sent, 0)
    for k in range(1, nd // 2):
        xt_copy(k).wait_send()
    for k in range(nd // 2):
        share_copy(k).wait_send()
    for t in range(tpd):
        for way in range(2):
            relay_copy(t, way).wait_send()
            for which in range(2):
                fold_copy(t, way, which).wait_send()
        for k in range(1, nz):
            last_copy(t, k).wait_send()
    mix_done.wait()
    gn_done.wait()
    wg_done.wait()


def settle_kernel(mix_in, gn_in, wg_in, mix_out, gn_out, wg_out, mix_vm, gn_vm, wg_vm, sem):
    triples = ((mix_in, mix_vm, mix_out), (gn_in, gn_vm, gn_out), (wg_in, wg_vm, wg_out))
    loads = [pltpu.make_async_copy(a, b, sem.at[0, n]) for n, (a, b, _) in enumerate(triples)]
    stores = [pltpu.make_async_copy(b, c, sem.at[1, n]) for n, (_, b, c) in enumerate(triples)]
    for load in loads:
        load.start()
    for load, store in zip(loads, stores):
        load.wait()
        store.start()
    for store in stores:
        store.wait()


def per_device(nd, ns, nodes, w_qkv, incoming_adjoint, block_cols, block_counts):
    rows, hidden = nodes.shape[1:]
    ny, nz = 4, ns // 4
    ng = ns // 4
    tpd = 3 * ng // nd
    chunk = nz * FEAT
    any_spec = pl.BlockSpec(memory_space=pl.ANY)
    dma = pltpu.SemaphoreType.DMA
    slots_first = jnp.swapaxes(block_cols, 1, 2)
    out_shape = (
        jax.ShapeDtypeStruct((rows, hidden), BF16),
        jax.ShapeDtypeStruct((rows, hidden), BF16),
        jax.ShapeDtypeStruct((FEAT, tpd * BLK), F32),
    )
    out_buffers = [pltpu.VMEM(out.shape, out.dtype) for out in out_shape]
    results = pl.pallas_call(
        functools.partial(whole_kernel, nd, ns, ny, nz, tpd),
        out_shape=out_shape,
        in_specs=[any_spec] * 5,
        out_specs=(any_spec,) * 3,
        scratch_shapes=[
            pltpu.SMEM((1, SLOTS, ns), jnp.int32),
            pltpu.VMEM((SLOTS, ns), jnp.int32),
            pltpu.SMEM((1, ns), jnp.int32),
            *out_buffers,
            pltpu.VMEM((rows, hidden), BF16),
            pltpu.VMEM((rows, hidden), BF16),
            pltpu.VMEM((ng, hidden, 3 * BLK), BF16),
            pltpu.VMEM((ns, BLK, BLK), BF16),
            pltpu.VMEM((ns, BLK, BLK), BF16),
            pltpu.VMEM((hidden, BLK), BF16),
            pltpu.VMEM((hidden, nd * BLK), BF16),
            pltpu.VMEM((ns, 2 * FEAT, BLK), BF16),
            pltpu.VMEM((ns, 2 * BLK, BLK), BF16),
            pltpu.VMEM((ns, 2 * FEAT, 2 * BLK), BF16),
            pltpu.VMEM((SLOTS * ns + 1, 2 * FEAT, BLK), F32),
            pltpu.VMEM((ns, 2 * FEAT, BLK), BF16),
            pltpu.VMEM((ns, 2 * FEAT, BLK), BF16),
            pltpu.VMEM((ns, 2 * FEAT, BLK), BF16),
            pltpu.VMEM((ns, 2 * FEAT, BLK), BF16),
            pltpu.VMEM((SLOTS, BLK, 2 * BLK), F32),
            pltpu.VMEM((SLOTS, BLK, 2 * BLK), F32),
            pltpu.VMEM((1, BLK), F32),
            pltpu.VMEM((1, BLK), F32),
            pltpu.VMEM((SLOTS * BLK, 2 * BLK), BF16),
            pltpu.VMEM((SLOTS * BLK, 2 * BLK), BF16),
            pltpu.VMEM((8, BLK), jnp.int32),
            pltpu.SMEM((8, BLK), jnp.int32),
            pltpu.VMEM((ng, 3 * BLK, BLK), BF16),
            pltpu.VMEM((tpd, BLK, nd * BLK), BF16),
            pltpu.VMEM((tpd, hidden, BLK), BF16),
            pltpu.VMEM((tpd, 2, chunk // 2, BLK), BF16),
            pltpu.VMEM((tpd, 2, 2, chunk // 2, BLK), BF16),
            pltpu.VMEM((tpd, chunk, BLK), BF16),
            pltpu.VMEM((tpd, nz - 1, FEAT, BLK), BF16),
            dma((ng, 3)),
            dma((5,)),
            dma((ng, 4)),
            dma((ng, 4)),
            dma((nd,)),
            dma((nd,)),
            dma((ng, 4)),
            dma((ng, 4)),
            dma((ng, 4)),
            dma((ng, 4)),
            dma((5,)),
            dma((ng, 3)),
            dma((nd, tpd)),
            dma((tpd,)),
            dma((tpd, 2)),
            dma((tpd, 2)),
            dma((tpd, 2, 2)),
            dma((tpd, 2, 2)),
            dma((tpd, nz)),
            dma((tpd, nz)),
            dma((ng, 4)),
            dma((ng, 4)),
            dma((nd // 2,)),
            dma((nd // 2,)),
            dma((3,)),
        ],
        compiler_params=pltpu.CompilerParams(
            collective_id=1, has_side_effects=True, vmem_limit_bytes=VMEM_LIMIT
        ),
        name="whole",
    )(nodes, w_qkv, incoming_adjoint, slots_first, block_counts)
    mixture, grad_nodes, weight_grad = pl.pallas_call(
        settle_kernel,
        out_shape=out_shape,
        in_specs=[any_spec] * 3,
        out_specs=(any_spec,) * 3,
        scratch_shapes=[*out_buffers, dma((2, 3))],
        compiler_params=pltpu.CompilerParams(vmem_limit_bytes=VMEM_LIMIT),
        name="settle",
    )(*results)
    return (mixture[None], grad_nodes[None], jnp.transpose(weight_grad))


def solution(mesh):
    nd, ns = mesh.shape["dp"], mesh.shape["seq"]
    in_specs = (P("dp", "seq", None), P(), P("dp", "seq", None), P("dp", None, None), P("dp", None))
    out_specs = (P("dp", "seq", None), P("dp", "seq", None), P("dp", "seq"))
    return jax.shard_map(
        functools.partial(per_device, nd, ns),
        mesh=mesh,
        in_specs=in_specs,
        out_specs=out_specs,
        check_vma=False,
    )
```

```python
import functools
import math

import jax
import jax.numpy as jnp
from jax import lax
from jax.experimental import pallas as pl
from jax.experimental.pallas import tpu as pltpu
from jax.sharding import PartitionSpec as P

MESH = pl.DeviceIdType.MESH
BLK = 128
FEAT = 32
SLOTS = 4
F32 = jnp.float32
BF16 = jnp.bfloat16
VMEM_LIMIT = 62 * 1024 * 1024


def lane_ids(shape):
    return lax.broadcasted_iota(jnp.int32, shape, len(shape) - 1)


def swap_quarters(tiles):
    lane = lane_ids(tiles[0].shape)
    low = lane < 64
    even = (lane // 32) % 2 == 0
    a0, a1, a2, a3 = tiles
    b0 = jnp.where(low, a0, pltpu.roll(a2, 64, 1))
    b2 = jnp.where(low, pltpu.roll(a0, 64, 1), a2)
    b1 = jnp.where(low, a1, pltpu.roll(a3, 64, 1))
    b3 = jnp.where(low, pltpu.roll(a1, 64, 1), a3)
    return (
        jnp.where(even, b0, pltpu.roll(b1, 32, 1)),
        jnp.where(even, pltpu.roll(b0, 96, 1), b1),
        jnp.where(even, b2, pltpu.roll(b3, 32, 1)),
        jnp.where(even, pltpu.roll(b2, 96, 1), b3),
    )


def greet(me_d, me_s, nd, ns):
    barrier = pltpu.get_barrier_semaphore()

    def seq_hello(k, c):
        pl.semaphore_signal(
            barrier, inc=1, device_id=(me_d, lax.rem(me_s + k, ns)), device_id_type=MESH
        )
        return c

    def dp_hello(k, c):
        pl.semaphore_signal(
            barrier, inc=1, device_id=(lax.rem(me_d + k, nd), me_s), device_id_type=MESH
        )
        return c

    lax.fori_loop(1, ns, seq_hello, 0)
    lax.fori_loop(1, nd, dp_hello, 0)
    return barrier


def peer_at(me_s, i, j, ng, sign):
    group = lax.rem(me_s // 4 + sign * i + ng, ng)
    return 4 * group + lax.rem(me_s % 4 + sign * j + 4, 4)


def whole_kernel(
    nd, ns, ny, nz, tpd,
    x_in, w_in, cot_in, cols_in, counts_in,
    mix_out, gn_out, wg_out,
    cols_ref, cols_vec, counts_ref, mix_ref, gn_ref, wg_ref, x_vm, cot_vm, w_vm, head_out, head_in, xt_own, xt_all,
    turned_kv, left, right, chain, row_out, col_out, row_in, col_in,
    raw_even, raw_odd, top_even, top_odd, pair_even, pair_odd,
    table_vm, table, dq, wg_in, part, relay, fold, mid, last_in,
    w_sem, load_sem, head_s, head_r, xt_s, xt_r, row_s, row_r, col_s, col_r,
    own_sem, tile_s, tile_r, tile_o, relay_s, relay_r, fold_s, fold_r, last_s, last_r, late_s, late_r, share_s, share_r, out_sem,
):
    me_d, me_s = lax.axis_index("dp"), lax.axis_index("seq")
    me_y, me_z = me_s // nz, me_s % nz
    ng = ns // 4
    my_group = me_s // 4
    hidden = ng * BLK
    nb = ns
    scale = 1.0 / math.sqrt(FEAT)
    to_exp2 = scale * math.log2(math.e)

    def lanes(t):
        return pl.ds(pl.multiple_of(t * BLK, BLK), BLK)

    def sent_group(i):
        return lax.rem(my_group + i, ng)

    def got_group(i):
        return lax.rem(my_group - i + ng, ng)

    def row_at(k):
        return peer_at(me_s, k // 4, k % 4, ng, 1)

    def remote(src, dst, send_sem, recv_sem, d, s):
        return pltpu.make_async_remote_copy(
            src_ref=src, dst_ref=dst, send_sem=send_sem, recv_sem=recv_sem,
            device_id=(d, s), device_id_type=MESH,
        )

    barrier = greet(me_d, me_s, nd, ns)
    load_x = pltpu.make_async_copy(x_in.at[0], x_vm, load_sem.at[0])
    load_cot = pltpu.make_async_copy(cot_in.at[0], cot_vm, load_sem.at[1])
    load_x.start()

    def w_copy(i, m):
        g = sent_group(i)
        return pltpu.make_async_copy(
            w_in.at[:, lanes(m * ng + g)],
            w_vm.at[g, :, pl.ds(m * BLK, BLK)],
            w_sem.at[i, m],
        )

    def w_start(i, c):
        for m in range(3):
            w_copy(i, m).start()
        return c

    small_loads = [
        pltpu.make_async_copy(src, dst, load_sem.at[2 + n])
        for n, (src, dst) in enumerate(
            ((cols_in, cols_ref), (cols_in.at[0], cols_vec), (counts_in, counts_ref))
        )
    ]
    w_start(0, 0)
    load_cot.start()
    lax.fori_loop(1, ng, w_start, 0)
    for load in small_loads:
        load.start()
    load_x.wait()
    load_cot.wait()

    def head_copy(i, j):
        peer = peer_at(me_s, i, j, ng, 1)
        return remote(
            head_out.at[peer], head_in.at[me_s], head_s.at[i, j], head_r.at[i, j], me_d, peer
        )

    own_head = pltpu.make_async_copy(head_out.at[me_s], head_in.at[me_s], own_sem.at[0])

    def project(i, c):
        g = sent_group(i)
        for m in range(3):
            w_copy(i, m).wait()
        qkv = jnp.dot(x_vm[...], w_vm[g], preferred_element_type=F32).astype(BF16)
        packed = swap_quarters(
            (qkv[:, :BLK], qkv[:, BLK : 2 * BLK], qkv[:, 2 * BLK :], cot_vm[:, lanes(g)])
        )
        for j in range(4):
            head_out[4 * g + j] = packed[j]

        @pl.when(i == 0)
        def _():
            pl.semaphore_wait(barrier, ns + nd - 2)
            own_head.start()

        @pl.when(i > 0)
        def _():
            head_copy(i, 0).start()

        for j in range(1, 4):
            head_copy(i, j).start()
        return c

    lax.fori_loop(0, ng, project, 0)

    xt_own[...] = jnp.transpose(x_vm[...].astype(F32)).astype(BF16)
    xt_keep = pltpu.make_async_copy(xt_own, xt_all.at[:, lanes(me_d)], own_sem.at[1])
    xt_keep.start()

    sibling = me_d + 1 - 2 * (me_d % 2)

    def xt_copy(k):
        return remote(
            xt_own, xt_all.at[:, lanes(me_d)], xt_s.at[k], xt_r.at[k],
            lax.rem(me_d + 2 * k, nd), me_s,
        )

    def share_copy(k):
        here = lanes(lax.rem(me_d - 2 * k + nd, nd))
        return remote(
            xt_all.at[:, here] if k else xt_own, xt_all.at[:, here],
            share_s.at[k], share_r.at[k], sibling, me_s,
        )

    for k in range(1, nd // 2):
        xt_copy(k).start()
    share_copy(0).start()

    for load in small_loads:
        load.wait()
    named_now = cols_vec[...]
    row_ids = lane_ids((SLOTS, nb))
    place = 4 * lax.rem(row_ids // 4 - my_group + ng, ng) + lax.rem(
        row_ids % 4 - me_s % 4 + 4, 4
    )
    col_ids = lane_ids((1, nb))

    def link(k, carry):
        before, final = carry
        r = row_at(k)
        for s in range(SLOTS):
            name = cols_ref[0, s, r]
            before = jnp.where((named_now == name) & (place > k), 4 * k + s, before)
            final = jnp.where(col_ids == name, 4 * k + s, final)
        return before, final

    before, final = lax.fori_loop(
        0, nb, link,
        (jnp.full((SLOTS, nb), SLOTS * nb, jnp.int32), jnp.zeros((1, nb), jnp.int32)),
    )
    table_vm[...] = jnp.zeros_like(table_vm)
    table_vm[:SLOTS, :nb] = before
    table_vm[SLOTS : SLOTS + 1, :nb] = final
    table_copy = pltpu.make_async_copy(table_vm, table, own_sem.at[2])
    table_copy.start()
    chain[SLOTS * nb] = jnp.zeros((2 * FEAT, BLK), F32)

    raw, top, pair = (raw_even, raw_odd), (top_even, top_odd), (pair_even, pair_odd)
    quarter = lane_ids((BLK, BLK)) // FEAT

    def prepare(b):
        mine = head_in[b]
        zero = jnp.zeros_like(mine)
        turned = jnp.transpose(mine.astype(F32)).astype(BF16)
        empty = jnp.zeros((FEAT, BLK), BF16)
        turned_kv[b] = turned[FEAT : 3 * FEAT]
        left[b, :BLK] = jnp.where(quarter == 1, pltpu.roll(mine, 32, 1), zero)
        left[b, BLK:] = jnp.where(quarter == 2, pltpu.roll(mine, 96, 1), zero)
        right[b, :FEAT, :BLK] = empty
        right[b, :FEAT, BLK:] = turned[:FEAT]
        right[b, FEAT:, :BLK] = turned[3 * FEAT :]
        right[b, FEAT:, BLK:] = empty

    def arrive(i, c):
        for j in range(4):
            if j == 0:

                @pl.when(i == 0)
                def _():
                    own_head.wait()

                @pl.when(i > 0)
                def _():
                    head_copy(i, 0).wait_recv()

            else:
                head_copy(i, j).wait_recv()
            prepare(4 * got_group(i) + lax.rem(me_s % 4 - j + 4, 4))
        return c

    lax.fori_loop(0, ng - 1, arrive, 0)
    for k in range(1, nd // 2):
        xt_copy(k).wait_recv()
        share_copy(k).start()
    lax.fori_loop(ng - 1, ng, arrive, 0)
    table_copy.wait()

    def score_stage(k, p):
        r = row_at(k)
        count = counts_ref[0, r]
        keys = jnp.concatenate([head_in[cols_ref[0, s, r]] for s in range(SLOTS)], axis=0)
        both = lax.dot_general(
            keys, left[r], (((1,), (1,)), ((), ())), preferred_element_type=F32
        )
        best = None
        for s in range(SLOTS):
            block = both[s * BLK : (s + 1) * BLK]
            scores = block[:, :BLK]
            if s:
                scores = jnp.where(s < count, scores, -jnp.inf)
            raw[p][s, :, :BLK] = scores
            raw[p][s, :, BLK:] = block[:, BLK:]
            peak = jnp.max(scores, axis=0, keepdims=True)
            best = peak if best is None else jnp.maximum(best, peak)
        top[p][...] = best * to_exp2

    def soft_stage(p):
        peak = top[p][...]
        total = mixed = None
        for s in range(SLOTS):
            weights = jnp.exp2(raw[p][s, :, :BLK] * to_exp2 - peak)
            t = jnp.sum(weights, axis=0, keepdims=True)
            m = jnp.sum(weights * raw[p][s, :, BLK:], axis=0, keepdims=True)
            total = t if total is None else total + t
            mixed = m if mixed is None else mixed + m
            raw[p][s, :, :BLK] = weights
        inverse = 1.0 / total
        delta = mixed * inverse
        for s in range(SLOTS):
            prob = raw[p][s, :, :BLK] * inverse
            rows = slice(s * BLK, (s + 1) * BLK)
            pair[p][rows, :BLK] = prob.astype(BF16)
            pair[p][rows, BLK:] = (prob * (raw[p][s, :, BLK:] - delta)).astype(BF16)

    def grad_stage(k, p):
        r = row_at(k)
        named = [cols_ref[0, s, r] for s in range(SLOTS)]
        both = pair[p][...]
        turned = jnp.concatenate([turned_kv[n] for n in named], axis=1)
        row_side = jnp.dot(turned, both, preferred_element_type=F32)
        row_out[r, :FEAT] = row_side[FEAT:, :BLK].astype(BF16)
        row_out[r, FEAT:] = (row_side[:FEAT, BLK:] * scale).astype(BF16)
        key_side = lax.dot_general(
            right[r], both, (((1,), (1,)), ((), ())), preferred_element_type=F32
        )
        for s in range(SLOTS):
            chain[4 * k + s] = key_side[:, s * BLK : (s + 1) * BLK] + chain[table[s, r]]

    def piece_copy(lo, send_sem, recv_sem):
        def copy(i, j):
            peer = peer_at(me_s, i, j, ng, 1)
            piece = pl.ds(lo, FEAT)
            return remote(
                row_out.at[peer, piece], row_in.at[me_s, piece],
                send_sem.at[i, j], recv_sem.at[i, j], me_d, peer,
            )

        return copy

    late_copy = piece_copy(0, late_s, late_r)
    row_copy = piece_copy(FEAT, row_s, row_r)

    def col_copy(i, j):
        peer = peer_at(me_s, i, j, ng, 1)
        return remote(
            col_out.at[peer], col_in.at[me_s], col_s.at[i, j], col_r.at[i, j], me_d, peer
        )

    own_row = pltpu.make_async_copy(row_out.at[me_s], row_in.at[me_s], own_sem.at[3])
    own_col = pltpu.make_async_copy(col_out.at[me_s], col_in.at[me_s], own_sem.at[4])
    score_stage(0, 0)
    score_stage(1, 1)
    soft_stage(0)

    def steps(i, c):
        for u in range(2):
            k, p = 1 + 2 * i + u, (1 + u) % 2
            score_stage(k + 1, 1 - p)
            soft_stage(p)
            grad_stage(k - 1, 1 - p)
        return c

    def send_steps(i, c):
        row_copy((i - 1) // 2, 2 * ((i - 1) % 2)).start()
        row_copy((i - 1) // 2, 2 * ((i - 1) % 2) + 1).start()
        return steps(i, c)

    steps(0, 0)
    row_copy(0, 1).start()
    steps(1, 0)
    lax.fori_loop(2, (nb - 2) // 2, send_steps, 0)
    own_row.start()
    row_copy(ng - 1, 0).start()
    row_copy(ng - 1, 1).start()
    soft_stage(1)
    grad_stage(nb - 2, 0)
    grad_stage(nb - 1, 1)
    row_copy(ng - 1, 2).start()
    row_copy(ng - 1, 3).start()

    def col_send(i, c):
        for j in range(4):
            peer = peer_at(me_s, i, j, ng, 1)
            total = chain[table[SLOTS, peer]]
            col_out[peer, :FEAT] = (total[:FEAT] * scale).astype(BF16)
            col_out[peer, FEAT:] = total[FEAT:].astype(BF16)
            if j == 0:

                @pl.when(i == 0)
                def _():
                    own_col.start()

                @pl.when(i > 0)
                def _():
                    col_copy(i, 0).start()

            else:
                col_copy(i, j).start()
        return c

    lax.fori_loop(0, ng, col_send, 0)

    def depart(i, *copies):
        @pl.when(i > 0)
        def _():
            for copy in copies:
                copy(i, 0).wait_send()

        for copy in copies:
            for j in range(1, 4):
                copy(i, j).wait_send()

    def late_send(i, c):
        @pl.when(i > 0)
        def _():
            late_copy(i, 0).start()

        for j in range(1, 4):
            late_copy(i, j).start()
        depart(i, head_copy)
        return c

    lax.fori_loop(0, ng, late_send, 0)
    for k in range(1, nd // 2):
        xt_copy(k).wait_send()
    for k in range(nd // 2):
        share_copy(k).wait_send()

    def tile_own(g, m):
        t = m * ng + g
        return pltpu.make_async_copy(
            dq.at[g, pl.ds(m * BLK, BLK)], wg_in.at[lanes(t % tpd), lanes(me_d)],
            tile_o.at[t % tpd],
        )

    def tile_copy(g, m):
        t = m * ng + g
        return remote(
            dq.at[g, pl.ds(m * BLK, BLK)], wg_in.at[lanes(t % tpd), lanes(me_d)],
            tile_s.at[g, m], tile_r.at[me_d, t % tpd], t // tpd, me_s,
        )

    def tile_send(g, m):
        t = m * ng + g

        @pl.when(t // tpd == me_d)
        def _():
            tile_own(g, m).start()

        @pl.when(t // tpd != me_d)
        def _():
            tile_copy(g, m).start()

    def await_group(i, own, copy):
        @pl.when(i == 0)
        def _():
            own.wait()

        @pl.when(i > 0)
        def _():
            copy(i, 0).wait_recv()

        for j in range(1, 4):
            copy(i, j).wait_recv()

    def take_rows(i, c):
        g = got_group(i)
        await_group(i, own_row, row_copy)
        for j in range(4):
            dq[g, j * FEAT : (j + 1) * FEAT] = row_in[4 * g + j, FEAT:]
        tile_send(g, 0)
        depart(i, row_copy)
        return c

    def take_late(i, c):
        g = got_group(i)

        @pl.when(i > 0)
        def _():
            late_copy(i, 0).wait_recv()

        for j in range(1, 4):
            late_copy(i, j).wait_recv()
        mix = jnp.concatenate([row_in[4 * g + j, :FEAT] for j in range(4)], axis=0)
        mix_ref[:, lanes(g)] = jnp.transpose(mix.astype(F32)).astype(BF16)
        return c

    def take_cols(i, c):
        g = got_group(i)
        await_group(i, own_col, col_copy)
        for j in range(4):
            dq[g, BLK + j * FEAT : BLK + (j + 1) * FEAT] = col_in[4 * g + j, :FEAT]
            dq[g, 2 * BLK + j * FEAT : 2 * BLK + (j + 1) * FEAT] = col_in[4 * g + j, FEAT:]
        tile_send(g, 1)
        tile_send(g, 2)
        return c

    lax.fori_loop(0, ng, take_rows, 0)
    lax.fori_loop(0, ng, take_cols, 0)
    xt_keep.wait()
    for k in range(nd // 2):
        share_copy(k).wait_recv()

    chunk = nz * FEAT
    half = chunk // 2
    up, down = lax.rem(me_y + 1, ny), lax.rem(me_y + ny - 1, ny)
    across = lax.rem(me_y + 2, ny)

    def rows_of(y, which):
        return pl.ds(pl.multiple_of(y * chunk + which * half, half), half)

    def relay_copy(t, way):
        return remote(
            part.at[t, rows_of(across, way)], relay.at[t, way],
            relay_s.at[t, way], relay_r.at[t, way], me_d, (up, down)[way] * nz + me_z,
        )

    def fold_copy(t, way, which):
        return remote(
            part.at[t, rows_of((up, down)[way], which)], fold.at[t, way, which],
            fold_s.at[t, way, which], fold_r.at[t, way, which],
            me_d, (up, down)[way] * nz + me_z,
        )

    def last_copy(t, k):
        to = lax.rem(me_z + k, nz)
        return remote(
            mid.at[t, pl.ds(pl.multiple_of(to * FEAT, FEAT), FEAT)], last_in.at[t, k - 1],
            last_s.at[t, k], last_r.at[t, k], me_d, me_y * nz + to,
        )

    def tile_done(t, k):
        src = lax.rem(me_d + k, nd)
        return remote(
            dq.at[0, pl.ds(0, BLK)], wg_in.at[pl.ds(t * BLK, BLK), lanes(src)],
            tile_s.at[0, 0], tile_r.at[src, t], src, me_s,
        )

    for first, last in ((0, tpd - 1), (tpd - 1, tpd)):
        for t in range(first, last):
            pltpu.make_async_copy(
                dq.at[0, pl.ds(0, BLK)], wg_in.at[pl.ds(t * BLK, BLK), lanes(me_d)], tile_o.at[t]
            ).wait()

            def arrived(k, c):
                tile_done(t, k).wait_recv()
                return c

            lax.fori_loop(1, nd, arrived, 0)
        partial_sum = lax.dot_general(
            xt_all[...], wg_in[first * BLK : last * BLK], (((1,), (1,)), ((), ())),
            preferred_element_type=F32,
        ).astype(BF16)
        for t in range(first, last):
            part[t] = partial_sum[:, (t - first) * BLK : (t - first + 1) * BLK]
            for way in range(2):
                relay_copy(t, way).start()
                fold_copy(t, way, 1 - way).start()

    def node_cols(n, c):
        width = 2 * BLK
        cols = pl.ds(pl.multiple_of(n * width, width), width)
        total = jnp.zeros((width, BLK), F32)
        for g in range(ng):
            total += jnp.dot(w_vm[g, cols], dq[g], preferred_element_type=F32)
        gn_ref[:, cols] = jnp.transpose(total).astype(BF16)
        return c

    def sent(i, c):
        depart(i, col_copy, late_copy)
        for m in range(3):

            @pl.when((m * ng + i) // tpd != me_d)
            def _():
                tile_copy(i, m).wait_send()

        return c

    steps_gn = hidden // (2 * BLK)
    lax.fori_loop(0, steps_gn // 2, node_cols, 0)
    for t in range(tpd):
        for way in range(2):
            relay_copy(t, way).wait_recv()
            rows = rows_of((up, down)[way], way)
            part[t, rows] = (
                part[t, rows].astype(F32) + relay[t, way].astype(F32)
            ).astype(BF16)
            fold_copy(t, way, way).start()
    lax.fori_loop(0, ng, take_late, 0)
    mix_done = pltpu.make_async_copy(mix_ref, mix_out, out_sem.at[0])
    mix_done.start()
    lax.fori_loop(steps_gn // 2, steps_gn, node_cols, 0)
    gn_done = pltpu.make_async_copy(gn_ref, gn_out, out_sem.at[1])
    gn_done.start()
    lax.fori_loop(0, ng, sent, 0)
    for t in range(tpd):
        for which in range(2):
            total = part[t, rows_of(me_y, which)].astype(F32)
            for way in range(2):
                fold_copy(t, way, which).wait_recv()
                total += fold[t, way, which].astype(F32)
            mid[t, which * half : (which + 1) * half] = total.astype(BF16)
        for k in sorted(range(1, nz), key=lambda k: -min(k, nz - k)):
            last_copy(t, k).start()
    for t in range(tpd):
        total = mid[t, pl.ds(pl.multiple_of(me_z * FEAT, FEAT), FEAT)].astype(F32)
        for k in range(1, nz):
            last_copy(t, k).wait_recv()
            total += last_in[t, k - 1].astype(F32)
        wg_ref[:, t * BLK : (t + 1) * BLK] = total
    wg_done = pltpu.make_async_copy(wg_ref, wg_out, out_sem.at[2])
    wg_done.start()

    for t in range(tpd):
        for way in range(2):
            relay_copy(t, way).wait_send()
            for which in range(2):
                fold_copy(t, way, which).wait_send()
        for k in range(1, nz):
            last_copy(t, k).wait_send()
    mix_done.wait()
    gn_done.wait()
    wg_done.wait()


def settle_kernel(mix_in, gn_in, wg_in, mix_out, gn_out, wg_out, mix_vm, gn_vm, wg_vm, sem):
    triples = ((mix_in, mix_vm, mix_out), (gn_in, gn_vm, gn_out), (wg_in, wg_vm, wg_out))
    loads = [pltpu.make_async_copy(a, b, sem.at[0, n]) for n, (a, b, _) in enumerate(triples)]
    stores = [pltpu.make_async_copy(b, c, sem.at[1, n]) for n, (_, b, c) in enumerate(triples)]
    for load in loads:
        load.start()
    for load, store in zip(loads, stores):
        load.wait()
        store.start()
    for store in stores:
        store.wait()


def per_device(nd, ns, nodes, w_qkv, incoming_adjoint, block_cols, block_counts):
    rows, hidden = nodes.shape[1:]
    ny, nz = 4, ns // 4
    ng = ns // 4
    tpd = 3 * ng // nd
    chunk = nz * FEAT
    any_spec = pl.BlockSpec(memory_space=pl.ANY)
    dma = pltpu.SemaphoreType.DMA
    slots_first = jnp.swapaxes(block_cols, 1, 2)
    out_shape = (
        jax.ShapeDtypeStruct((rows, hidden), BF16),
        jax.ShapeDtypeStruct((rows, hidden), BF16),
        jax.ShapeDtypeStruct((FEAT, tpd * BLK), F32),
    )
    out_buffers = [pltpu.VMEM(out.shape, out.dtype) for out in out_shape]
    results = pl.pallas_call(
        functools.partial(whole_kernel, nd, ns, ny, nz, tpd),
        out_shape=out_shape,
        in_specs=[any_spec] * 5,
        out_specs=(any_spec,) * 3,
        scratch_shapes=[
            pltpu.SMEM((1, SLOTS, ns), jnp.int32),
            pltpu.VMEM((SLOTS, ns), jnp.int32),
            pltpu.SMEM((1, ns), jnp.int32),
            *out_buffers,
            pltpu.VMEM((rows, hidden), BF16),
            pltpu.VMEM((rows, hidden), BF16),
            pltpu.VMEM((ng, hidden, 3 * BLK), BF16),
            pltpu.VMEM((ns, BLK, BLK), BF16),
            pltpu.VMEM((ns, BLK, BLK), BF16),
            pltpu.VMEM((hidden, BLK), BF16),
            pltpu.VMEM((hidden, nd * BLK), BF16),
            pltpu.VMEM((ns, 2 * FEAT, BLK), BF16),
            pltpu.VMEM((ns, 2 * BLK, BLK), BF16),
            pltpu.VMEM((ns, 2 * FEAT, 2 * BLK), BF16),
            pltpu.VMEM((SLOTS * ns + 1, 2 * FEAT, BLK), F32),
            pltpu.VMEM((ns, 2 * FEAT, BLK), BF16),
            pltpu.VMEM((ns, 2 * FEAT, BLK), BF16),
            pltpu.VMEM((ns, 2 * FEAT, BLK), BF16),
            pltpu.VMEM((ns, 2 * FEAT, BLK), BF16),
            pltpu.VMEM((SLOTS, BLK, 2 * BLK), F32),
            pltpu.VMEM((SLOTS, BLK, 2 * BLK), F32),
            pltpu.VMEM((1, BLK), F32),
            pltpu.VMEM((1, BLK), F32),
            pltpu.VMEM((SLOTS * BLK, 2 * BLK), BF16),
            pltpu.VMEM((SLOTS * BLK, 2 * BLK), BF16),
            pltpu.VMEM((8, BLK), jnp.int32),
            pltpu.SMEM((8, BLK), jnp.int32),
            pltpu.VMEM((ng, 3 * BLK, BLK), BF16),
            pltpu.VMEM((tpd * BLK, nd * BLK), BF16),
            pltpu.VMEM((tpd, hidden, BLK), BF16),
            pltpu.VMEM((tpd, 2, chunk // 2, BLK), BF16),
            pltpu.VMEM((tpd, 2, 2, chunk // 2, BLK), BF16),
            pltpu.VMEM((tpd, chunk, BLK), BF16),
            pltpu.VMEM((tpd, nz - 1, FEAT, BLK), BF16),
            dma((ng, 3)),
            dma((5,)),
            dma((ng, 4)),
            dma((ng, 4)),
            dma((nd,)),
            dma((nd,)),
            dma((ng, 4)),
            dma((ng, 4)),
            dma((ng, 4)),
            dma((ng, 4)),
            dma((5,)),
            dma((ng, 3)),
            dma((nd, tpd)),
            dma((tpd,)),
            dma((tpd, 2)),
            dma((tpd, 2)),
            dma((tpd, 2, 2)),
            dma((tpd, 2, 2)),
            dma((tpd, nz)),
            dma((tpd, nz)),
            dma((ng, 4)),
            dma((ng, 4)),
            dma((nd // 2,)),
            dma((nd // 2,)),
            dma((3,)),
        ],
        compiler_params=pltpu.CompilerParams(
            collective_id=1, has_side_effects=True, vmem_limit_bytes=VMEM_LIMIT
        ),
        name="whole",
    )(nodes, w_qkv, incoming_adjoint, slots_first, block_counts)
    mixture, grad_nodes, weight_grad = pl.pallas_call(
        settle_kernel,
        out_shape=out_shape,
        in_specs=[any_spec] * 3,
        out_specs=(any_spec,) * 3,
        scratch_shapes=[*out_buffers, dma((2, 3))],
        compiler_params=pltpu.CompilerParams(vmem_limit_bytes=VMEM_LIMIT),
        name="settle",
    )(*results)
    return (mixture[None], grad_nodes[None], jnp.transpose(weight_grad))


def solution(mesh):
    nd, ns = mesh.shape["dp"], mesh.shape["seq"]
    in_specs = (P("dp", "seq", None), P(), P("dp", "seq", None), P("dp", None, None), P("dp", None))
    out_specs = (P("dp", "seq", None), P("dp", "seq", None), P("dp", "seq"))
    return jax.shard_map(
        functools.partial(per_device, nd, ns),
        mesh=mesh,
        in_specs=in_specs,
        out_specs=out_specs,
        check_vma=False,
    )
```

```python
import functools
import math

import jax
import jax.numpy as jnp
from jax import lax
from jax.experimental import pallas as pl
from jax.experimental.pallas import tpu as pltpu
from jax.sharding import PartitionSpec as P

MESH = pl.DeviceIdType.MESH
BLK = 128
FEAT = 32
SLOTS = 4
F32 = jnp.float32
BF16 = jnp.bfloat16
VMEM_LIMIT = 62 * 1024 * 1024


def lane_ids(shape):
    return lax.broadcasted_iota(jnp.int32, shape, len(shape) - 1)


def swap_quarters(tiles):
    lane = lane_ids(tiles[0].shape)
    low = lane < 64
    even = (lane // 32) % 2 == 0
    a0, a1, a2, a3 = tiles
    b0 = jnp.where(low, a0, pltpu.roll(a2, 64, 1))
    b2 = jnp.where(low, pltpu.roll(a0, 64, 1), a2)
    b1 = jnp.where(low, a1, pltpu.roll(a3, 64, 1))
    b3 = jnp.where(low, pltpu.roll(a1, 64, 1), a3)
    return (
        jnp.where(even, b0, pltpu.roll(b1, 32, 1)),
        jnp.where(even, pltpu.roll(b0, 96, 1), b1),
        jnp.where(even, b2, pltpu.roll(b3, 32, 1)),
        jnp.where(even, pltpu.roll(b2, 96, 1), b3),
    )


def greet(me_d, me_s, nd, ns):
    barrier = pltpu.get_barrier_semaphore()

    def seq_hello(k, c):
        pl.semaphore_signal(
            barrier, inc=1, device_id=(me_d, lax.rem(me_s + k, ns)), device_id_type=MESH
        )
        return c

    def dp_hello(k, c):
        pl.semaphore_signal(
            barrier, inc=1, device_id=(lax.rem(me_d + k, nd), me_s), device_id_type=MESH
        )
        return c

    lax.fori_loop(1, ns, seq_hello, 0)
    lax.fori_loop(1, nd, dp_hello, 0)
    return barrier


def peer_at(me_s, i, j, ng, sign):
    group = lax.rem(me_s // 4 + sign * i + ng, ng)
    return 4 * group + lax.rem(me_s % 4 + sign * j + 4, 4)


def whole_kernel(
    nd, ns, ny, nz, tpd,
    x_in, w_in, cot_in, cols_in, counts_in,
    mix_out, gn_out, wg_out,
    cols_ref, cols_vec, counts_ref, mix_ref, gn_ref, wg_ref, x_vm, cot_vm, w_vm, head_out, head_in, xt_own, xt_all,
    turned_kv, left, right, chain, row_out, col_out, row_in, col_in,
    raw_even, raw_odd, top_even, top_odd, pair_even, pair_odd,
    table_vm, table, dq, wg_in, part, relay, fold, mid, last_in,
    w_sem, load_sem, head_s, head_r, xt_s, xt_r, row_s, row_r, col_s, col_r,
    own_sem, tile_s, tile_r, relay_s, relay_r, fold_s, fold_r, last_s, last_r, late_s, late_r, share_s, share_r, out_sem,
):
    me_d, me_s = lax.axis_index("dp"), lax.axis_index("seq")
    me_y, me_z = me_s // nz, me_s % nz
    ng = ns // 4
    my_group = me_s // 4
    hidden = ng * BLK
    nb = ns
    scale = 1.0 / math.sqrt(FEAT)
    to_exp2 = scale * math.log2(math.e)

    def lanes(t):
        return pl.ds(pl.multiple_of(t * BLK, BLK), BLK)

    def sent_group(i):
        return lax.rem(my_group + i, ng)

    def got_group(i):
        return lax.rem(my_group - i + ng, ng)

    def row_at(k):
        return peer_at(me_s, k // 4, k % 4, ng, 1)

    def remote(src, dst, send_sem, recv_sem, d, s):
        return pltpu.make_async_remote_copy(
            src_ref=src, dst_ref=dst, send_sem=send_sem, recv_sem=recv_sem,
            device_id=(d, s), device_id_type=MESH,
        )

    def landed(ref, sem):
        pltpu.make_async_copy(ref, ref, sem).wait()

    barrier = greet(me_d, me_s, nd, ns)
    load_x = pltpu.make_async_copy(x_in.at[0], x_vm, load_sem.at[0])
    load_cot = pltpu.make_async_copy(cot_in.at[0], cot_vm, load_sem.at[1])
    load_x.start()

    def w_copy(i, m):
        g = sent_group(i)
        return pltpu.make_async_copy(
            w_in.at[:, lanes(m * ng + g)],
            w_vm.at[g, :, pl.ds(m * BLK, BLK)],
            w_sem.at[i],
        )

    def w_start(i, c):
        for m in range(3):
            w_copy(i, m).start()
        return c

    small_loads = [
        pltpu.make_async_copy(src, dst, load_sem.at[2 + n])
        for n, (src, dst) in enumerate(
            ((cols_in, cols_ref), (cols_in.at[0], cols_vec), (counts_in, counts_ref))
        )
    ]
    w_start(0, 0)
    load_cot.start()
    lax.fori_loop(1, ng, w_start, 0)
    for load in small_loads:
        load.start()
    load_x.wait()
    load_cot.wait()

    def head_copy(i, j):
        peer = peer_at(me_s, i, j, ng, 1)
        return remote(
            head_out.at[peer], head_in.at[me_s], head_s, head_r.at[i], me_d, peer
        )

    own_head = pltpu.make_async_copy(head_out.at[me_s], head_in.at[me_s], head_r.at[0])

    def project(i, c):
        g = sent_group(i)
        landed(w_vm.at[g], w_sem.at[i])
        qkv = jnp.dot(x_vm[...], w_vm[g], preferred_element_type=F32).astype(BF16)
        packed = swap_quarters(
            (qkv[:, :BLK], qkv[:, BLK : 2 * BLK], qkv[:, 2 * BLK :], cot_vm[:, lanes(g)])
        )
        for j in range(4):
            head_out[4 * g + j] = packed[j]

        @pl.when(i == 0)
        def _():
            pl.semaphore_wait(barrier, ns + nd - 2)
            own_head.start()

        @pl.when(i > 0)
        def _():
            head_copy(i, 0).start()

        for j in range(1, 4):
            head_copy(i, j).start()
        return c

    lax.fori_loop(0, ng, project, 0)

    xt_own[...] = jnp.transpose(x_vm[...].astype(F32)).astype(BF16)
    xt_keep = pltpu.make_async_copy(xt_own, xt_all.at[:, lanes(me_d)], own_sem.at[0])
    xt_keep.start()

    sibling = me_d + 1 - 2 * (me_d % 2)

    def xt_copy(k):
        return remote(
            xt_own, xt_all.at[:, lanes(me_d)], xt_s, xt_r,
            lax.rem(me_d + 2 * k, nd), me_s,
        )

    def share_copy(k):
        here = lanes(lax.rem(me_d - 2 * k + nd, nd))
        return remote(
            xt_all.at[:, here] if k else xt_own, xt_all.at[:, here],
            share_s, share_r, sibling, me_s,
        )

    for k in range(1, nd // 2):
        xt_copy(k).start()
    share_copy(0).start()

    for load in small_loads:
        load.wait()
    named_now = cols_vec[...]
    row_ids = lane_ids((SLOTS, nb))
    place = 4 * lax.rem(row_ids // 4 - my_group + ng, ng) + lax.rem(
        row_ids % 4 - me_s % 4 + 4, 4
    )
    col_ids = lane_ids((1, nb))

    def link(k, carry):
        before, final = carry
        r = row_at(k)
        for s in range(SLOTS):
            name = cols_ref[0, s, r]
            before = jnp.where((named_now == name) & (place > k), 4 * k + s, before)
            final = jnp.where(col_ids == name, 4 * k + s, final)
        return before, final

    before, final = lax.fori_loop(
        0, nb, link,
        (jnp.full((SLOTS, nb), SLOTS * nb, jnp.int32), jnp.zeros((1, nb), jnp.int32)),
    )
    table_vm[...] = jnp.zeros_like(table_vm)
    table_vm[:SLOTS, :nb] = before
    table_vm[SLOTS : SLOTS + 1, :nb] = final
    table_copy = pltpu.make_async_copy(table_vm, table, own_sem.at[1])
    table_copy.start()
    chain[SLOTS * nb] = jnp.zeros((2 * FEAT, BLK), F32)

    raw, top, pair = (raw_even, raw_odd), (top_even, top_odd), (pair_even, pair_odd)
    quarter = lane_ids((BLK, BLK)) // FEAT

    def prepare(b):
        mine = head_in[b]
        zero = jnp.zeros_like(mine)
        turned = jnp.transpose(mine.astype(F32)).astype(BF16)
        empty = jnp.zeros((FEAT, BLK), BF16)
        turned_kv[b] = turned[FEAT : 3 * FEAT]
        left[b, :BLK] = jnp.where(quarter == 1, pltpu.roll(mine, 32, 1), zero)
        left[b, BLK:] = jnp.where(quarter == 2, pltpu.roll(mine, 96, 1), zero)
        right[b, :FEAT, :BLK] = empty
        right[b, :FEAT, BLK:] = turned[:FEAT]
        right[b, FEAT:, :BLK] = turned[3 * FEAT :]
        right[b, FEAT:, BLK:] = empty

    def arrive(i, c):
        landed(head_in.at[pl.ds(0, 4)], head_r.at[i])
        for j in range(4):
            prepare(4 * got_group(i) + lax.rem(me_s % 4 - j + 4, 4))
        return c

    lax.fori_loop(0, ng - 1, arrive, 0)
    others = nd // 2 - 1
    if others:
        landed(xt_all.at[:, pl.ds(0, others * BLK)], xt_r)
    for k in range(1, nd // 2):
        share_copy(k).start()
    lax.fori_loop(ng - 1, ng, arrive, 0)
    table_copy.wait()

    def score_stage(k, p):
        r = row_at(k)
        count = counts_ref[0, r]
        keys = jnp.concatenate([head_in[cols_ref[0, s, r]] for s in range(SLOTS)], axis=0)
        both = lax.dot_general(
            keys, left[r], (((1,), (1,)), ((), ())), preferred_element_type=F32
        )
        best = None
        for s in range(SLOTS):
            block = both[s * BLK : (s + 1) * BLK]
            scores = block[:, :BLK]
            if s:
                scores = jnp.where(s < count, scores, -jnp.inf)
            raw[p][s, :, :BLK] = scores
            raw[p][s, :, BLK:] = block[:, BLK:]
            peak = jnp.max(scores, axis=0, keepdims=True)
            best = peak if best is None else jnp.maximum(best, peak)
        top[p][...] = best * to_exp2

    def soft_stage(p):
        peak = top[p][...]
        total = mixed = None
        for s in range(SLOTS):
            weights = jnp.exp2(raw[p][s, :, :BLK] * to_exp2 - peak)
            t = jnp.sum(weights, axis=0, keepdims=True)
            m = jnp.sum(weights * raw[p][s, :, BLK:], axis=0, keepdims=True)
            total = t if total is None else total + t
            mixed = m if mixed is None else mixed + m
            raw[p][s, :, :BLK] = weights
        inverse = 1.0 / total
        delta = mixed * inverse
        for s in range(SLOTS):
            prob = raw[p][s, :, :BLK] * inverse
            rows = slice(s * BLK, (s + 1) * BLK)
            pair[p][rows, :BLK] = prob.astype(BF16)
            pair[p][rows, BLK:] = (prob * (raw[p][s, :, BLK:] - delta)).astype(BF16)

    def grad_stage(k, p):
        r = row_at(k)
        named = [cols_ref[0, s, r] for s in range(SLOTS)]
        both = pair[p][...]
        turned = jnp.concatenate([turned_kv[n] for n in named], axis=1)
        row_side = jnp.dot(turned, both, preferred_element_type=F32)
        row_out[r, :FEAT] = row_side[FEAT:, :BLK].astype(BF16)
        row_out[r, FEAT:] = (row_side[:FEAT, BLK:] * scale).astype(BF16)
        key_side = lax.dot_general(
            right[r], both, (((1,), (1,)), ((), ())), preferred_element_type=F32
        )
        for s in range(SLOTS):
            chain[4 * k + s] = key_side[:, s * BLK : (s + 1) * BLK] + chain[table[s, r]]

    def piece_copy(lo, send_sem, recv_sem):
        def copy(i, j):
            peer = peer_at(me_s, i, j, ng, 1)
            piece = pl.ds(lo, FEAT)
            return remote(
                row_out.at[peer, piece], row_in.at[me_s, piece],
                send_sem, recv_sem(i), me_d, peer,
            )

        return copy

    late_copy = piece_copy(0, late_s, lambda i: late_r)
    row_copy = piece_copy(FEAT, row_s, lambda i: row_r.at[i])

    def col_copy(i, j):
        peer = peer_at(me_s, i, j, ng, 1)
        return remote(
            col_out.at[peer], col_in.at[me_s], col_s, col_r.at[i], me_d, peer
        )

    def own_piece(lo, sem):
        piece = pl.ds(lo, FEAT)
        return pltpu.make_async_copy(row_out.at[me_s, piece], row_in.at[me_s, piece], sem)

    own_late = own_piece(0, late_r)
    own_row = own_piece(FEAT, row_r.at[0])
    own_col = pltpu.make_async_copy(col_out.at[me_s], col_in.at[me_s], col_r.at[0])
    score_stage(0, 0)
    score_stage(1, 1)
    soft_stage(0)

    def steps(i, c):
        for u in range(2):
            k, p = 1 + 2 * i + u, (1 + u) % 2
            score_stage(k + 1, 1 - p)
            soft_stage(p)
            grad_stage(k - 1, 1 - p)
        return c

    def send_steps(i, c):
        row_copy((i - 1) // 2, 2 * ((i - 1) % 2)).start()
        row_copy((i - 1) // 2, 2 * ((i - 1) % 2) + 1).start()
        return steps(i, c)

    steps(0, 0)
    row_copy(0, 1).start()
    steps(1, 0)
    lax.fori_loop(2, (nb - 2) // 2, send_steps, 0)
    own_row.start()
    own_late.start()
    row_copy(ng - 1, 0).start()
    row_copy(ng - 1, 1).start()
    soft_stage(1)
    grad_stage(nb - 2, 0)
    grad_stage(nb - 1, 1)
    row_copy(ng - 1, 2).start()
    row_copy(ng - 1, 3).start()

    def col_send(i, c):
        for j in range(4):
            peer = peer_at(me_s, i, j, ng, 1)
            total = chain[table[SLOTS, peer]]
            col_out[peer, :FEAT] = (total[:FEAT] * scale).astype(BF16)
            col_out[peer, FEAT:] = total[FEAT:].astype(BF16)
            if j == 0:

                @pl.when(i == 0)
                def _():
                    own_col.start()

                @pl.when(i > 0)
                def _():
                    col_copy(i, 0).start()

            else:
                col_copy(i, j).start()
        return c

    lax.fori_loop(0, ng, col_send, 0)

    def late_send(i, c):
        @pl.when(i > 0)
        def _():
            late_copy(i, 0).start()

        for j in range(1, 4):
            late_copy(i, j).start()
        return c

    lax.fori_loop(0, ng, late_send, 0)
    landed(head_out.at[pl.ds(0, ns - 1)], head_s)
    if others:
        landed(xt_all.at[:, pl.ds(0, others * BLK)], xt_s)
    landed(xt_all.at[:, pl.ds(0, nd // 2 * BLK)], share_s)

    def tile_own(g, m):
        t = m * ng + g
        return pltpu.make_async_copy(
            dq.at[g, pl.ds(m * BLK, BLK)], wg_in.at[lanes(t % tpd), lanes(me_d)],
            tile_r.at[t % tpd],
        )

    def tile_copy(g, m):
        t = m * ng + g
        return remote(
            dq.at[g, pl.ds(m * BLK, BLK)], wg_in.at[lanes(t % tpd), lanes(me_d)],
            tile_s, tile_r.at[t % tpd], t // tpd, me_s,
        )

    def tile_send(g, m):
        t = m * ng + g

        @pl.when(t // tpd == me_d)
        def _():
            tile_own(g, m).start()

        @pl.when(t // tpd != me_d)
        def _():
            tile_copy(g, m).start()

    def take_rows(i, c):
        g = got_group(i)
        landed(row_in.at[pl.ds(0, 4), pl.ds(FEAT, FEAT)], row_r.at[i])
        for j in range(4):
            dq[g, j * FEAT : (j + 1) * FEAT] = row_in[4 * g + j, FEAT:]
        tile_send(g, 0)
        return c

    def take_late(g, c):
        mix = jnp.concatenate([row_in[4 * g + j, :FEAT] for j in range(4)], axis=0)
        mix_ref[:, lanes(g)] = jnp.transpose(mix.astype(F32)).astype(BF16)
        return c

    def take_cols(i, c):
        g = got_group(i)
        landed(col_in.at[pl.ds(0, 4)], col_r.at[i])
        for j in range(4):
            dq[g, BLK + j * FEAT : BLK + (j + 1) * FEAT] = col_in[4 * g + j, :FEAT]
            dq[g, 2 * BLK + j * FEAT : 2 * BLK + (j + 1) * FEAT] = col_in[4 * g + j, FEAT:]
        tile_send(g, 1)
        tile_send(g, 2)
        return c

    lax.fori_loop(0, ng, take_rows, 0)
    lax.fori_loop(0, ng, take_cols, 0)
    xt_keep.wait()
    landed(xt_all.at[:, pl.ds(0, nd // 2 * BLK)], share_r)

    chunk = nz * FEAT
    half = chunk // 2
    up, down = lax.rem(me_y + 1, ny), lax.rem(me_y + ny - 1, ny)
    across = lax.rem(me_y + 2, ny)

    def rows_of(y, which):
        return pl.ds(pl.multiple_of(y * chunk + which * half, half), half)

    def relay_copy(t, way):
        return remote(
            part.at[t, rows_of(across, way)], relay.at[t, way],
            relay_s, relay_r.at[t], me_d, (up, down)[way] * nz + me_z,
        )

    def fold_copy(t, way, which):
        return remote(
            part.at[t, rows_of((up, down)[way], which)], fold.at[t, way, which],
            fold_s, fold_r.at[t],
            me_d, (up, down)[way] * nz + me_z,
        )

    def last_copy(k):
        to = lax.rem(me_z + k, nz)
        return remote(
            mid.at[pl.ds(pl.multiple_of(to * FEAT, FEAT), FEAT)], last_in.at[k - 1],
            last_s, last_r, me_d, me_y * nz + to,
        )

    for first, last in ((0, tpd - 1), (tpd - 1, tpd)):
        for t in range(first, last):
            landed(wg_in.at[pl.ds(t * BLK, BLK)], tile_r.at[t])
        partial_sum = lax.dot_general(
            xt_all[...], wg_in[first * BLK : last * BLK], (((1,), (1,)), ((), ())),
            preferred_element_type=F32,
        ).astype(BF16)
        for t in range(first, last):
            part[t] = partial_sum[:, (t - first) * BLK : (t - first + 1) * BLK]
            for way in range(2):
                relay_copy(t, way).start()
                fold_copy(t, way, 1 - way).start()

    def node_cols(n, c):
        width = 2 * BLK
        cols = pl.ds(pl.multiple_of(n * width, width), width)
        total = jnp.zeros((width, BLK), F32)
        for g in range(ng):
            total += jnp.dot(w_vm[g, cols], dq[g], preferred_element_type=F32)
        gn_ref[:, cols] = jnp.transpose(total).astype(BF16)
        return c

    steps_gn = hidden // (2 * BLK)
    lax.fori_loop(0, steps_gn // 2, node_cols, 0)
    for t in range(tpd):
        landed(relay.at[t], relay_r.at[t])
        for way in range(2):
            rows = rows_of((up, down)[way], way)
            part[t, rows] = (
                part[t, rows].astype(F32) + relay[t, way].astype(F32)
            ).astype(BF16)
            fold_copy(t, way, way).start()
    lax.fori_loop(steps_gn // 2, steps_gn, node_cols, 0)
    gn_done = pltpu.make_async_copy(gn_ref, gn_out, out_sem.at[1])
    gn_done.start()
    for t in range(tpd):
        landed(fold.at[t], fold_r.at[t])
        for which in range(2):
            total = part[t, rows_of(me_y, which)].astype(F32)
            for way in range(2):
                total += fold[t, way, which].astype(F32)
            mid[which * half : (which + 1) * half, t * BLK : (t + 1) * BLK] = total.astype(BF16)
    for k in sorted(range(1, nz), key=lambda k: -min(k, nz - k)):
        last_copy(k).start()

    landed(row_in.at[:, pl.ds(0, FEAT)], late_r)
    lax.fori_loop(0, ng, take_late, 0)
    mix_done = pltpu.make_async_copy(mix_ref, mix_out, out_sem.at[0])
    mix_done.start()
    landed(row_out.at[pl.ds(0, ns - 1), pl.ds(FEAT, FEAT)], row_s)
    landed(row_out.at[pl.ds(0, ns - 1), pl.ds(0, FEAT)], late_s)
    landed(col_out.at[pl.ds(0, ns - 1)], col_s)
    landed(dq.at[pl.ds(0, ng - 1)], tile_s)
    landed(relay, relay_s)
    landed(fold, fold_s)
    landed(last_in, last_r)
    total = mid[pl.ds(pl.multiple_of(me_z * FEAT, FEAT), FEAT)].astype(F32)
    for k in range(1, nz):
        total += last_in[k - 1].astype(F32)
    wg_ref[...] = total
    wg_done = pltpu.make_async_copy(wg_ref, wg_out, out_sem.at[2])
    wg_done.start()
    landed(last_in, last_s)
    mix_done.wait()
    gn_done.wait()
    wg_done.wait()


def settle_kernel(mix_in, gn_in, wg_in, mix_out, gn_out, wg_out, mix_vm, gn_vm, wg_vm, sem):
    triples = ((mix_in, mix_vm, mix_out), (gn_in, gn_vm, gn_out), (wg_in, wg_vm, wg_out))
    loads = [pltpu.make_async_copy(a, b, sem.at[0, n]) for n, (a, b, _) in enumerate(triples)]
    stores = [pltpu.make_async_copy(b, c, sem.at[1, n]) for n, (_, b, c) in enumerate(triples)]
    for load in loads:
        load.start()
    for load, store in zip(loads, stores):
        load.wait()
        store.start()
    for store in stores:
        store.wait()


def per_device(nd, ns, nodes, w_qkv, incoming_adjoint, block_cols, block_counts):
    rows, hidden = nodes.shape[1:]
    ny, nz = 4, ns // 4
    ng = ns // 4
    tpd = 3 * ng // nd
    chunk = nz * FEAT
    any_spec = pl.BlockSpec(memory_space=pl.ANY)
    dma = pltpu.SemaphoreType.DMA
    slots_first = jnp.swapaxes(block_cols, 1, 2)
    out_shape = (
        jax.ShapeDtypeStruct((rows, hidden), BF16),
        jax.ShapeDtypeStruct((rows, hidden), BF16),
        jax.ShapeDtypeStruct((FEAT, tpd * BLK), F32),
    )
    out_buffers = [pltpu.VMEM(out.shape, out.dtype) for out in out_shape]
    results = pl.pallas_call(
        functools.partial(whole_kernel, nd, ns, ny, nz, tpd),
        out_shape=out_shape,
        in_specs=[any_spec] * 5,
        out_specs=(any_spec,) * 3,
        scratch_shapes=[
            pltpu.SMEM((1, SLOTS, ns), jnp.int32),
            pltpu.VMEM((SLOTS, ns), jnp.int32),
            pltpu.SMEM((1, ns), jnp.int32),
            *out_buffers,
            pltpu.VMEM((rows, hidden), BF16),
            pltpu.VMEM((rows, hidden), BF16),
            pltpu.VMEM((ng, hidden, 3 * BLK), BF16),
            pltpu.VMEM((ns, BLK, BLK), BF16),
            pltpu.VMEM((ns, BLK, BLK), BF16),
            pltpu.VMEM((hidden, BLK), BF16),
            pltpu.VMEM((hidden, nd * BLK), BF16),
            pltpu.VMEM((ns, 2 * FEAT, BLK), BF16),
            pltpu.VMEM((ns, 2 * BLK, BLK), BF16),
            pltpu.VMEM((ns, 2 * FEAT, 2 * BLK), BF16),
            pltpu.VMEM((SLOTS * ns + 1, 2 * FEAT, BLK), F32),
            pltpu.VMEM((ns, 2 * FEAT, BLK), BF16),
            pltpu.VMEM((ns, 2 * FEAT, BLK), BF16),
            pltpu.VMEM((ns, 2 * FEAT, BLK), BF16),
            pltpu.VMEM((ns, 2 * FEAT, BLK), BF16),
            pltpu.VMEM((SLOTS, BLK, 2 * BLK), F32),
            pltpu.VMEM((SLOTS, BLK, 2 * BLK), F32),
            pltpu.VMEM((1, BLK), F32),
            pltpu.VMEM((1, BLK), F32),
            pltpu.VMEM((SLOTS * BLK, 2 * BLK), BF16),
            pltpu.VMEM((SLOTS * BLK, 2 * BLK), BF16),
            pltpu.VMEM((8, BLK), jnp.int32),
            pltpu.SMEM((8, BLK), jnp.int32),
            pltpu.VMEM((ng, 3 * BLK, BLK), BF16),
            pltpu.VMEM((tpd * BLK, nd * BLK), BF16),
            pltpu.VMEM((tpd, hidden, BLK), BF16),
            pltpu.VMEM((tpd, 2, chunk // 2, BLK), BF16),
            pltpu.VMEM((tpd, 2, 2, chunk // 2, BLK), BF16),
            pltpu.VMEM((chunk, tpd * BLK), BF16),
            pltpu.VMEM((nz - 1, FEAT, tpd * BLK), BF16),
            dma((ng,)),
            dma((5,)),
            dma,
            dma((ng,)),
            dma,
            dma,
            dma,
            dma((ng,)),
            dma,
            dma((ng,)),
            dma((2,)),
            dma,
            dma((tpd,)),
            dma,
            dma((tpd,)),
            dma,
            dma((tpd,)),
            dma,
            dma,
            dma,
            dma,
            dma,
            dma,
            dma((3,)),
        ],
        compiler_params=pltpu.CompilerParams(
            collective_id=1, has_side_effects=True, vmem_limit_bytes=VMEM_LIMIT
        ),
        name="whole",
    )(nodes, w_qkv, incoming_adjoint, slots_first, block_counts)
    mixture, grad_nodes, weight_grad = pl.pallas_call(
        settle_kernel,
        out_shape=out_shape,
        in_specs=[any_spec] * 3,
        out_specs=(any_spec,) * 3,
        scratch_shapes=[*out_buffers, dma((2, 3))],
        compiler_params=pltpu.CompilerParams(vmem_limit_bytes=VMEM_LIMIT),
        name="settle",
    )(*results)
    return (mixture[None], grad_nodes[None], jnp.transpose(weight_grad))


def solution(mesh):
    nd, ns = mesh.shape["dp"], mesh.shape["seq"]
    in_specs = (P("dp", "seq", None), P(), P("dp", "seq", None), P("dp", None, None), P("dp", None))
    out_specs = (P("dp", "seq", None), P("dp", "seq", None), P("dp", "seq"))
    return jax.shard_map(
        functools.partial(per_device, nd, ns),
        mesh=mesh,
        in_specs=in_specs,
        out_specs=out_specs,
        check_vma=False,
    )
```

```python
import functools
import math

import jax
import jax.numpy as jnp
from jax import lax
from jax.experimental import pallas as pl
from jax.experimental.pallas import tpu as pltpu
from jax.sharding import PartitionSpec as P

MESH = pl.DeviceIdType.MESH
BLK = 128
FEAT = 32
SLOTS = 4
F32 = jnp.float32
BF16 = jnp.bfloat16
VMEM_LIMIT = 62 * 1024 * 1024


def lane_ids(shape):
    return lax.broadcasted_iota(jnp.int32, shape, len(shape) - 1)


def greet(me_d, me_s, nd, ns):
    barrier = pltpu.get_barrier_semaphore()

    def seq_hello(k, c):
        pl.semaphore_signal(
            barrier, inc=1, device_id=(me_d, lax.rem(me_s + k, ns)), device_id_type=MESH
        )
        return c

    def dp_hello(k, c):
        pl.semaphore_signal(
            barrier, inc=1, device_id=(lax.rem(me_d + k, nd), me_s), device_id_type=MESH
        )
        return c

    lax.fori_loop(1, ns, seq_hello, 0)
    lax.fori_loop(1, nd, dp_hello, 0)
    return barrier


def peer_at(me_s, i, j, ng, sign):
    group = lax.rem(me_s // 4 + sign * i + ng, ng)
    return 4 * group + lax.rem(me_s % 4 + sign * j + 4, 4)


def whole_kernel(
    nd, ns, ny, nz, tpd,
    x_in, w_in, cot_in, cols_in, counts_in,
    mix_out, gn_out, wg_out,
    cols_ref, cols_vec, counts_ref, mix_ref, gn_ref, wg_ref, x_vm, cot_vm, w_vm, kv_out, kv_in, qd_out, qd_in, natural, xt_own, xt_all,
    chain, row_out, col_out, row_in, col_in,
    raw_even, raw_odd, top_even, top_odd, pair_even, pair_odd,
    table_vm, table, dq, wg_in, part, relay, fold, mid, last_in,
    w_sem, load_sem, kv_s, kv_r, qd_s, qd_r, xt_s, xt_r, row_s, row_r, col_s, col_r,
    own_sem, tile_s, tile_r, relay_s, relay_r, fold_s, fold_r, last_s, last_r, late_s, late_r, share_s, share_r, out_sem,
):
    me_d, me_s = lax.axis_index("dp"), lax.axis_index("seq")
    me_y, me_z = me_s // nz, me_s % nz
    ng = ns // 4
    my_group = me_s // 4
    hidden = ng * BLK
    nb = ns
    scale = 1.0 / math.sqrt(FEAT)
    to_exp2 = scale * math.log2(math.e)

    def lanes(t):
        return pl.ds(pl.multiple_of(t * BLK, BLK), BLK)

    def sent_group(i):
        return lax.rem(my_group + i, ng)

    def got_group(i):
        return lax.rem(my_group - i + ng, ng)

    def row_at(k):
        return peer_at(me_s, k // 4, k % 4, ng, -1)

    def remote(src, dst, send_sem, recv_sem, d, s):
        return pltpu.make_async_remote_copy(
            src_ref=src, dst_ref=dst, send_sem=send_sem, recv_sem=recv_sem,
            device_id=(d, s), device_id_type=MESH,
        )

    def landed(ref, sem):
        pltpu.make_async_copy(ref, ref, sem).wait()

    barrier = greet(me_d, me_s, nd, ns)
    load_x = pltpu.make_async_copy(x_in.at[0], x_vm, load_sem.at[0])
    load_cot = pltpu.make_async_copy(cot_in.at[0], cot_vm, load_sem.at[1])
    load_x.start()

    def w_start(part, i):
        g = sent_group(i)
        for m in ((1, 2), (0,))[part]:
            pltpu.make_async_copy(
                w_in.at[:, lanes(m * ng + g)],
                w_vm.at[g, :, pl.ds(m * BLK, BLK)],
                w_sem.at[part, i],
            ).start()

    def kv_weights(i, c):
        w_start(0, i)
        return c

    def q_weights(i, c):
        w_start(1, i)
        return c

    small_loads = [
        pltpu.make_async_copy(src, dst, load_sem.at[2 + n])
        for n, (src, dst) in enumerate(
            ((cols_in, cols_ref), (cols_in.at[0], cols_vec), (counts_in, counts_ref))
        )
    ]
    lax.fori_loop(0, ng, kv_weights, 0)
    load_cot.start()
    lax.fori_loop(0, ng, q_weights, 0)
    for load in small_loads:
        load.start()
    load_x.wait()

    def pieces_copy(out, into, send_sem, recv_sem):
        def copy(i, j):
            peer = peer_at(me_s, i, j, ng, 1)
            return remote(out.at[peer], into.at[me_s], send_sem, recv_sem.at[i], me_d, peer)

        return copy, pltpu.make_async_copy(out.at[me_s], into.at[me_s], recv_sem.at[0])

    kv_copy, own_kv = pieces_copy(kv_out, kv_in, kv_s, kv_r)
    qd_copy, own_qd = pieces_copy(qd_out, qd_in, qd_s, qd_r)

    def start_group(i, own, copy):
        @pl.when(i == 0)
        def _():
            own.start()

        @pl.when(i > 0)
        def _():
            copy(i, 0).start()

        for j in range(1, 4):
            copy(i, j).start()

    def project_kv(i, c):
        g = sent_group(i)
        landed(w_vm.at[g, :, pl.ds(BLK, 2 * BLK)], w_sem.at[0, i])
        flat = jnp.dot(x_vm[...], w_vm[g, :, BLK:], preferred_element_type=F32)
        for m in range(2):
            turned = jnp.transpose(flat[:, m * BLK : (m + 1) * BLK]).astype(BF16)
            for j in range(4):
                kv_out[4 * g + j, m * FEAT : (m + 1) * FEAT] = turned[
                    j * FEAT : (j + 1) * FEAT
                ]

        @pl.when(i == 0)
        def _():
            pl.semaphore_wait(barrier, ns + nd - 2)

        start_group(i, own_kv, kv_copy)
        return c

    def project_q(i, c):
        g = sent_group(i)
        landed(w_vm.at[g, :, pl.ds(0, BLK)], w_sem.at[1, i])
        flat = jnp.dot(x_vm[...], w_vm[g, :, :BLK], preferred_element_type=F32)
        for m, piece in enumerate((flat, cot_vm[:, lanes(g)].astype(F32))):
            turned = jnp.transpose(piece).astype(BF16)
            for j in range(4):
                qd_out[4 * g + j, m * FEAT : (m + 1) * FEAT] = turned[
                    j * FEAT : (j + 1) * FEAT
                ]
        start_group(i, own_qd, qd_copy)
        return c

    lax.fori_loop(0, ng, project_kv, 0)
    load_cot.wait()
    lax.fori_loop(0, ng, project_q, 0)

    xt_own[...] = jnp.transpose(x_vm[...].astype(F32)).astype(BF16)
    xt_keep = pltpu.make_async_copy(xt_own, xt_all.at[:, lanes(me_d)], own_sem.at[0])
    xt_keep.start()

    sibling = me_d + 1 - 2 * (me_d % 2)

    def xt_copy(k):
        return remote(
            xt_own, xt_all.at[:, lanes(me_d)], xt_s, xt_r,
            lax.rem(me_d + 2 * k, nd), me_s,
        )

    def share_copy(k):
        here = lanes(lax.rem(me_d - 2 * k + nd, nd))
        return remote(
            xt_all.at[:, here] if k else xt_own, xt_all.at[:, here],
            share_s, share_r, sibling, me_s,
        )

    for k in range(1, nd // 2):
        xt_copy(k).start()
    share_copy(0).start()

    for load in small_loads:
        load.wait()
    named_now = cols_vec[...]
    row_ids = lane_ids((SLOTS, nb))
    place = 4 * lax.rem(my_group - row_ids // 4 + ng, ng) + lax.rem(
        me_s % 4 - row_ids % 4 + 4, 4
    )
    col_ids = lane_ids((1, nb))

    def link(k, carry):
        before, final = carry
        r = row_at(k)
        for s in range(SLOTS):
            name = cols_ref[0, s, r]
            before = jnp.where((named_now == name) & (place > k), 4 * k + s, before)
            final = jnp.where(col_ids == name, 4 * k + s, final)
        return before, final

    before, final = lax.fori_loop(
        0, nb, link,
        (jnp.full((SLOTS, nb), SLOTS * nb, jnp.int32), jnp.zeros((1, nb), jnp.int32)),
    )
    table_vm[...] = jnp.zeros_like(table_vm)
    table_vm[:SLOTS, :nb] = before
    table_vm[SLOTS : SLOTS + 1, :nb] = final
    table_copy = pltpu.make_async_copy(table_vm, table, own_sem.at[1])
    table_copy.start()
    chain[SLOTS * nb] = jnp.zeros((2 * FEAT, BLK), F32)

    raw, top, pair = (raw_even, raw_odd), (top_even, top_odd), (pair_even, pair_odd)

    def arrive(i, c):
        landed(kv_in.at[pl.ds(0, 4)], kv_r.at[i])
        for j in range(4):
            b = row_at(4 * i + j)
            natural[b] = jnp.transpose(kv_in[b].astype(F32)).astype(BF16)
        return c

    lax.fori_loop(0, ng, arrive, 0)
    table_copy.wait()

    def spread_pieces(r, side):
        queries, cot = qd_in[r, :FEAT], qd_in[r, FEAT:]
        empty = jnp.zeros((FEAT, BLK), BF16)
        upper, lower = [queries, empty], [empty, cot]
        if side:
            upper, lower = upper[::-1], lower[::-1]
        return jnp.concatenate(
            [jnp.concatenate(upper, axis=1), jnp.concatenate(lower, axis=1)], axis=0
        )

    def score_stage(k, p):
        r = row_at(k)
        count = counts_ref[0, r]
        keys = jnp.concatenate([natural[cols_ref[0, s, r]] for s in range(SLOTS)], axis=0)
        both = jnp.dot(keys, spread_pieces(r, 0), preferred_element_type=F32)
        best = None
        for s in range(SLOTS):
            block = both[s * BLK : (s + 1) * BLK]
            scores = block[:, :BLK]
            if s:
                scores = jnp.where(s < count, scores, -jnp.inf)
            raw[p][s, :, :BLK] = scores
            raw[p][s, :, BLK:] = block[:, BLK:]
            peak = jnp.max(scores, axis=0, keepdims=True)
            best = peak if best is None else jnp.maximum(best, peak)
        top[p][...] = best * to_exp2

    def soft_stage(p):
        peak = top[p][...]
        total = mixed = None
        for s in range(SLOTS):
            weights = jnp.exp2(raw[p][s, :, :BLK] * to_exp2 - peak)
            t = jnp.sum(weights, axis=0, keepdims=True)
            m = jnp.sum(weights * raw[p][s, :, BLK:], axis=0, keepdims=True)
            total = t if total is None else total + t
            mixed = m if mixed is None else mixed + m
            raw[p][s, :, :BLK] = weights
        inverse = 1.0 / total
        delta = mixed * inverse
        for s in range(SLOTS):
            prob = raw[p][s, :, :BLK] * inverse
            rows = slice(s * BLK, (s + 1) * BLK)
            pair[p][rows, :BLK] = prob.astype(BF16)
            pair[p][rows, BLK:] = (prob * (raw[p][s, :, BLK:] - delta)).astype(BF16)

    def grad_stage(k, p):
        r = row_at(k)
        named = [cols_ref[0, s, r] for s in range(SLOTS)]
        both = pair[p][...]
        turned = jnp.concatenate([kv_in[n] for n in named], axis=1)
        row_side = jnp.dot(turned, both, preferred_element_type=F32)
        row_out[r, :FEAT] = row_side[FEAT:, :BLK].astype(BF16)
        row_out[r, FEAT:] = (row_side[:FEAT, BLK:] * scale).astype(BF16)
        key_side = lax.dot_general(
            spread_pieces(r, 1), both, (((1,), (1,)), ((), ())), preferred_element_type=F32
        )
        for s in range(SLOTS):
            chain[4 * k + s] = key_side[:, s * BLK : (s + 1) * BLK] + chain[table[s, r]]

    def piece_copy(lo, send_sem, recv_sem):
        def copy(i, j):
            peer = row_at(4 * i + j)
            piece = pl.ds(lo, FEAT)
            return remote(
                row_out.at[peer, piece], row_in.at[me_s, piece],
                send_sem, recv_sem(i), me_d, peer,
            )

        return copy

    late_copy = piece_copy(0, late_s, lambda i: late_r)
    row_copy = piece_copy(FEAT, row_s, lambda i: row_r.at[i])

    def col_copy(i, j):
        peer = peer_at(me_s, i, j, ng, 1)
        return remote(
            col_out.at[peer], col_in.at[me_s], col_s, col_r.at[i], me_d, peer
        )

    def own_piece(lo, sem):
        piece = pl.ds(lo, FEAT)
        return pltpu.make_async_copy(row_out.at[me_s, piece], row_in.at[me_s, piece], sem)

    own_late = own_piece(0, late_r)
    own_row = own_piece(FEAT, row_r.at[0])
    own_col = pltpu.make_async_copy(col_out.at[me_s], col_in.at[me_s], col_r.at[0])
    def one_step(k, p, grad=True):
        score_stage(k + 1, 1 - p)
        soft_stage(p)
        if grad:
            grad_stage(k - 1, 1 - p)

    landed(qd_in.at[pl.ds(0, 4)], qd_r.at[0])
    score_stage(0, 0)
    one_step(0, 0, grad=False)
    one_step(1, 1)
    one_step(2, 0)

    def four_rows(i, c):
        @pl.when(i > 0)
        def _():
            start_group(i - 1, own_row, row_copy)

        landed(qd_in.at[pl.ds(0, 4)], qd_r.at[i + 1])
        for u in range(4):
            one_step(3 + 4 * i + u, (1 + u) % 2)
        return c

    lax.fori_loop(0, ng - 1, four_rows, 0)
    start_group(ng - 2, own_row, row_copy)
    soft_stage(1)
    grad_stage(nb - 2, 0)
    grad_stage(nb - 1, 1)
    start_group(ng - 1, own_row, row_copy)
    own_late.start()

    def col_send(i, c):
        for j in range(4):
            peer = peer_at(me_s, i, j, ng, 1)
            total = chain[table[SLOTS, peer]]
            col_out[peer, :FEAT] = (total[:FEAT] * scale).astype(BF16)
            col_out[peer, FEAT:] = total[FEAT:].astype(BF16)
        start_group(i, own_col, col_copy)
        return c

    lax.fori_loop(0, ng, col_send, 0)
    others = nd // 2 - 1
    if others:
        landed(xt_all.at[:, pl.ds(0, others * BLK)], xt_r)
    for k in range(1, nd // 2):
        share_copy(k).start()

    def late_send(i, c):
        @pl.when(i > 0)
        def _():
            late_copy(i, 0).start()

        for j in range(1, 4):
            late_copy(i, j).start()
        return c

    lax.fori_loop(0, ng, late_send, 0)
    landed(kv_out.at[pl.ds(0, ns - 1)], kv_s)
    landed(qd_out.at[pl.ds(0, ns - 1)], qd_s)
    if others:
        landed(xt_all.at[:, pl.ds(0, others * BLK)], xt_s)
    landed(xt_all.at[:, pl.ds(0, nd // 2 * BLK)], share_s)

    def tile_own(g, m):
        t = m * ng + g
        return pltpu.make_async_copy(
            dq.at[g, pl.ds(m * BLK, BLK)], wg_in.at[lanes(t % tpd), lanes(me_d)],
            tile_r.at[t % tpd],
        )

    def tile_copy(g, m):
        t = m * ng + g
        return remote(
            dq.at[g, pl.ds(m * BLK, BLK)], wg_in.at[lanes(t % tpd), lanes(me_d)],
            tile_s, tile_r.at[t % tpd], t // tpd, me_s,
        )

    def tile_send(g, m):
        t = m * ng + g

        @pl.when(t // tpd == me_d)
        def _():
            tile_own(g, m).start()

        @pl.when(t // tpd != me_d)
        def _():
            tile_copy(g, m).start()

    def take_rows(i, c):
        g = sent_group(i)
        landed(row_in.at[pl.ds(0, 4), pl.ds(FEAT, FEAT)], row_r.at[i])
        for j in range(4):
            dq[g, j * FEAT : (j + 1) * FEAT] = row_in[4 * g + j, FEAT:]
        tile_send(g, 0)
        return c

    def take_late(g, c):
        mix = jnp.concatenate([row_in[4 * g + j, :FEAT] for j in range(4)], axis=0)
        mix_ref[:, lanes(g)] = jnp.transpose(mix.astype(F32)).astype(BF16)
        return c

    def take_cols(i, c):
        g = got_group(i)
        landed(col_in.at[pl.ds(0, 4)], col_r.at[i])
        for j in range(4):
            dq[g, BLK + j * FEAT : BLK + (j + 1) * FEAT] = col_in[4 * g + j, :FEAT]
            dq[g, 2 * BLK + j * FEAT : 2 * BLK + (j + 1) * FEAT] = col_in[4 * g + j, FEAT:]
        tile_send(g, 1)
        tile_send(g, 2)
        return c

    lax.fori_loop(0, ng, take_rows, 0)
    lax.fori_loop(0, ng, take_cols, 0)
    xt_keep.wait()
    landed(xt_all.at[:, pl.ds(0, nd // 2 * BLK)], share_r)

    chunk = nz * FEAT
    half = chunk // 2
    up, down = lax.rem(me_y + 1, ny), lax.rem(me_y + ny - 1, ny)
    across = lax.rem(me_y + 2, ny)

    def rows_of(y, which):
        return pl.ds(pl.multiple_of(y * chunk + which * half, half), half)

    def relay_copy(t, way):
        return remote(
            part.at[t, rows_of(across, way)], relay.at[t, way],
            relay_s, relay_r.at[t], me_d, (up, down)[way] * nz + me_z,
        )

    def fold_copy(t, way, which):
        return remote(
            part.at[t, rows_of((up, down)[way], which)], fold.at[t, way, which],
            fold_s, fold_r.at[t],
            me_d, (up, down)[way] * nz + me_z,
        )

    def last_copy(k):
        to = lax.rem(me_z + k, nz)
        return remote(
            mid.at[pl.ds(pl.multiple_of(to * FEAT, FEAT), FEAT)], last_in.at[k - 1],
            last_s, last_r, me_d, me_y * nz + to,
        )

    for first, last in ((0, tpd - 1), (tpd - 1, tpd)):
        for t in range(first, last):
            landed(wg_in.at[pl.ds(t * BLK, BLK)], tile_r.at[t])
        partial_sum = lax.dot_general(
            xt_all[...], wg_in[first * BLK : last * BLK], (((1,), (1,)), ((), ())),
            preferred_element_type=F32,
        ).astype(BF16)
        for t in range(first, last):
            part[t] = partial_sum[:, (t - first) * BLK : (t - first + 1) * BLK]
            for way in range(2):
                relay_copy(t, way).start()
                fold_copy(t, way, 1 - way).start()

    def node_cols(n, c):
        width = 2 * BLK
        cols = pl.ds(pl.multiple_of(n * width, width), width)
        total = jnp.zeros((width, BLK), F32)
        for g in range(ng):
            total += jnp.dot(w_vm[g, cols], dq[g], preferred_element_type=F32)
        gn_ref[:, cols] = jnp.transpose(total).astype(BF16)
        return c

    steps_gn = hidden // (2 * BLK)
    lax.fori_loop(0, steps_gn // 2, node_cols, 0)
    for t in range(tpd):
        landed(relay.at[t], relay_r.at[t])
        for way in range(2):
            rows = rows_of((up, down)[way], way)
            part[t, rows] = (
                part[t, rows].astype(F32) + relay[t, way].astype(F32)
            ).astype(BF16)
            fold_copy(t, way, way).start()
    lax.fori_loop(steps_gn // 2, steps_gn, node_cols, 0)
    gn_done = pltpu.make_async_copy(gn_ref, gn_out, out_sem.at[1])
    gn_done.start()
    for t in range(tpd):
        landed(fold.at[t], fold_r.at[t])
        for which in range(2):
            total = part[t, rows_of(me_y, which)].astype(F32)
            for way in range(2):
                total += fold[t, way, which].astype(F32)
            mid[which * half : (which + 1) * half, t * BLK : (t + 1) * BLK] = total.astype(BF16)
    for k in sorted(range(1, nz), key=lambda k: -min(k, nz - k)):
        last_copy(k).start()

    landed(row_in.at[:, pl.ds(0, FEAT)], late_r)
    lax.fori_loop(0, ng, take_late, 0)
    mix_done = pltpu.make_async_copy(mix_ref, mix_out, out_sem.at[0])
    mix_done.start()
    landed(row_out.at[pl.ds(0, ns - 1), pl.ds(FEAT, FEAT)], row_s)
    landed(row_out.at[pl.ds(0, ns - 1), pl.ds(0, FEAT)], late_s)
    landed(col_out.at[pl.ds(0, ns - 1)], col_s)
    landed(dq.at[pl.ds(0, ng - 1)], tile_s)
    landed(relay, relay_s)
    landed(fold, fold_s)
    landed(last_in, last_r)
    total = mid[pl.ds(pl.multiple_of(me_z * FEAT, FEAT), FEAT)].astype(F32)
    for k in range(1, nz):
        total += last_in[k - 1].astype(F32)
    wg_ref[...] = total
    wg_done = pltpu.make_async_copy(wg_ref, wg_out, out_sem.at[2])
    wg_done.start()
    landed(last_in, last_s)
    mix_done.wait()
    gn_done.wait()
    wg_done.wait()


def settle_kernel(mix_in, gn_in, wg_in, mix_out, gn_out, wg_out, mix_vm, gn_vm, wg_vm, sem):
    triples = ((mix_in, mix_vm, mix_out), (gn_in, gn_vm, gn_out), (wg_in, wg_vm, wg_out))
    loads = [pltpu.make_async_copy(a, b, sem.at[0, n]) for n, (a, b, _) in enumerate(triples)]
    stores = [pltpu.make_async_copy(b, c, sem.at[1, n]) for n, (_, b, c) in enumerate(triples)]
    for load in loads:
        load.start()
    for load, store in zip(loads, stores):
        load.wait()
        store.start()
    for store in stores:
        store.wait()


def per_device(nd, ns, nodes, w_qkv, incoming_adjoint, block_cols, block_counts):
    rows, hidden = nodes.shape[1:]
    ny, nz = 4, ns // 4
    ng = ns // 4
    tpd = 3 * ng // nd
    chunk = nz * FEAT
    any_spec = pl.BlockSpec(memory_space=pl.ANY)
    dma = pltpu.SemaphoreType.DMA
    slots_first = jnp.swapaxes(block_cols, 1, 2)
    out_shape = (
        jax.ShapeDtypeStruct((rows, hidden), BF16),
        jax.ShapeDtypeStruct((rows, hidden), BF16),
        jax.ShapeDtypeStruct((FEAT, tpd * BLK), F32),
    )
    out_buffers = [pltpu.VMEM(out.shape, out.dtype) for out in out_shape]
    results = pl.pallas_call(
        functools.partial(whole_kernel, nd, ns, ny, nz, tpd),
        out_shape=out_shape,
        in_specs=[any_spec] * 5,
        out_specs=(any_spec,) * 3,
        scratch_shapes=[
            pltpu.SMEM((1, SLOTS, ns), jnp.int32),
            pltpu.VMEM((SLOTS, ns), jnp.int32),
            pltpu.SMEM((1, ns), jnp.int32),
            *out_buffers,
            pltpu.VMEM((rows, hidden), BF16),
            pltpu.VMEM((rows, hidden), BF16),
            pltpu.VMEM((ng, hidden, 3 * BLK), BF16),
            pltpu.VMEM((ns, 2 * FEAT, BLK), BF16),
            pltpu.VMEM((ns, 2 * FEAT, BLK), BF16),
            pltpu.VMEM((ns, 2 * FEAT, BLK), BF16),
            pltpu.VMEM((ns, 2 * FEAT, BLK), BF16),
            pltpu.VMEM((ns, BLK, 2 * FEAT), BF16),
            pltpu.VMEM((hidden, BLK), BF16),
            pltpu.VMEM((hidden, nd * BLK), BF16),
            pltpu.VMEM((SLOTS * ns + 1, 2 * FEAT, BLK), F32),
            pltpu.VMEM((ns, 2 * FEAT, BLK), BF16),
            pltpu.VMEM((ns, 2 * FEAT, BLK), BF16),
            pltpu.VMEM((ns, 2 * FEAT, BLK), BF16),
            pltpu.VMEM((ns, 2 * FEAT, BLK), BF16),
            pltpu.VMEM((SLOTS, BLK, 2 * BLK), F32),
            pltpu.VMEM((SLOTS, BLK, 2 * BLK), F32),
            pltpu.VMEM((1, BLK), F32),
            pltpu.VMEM((1, BLK), F32),
            pltpu.VMEM((SLOTS * BLK, 2 * BLK), BF16),
            pltpu.VMEM((SLOTS * BLK, 2 * BLK), BF16),
            pltpu.VMEM((8, BLK), jnp.int32),
            pltpu.SMEM((8, BLK), jnp.int32),
            pltpu.VMEM((ng, 3 * BLK, BLK), BF16),
            pltpu.VMEM((tpd * BLK, nd * BLK), BF16),
            pltpu.VMEM((tpd, hidden, BLK), BF16),
            pltpu.VMEM((tpd, 2, chunk // 2, BLK), BF16),
            pltpu.VMEM((tpd, 2, 2, chunk // 2, BLK), BF16),
            pltpu.VMEM((chunk, tpd * BLK), BF16),
            pltpu.VMEM((nz - 1, FEAT, tpd * BLK), BF16),
            dma((2, ng)),
            dma((5,)),
            dma,
            dma((ng,)),
            dma,
            dma((ng,)),
            dma,
            dma,
            dma,
            dma((ng,)),
            dma,
            dma((ng,)),
            dma((2,)),
            dma,
            dma((tpd,)),
            dma,
            dma((tpd,)),
            dma,
            dma((tpd,)),
            dma,
            dma,
            dma,
            dma,
            dma,
            dma,
            dma((3,)),
        ],
        compiler_params=pltpu.CompilerParams(
            collective_id=1, has_side_effects=True, vmem_limit_bytes=VMEM_LIMIT
        ),
        name="whole",
    )(nodes, w_qkv, incoming_adjoint, slots_first, block_counts)
    mixture, grad_nodes, weight_grad = pl.pallas_call(
        settle_kernel,
        out_shape=out_shape,
        in_specs=[any_spec] * 3,
        out_specs=(any_spec,) * 3,
        scratch_shapes=[*out_buffers, dma((2, 3))],
        compiler_params=pltpu.CompilerParams(vmem_limit_bytes=VMEM_LIMIT),
        name="settle",
    )(*results)
    return (mixture[None], grad_nodes[None], jnp.transpose(weight_grad))


def solution(mesh):
    nd, ns = mesh.shape["dp"], mesh.shape["seq"]
    in_specs = (P("dp", "seq", None), P(), P("dp", "seq", None), P("dp", None, None), P("dp", None))
    out_specs = (P("dp", "seq", None), P("dp", "seq", None), P("dp", "seq"))
    return jax.shard_map(
        functools.partial(per_device, nd, ns),
        mesh=mesh,
        in_specs=in_specs,
        out_specs=out_specs,
        check_vma=False,
    )
```

```python
import functools
import math

import jax
import jax.numpy as jnp
from jax import lax
from jax.experimental import pallas as pl
from jax.experimental.pallas import tpu as pltpu
from jax.sharding import PartitionSpec as P

MESH = pl.DeviceIdType.MESH
BLK = 128
FEAT = 32
SLOTS = 4
F32 = jnp.float32
BF16 = jnp.bfloat16
VMEM_LIMIT = 62 * 1024 * 1024


def lane_ids(shape):
    return lax.broadcasted_iota(jnp.int32, shape, len(shape) - 1)


def greet(me_d, me_s, nd, ns):
    barrier = pltpu.get_barrier_semaphore()

    def seq_hello(k, c):
        pl.semaphore_signal(
            barrier, inc=1, device_id=(me_d, lax.rem(me_s + k, ns)), device_id_type=MESH
        )
        return c

    def dp_hello(k, c):
        pl.semaphore_signal(
            barrier, inc=1, device_id=(lax.rem(me_d + k, nd), me_s), device_id_type=MESH
        )
        return c

    lax.fori_loop(1, ns, seq_hello, 0)
    lax.fori_loop(1, nd, dp_hello, 0)
    return barrier


def peer_at(me_s, i, j, ng, sign):
    group = lax.rem(me_s // 4 + sign * i + ng, ng)
    return 4 * group + lax.rem(me_s % 4 + sign * j + 4, 4)


def whole_kernel(
    nd, ns, ny, nz, tpd,
    x_in, w_in, cot_in, cols_in, counts_in,
    mix_out, gn_out, wg_out,
    cols_ref, cols_vec, counts_ref, mix_ref, gn_ref, wg_ref, x_vm, cot_vm, w_vm, kv_out, kv_in, qd_out, qd_in, natural, xt_own, xt_all,
    chain, row_out, col_out, row_in, col_in,
    raw_even, raw_odd, top_even, top_odd, pair_even, pair_odd,
    table_vm, table, dq, wg_in, part, relay, fold, mid, last_in,
    w_sem, load_sem, kv_s, kv_r, qd_s, qd_r, xt_s, xt_r, row_s, row_r, col_s, col_r,
    own_sem, tile_s, tile_r, relay_s, relay_r, fold_s, fold_r, last_s, last_r, late_s, late_r, share_s, share_r, out_sem,
    zpart, z_in, z_mid, y_in, z_s, z_r, y_s, y_r,
):
    me_d, me_s = lax.axis_index("dp"), lax.axis_index("seq")
    me_y, me_z = me_s // nz, me_s % nz
    ng = ns // 4
    my_group = me_s // 4
    hidden = ng * BLK
    nb = ns
    scale = 1.0 / math.sqrt(FEAT)
    to_exp2 = scale * math.log2(math.e)

    def lanes(t):
        return pl.ds(pl.multiple_of(t * BLK, BLK), BLK)

    def sent_group(i):
        return lax.rem(my_group + i, ng)

    def got_group(i):
        return lax.rem(my_group - i + ng, ng)

    def row_at(k):
        return peer_at(me_s, k // 4, k % 4, ng, -1)

    def remote(src, dst, send_sem, recv_sem, d, s):
        return pltpu.make_async_remote_copy(
            src_ref=src, dst_ref=dst, send_sem=send_sem, recv_sem=recv_sem,
            device_id=(d, s), device_id_type=MESH,
        )

    def landed(ref, sem):
        pltpu.make_async_copy(ref, ref, sem).wait()

    barrier = greet(me_d, me_s, nd, ns)
    load_x = pltpu.make_async_copy(x_in.at[0], x_vm, load_sem.at[0])
    load_cot = pltpu.make_async_copy(cot_in.at[0], cot_vm, load_sem.at[1])
    load_x.start()

    def w_start(part, i):
        g = sent_group(i)
        for m in ((1, 2), (0,))[part]:
            pltpu.make_async_copy(
                w_in.at[:, lanes(m * ng + g)],
                w_vm.at[g, :, pl.ds(m * BLK, BLK)],
                w_sem.at[part, i],
            ).start()

    def kv_weights(i, c):
        w_start(0, i)
        return c

    def q_weights(i, c):
        w_start(1, i)
        return c

    small_loads = [
        pltpu.make_async_copy(src, dst, load_sem.at[2 + n])
        for n, (src, dst) in enumerate(
            ((cols_in, cols_ref), (cols_in.at[0], cols_vec), (counts_in, counts_ref))
        )
    ]
    lax.fori_loop(0, ng, kv_weights, 0)
    load_cot.start()
    lax.fori_loop(0, ng, q_weights, 0)
    for load in small_loads:
        load.start()
    load_x.wait()

    def pieces_copy(out, into, send_sem, recv_sem):
        def copy(i, j):
            peer = peer_at(me_s, i, j, ng, 1)
            return remote(out.at[peer], into.at[me_s], send_sem, recv_sem.at[i], me_d, peer)

        return copy, pltpu.make_async_copy(out.at[me_s], into.at[me_s], recv_sem.at[0])

    kv_copy, own_kv = pieces_copy(kv_out, kv_in, kv_s, kv_r)
    qd_copy, own_qd = pieces_copy(qd_out, qd_in, qd_s, qd_r)

    def start_group(i, own, copy):
        @pl.when(i == 0)
        def _():
            own.start()

        @pl.when(i > 0)
        def _():
            copy(i, 0).start()

        for j in range(1, 4):
            copy(i, j).start()

    def project_kv(i, c):
        g = sent_group(i)
        landed(w_vm.at[g, :, pl.ds(BLK, 2 * BLK)], w_sem.at[0, i])
        flat = jnp.dot(x_vm[...], w_vm[g, :, BLK:], preferred_element_type=F32)
        for m in range(2):
            turned = jnp.transpose(flat[:, m * BLK : (m + 1) * BLK]).astype(BF16)
            for j in range(4):
                kv_out[4 * g + j, m * FEAT : (m + 1) * FEAT] = turned[
                    j * FEAT : (j + 1) * FEAT
                ]

        @pl.when(i == 0)
        def _():
            pl.semaphore_wait(barrier, ns + nd - 2)

        start_group(i, own_kv, kv_copy)
        return c

    def project_q(i, c):
        g = sent_group(i)
        landed(w_vm.at[g, :, pl.ds(0, BLK)], w_sem.at[1, i])
        flat = jnp.dot(x_vm[...], w_vm[g, :, :BLK], preferred_element_type=F32)
        for m, piece in enumerate((flat, cot_vm[:, lanes(g)].astype(F32))):
            turned = jnp.transpose(piece).astype(BF16)
            for j in range(4):
                qd_out[4 * g + j, m * FEAT : (m + 1) * FEAT] = turned[
                    j * FEAT : (j + 1) * FEAT
                ]
        start_group(i, own_qd, qd_copy)
        return c

    lax.fori_loop(0, ng, project_kv, 0)
    load_cot.wait()
    lax.fori_loop(0, ng, project_q, 0)

    xt_own[...] = jnp.transpose(x_vm[...].astype(F32)).astype(BF16)
    xt_keep = pltpu.make_async_copy(xt_own, xt_all.at[:, lanes(me_d)], own_sem.at[0])
    xt_keep.start()

    sibling = me_d + 1 - 2 * (me_d % 2)

    def xt_copy(k):
        return remote(
            xt_own, xt_all.at[:, lanes(me_d)], xt_s, xt_r,
            lax.rem(me_d + 2 * k, nd), me_s,
        )

    def share_copy(k):
        here = lanes(lax.rem(me_d - 2 * k + nd, nd))
        return remote(
            xt_all.at[:, here] if k else xt_own, xt_all.at[:, here],
            share_s, share_r, sibling, me_s,
        )

    for k in range(1, nd // 2):
        xt_copy(k).start()
    share_copy(0).start()

    for load in small_loads:
        load.wait()
    named_now = cols_vec[...]
    row_ids = lane_ids((SLOTS, nb))
    place = 4 * lax.rem(my_group - row_ids // 4 + ng, ng) + lax.rem(
        me_s % 4 - row_ids % 4 + 4, 4
    )
    col_ids = lane_ids((1, nb))

    def link(k, carry):
        before, final = carry
        r = row_at(k)
        for s in range(SLOTS):
            name = cols_ref[0, s, r]
            before = jnp.where((named_now == name) & (place > k), 4 * k + s, before)
            final = jnp.where(col_ids == name, 4 * k + s, final)
        return before, final

    before, final = lax.fori_loop(
        0, nb, link,
        (jnp.full((SLOTS, nb), SLOTS * nb, jnp.int32), jnp.zeros((1, nb), jnp.int32)),
    )
    table_vm[...] = jnp.zeros_like(table_vm)
    table_vm[:SLOTS, :nb] = before
    table_vm[SLOTS : SLOTS + 1, :nb] = final
    table_copy = pltpu.make_async_copy(table_vm, table, own_sem.at[1])
    table_copy.start()
    chain[SLOTS * nb] = jnp.zeros((2 * FEAT, BLK), F32)

    raw, top, pair = (raw_even, raw_odd), (top_even, top_odd), (pair_even, pair_odd)

    def arrive(i, c):
        landed(kv_in.at[pl.ds(0, 4)], kv_r.at[i])
        for j in range(4):
            b = row_at(4 * i + j)
            natural[b] = jnp.transpose(kv_in[b].astype(F32)).astype(BF16)
        return c

    lax.fori_loop(0, ng, arrive, 0)
    table_copy.wait()

    def spread_pieces(r, side):
        queries, cot = qd_in[r, :FEAT], qd_in[r, FEAT:]
        empty = jnp.zeros((FEAT, BLK), BF16)
        upper, lower = [queries, empty], [empty, cot]
        if side:
            upper, lower = upper[::-1], lower[::-1]
        return jnp.concatenate(
            [jnp.concatenate(upper, axis=1), jnp.concatenate(lower, axis=1)], axis=0
        )

    def score_stage(k, p):
        r = row_at(k)
        count = counts_ref[0, r]
        keys = jnp.concatenate([natural[cols_ref[0, s, r]] for s in range(SLOTS)], axis=0)
        both = jnp.dot(keys, spread_pieces(r, 0), preferred_element_type=F32)
        best = None
        for s in range(SLOTS):
            block = both[s * BLK : (s + 1) * BLK]
            scores = block[:, :BLK]
            if s:
                scores = jnp.where(s < count, scores, -jnp.inf)
            raw[p][s, :, :BLK] = scores
            raw[p][s, :, BLK:] = block[:, BLK:]
            peak = jnp.max(scores, axis=0, keepdims=True)
            best = peak if best is None else jnp.maximum(best, peak)
        top[p][...] = best * to_exp2

    def soft_stage(p):
        peak = top[p][...]
        total = mixed = None
        for s in range(SLOTS):
            weights = jnp.exp2(raw[p][s, :, :BLK] * to_exp2 - peak)
            t = jnp.sum(weights, axis=0, keepdims=True)
            m = jnp.sum(weights * raw[p][s, :, BLK:], axis=0, keepdims=True)
            total = t if total is None else total + t
            mixed = m if mixed is None else mixed + m
            raw[p][s, :, :BLK] = weights
        inverse = 1.0 / total
        delta = mixed * inverse
        for s in range(SLOTS):
            prob = raw[p][s, :, :BLK] * inverse
            rows = slice(s * BLK, (s + 1) * BLK)
            pair[p][rows, :BLK] = prob.astype(BF16)
            pair[p][rows, BLK:] = (prob * (raw[p][s, :, BLK:] - delta)).astype(BF16)

    def grad_stage(k, p):
        r = row_at(k)
        named = [cols_ref[0, s, r] for s in range(SLOTS)]
        both = pair[p][...]
        turned = jnp.concatenate([kv_in[n] for n in named], axis=1)
        row_side = jnp.dot(turned, both, preferred_element_type=F32)
        row_out[r, :FEAT] = row_side[FEAT:, :BLK].astype(BF16)
        row_out[r, FEAT:] = (row_side[:FEAT, BLK:] * scale).astype(BF16)
        key_side = lax.dot_general(
            spread_pieces(r, 1), both, (((1,), (1,)), ((), ())), preferred_element_type=F32
        )
        for s in range(SLOTS):
            chain[4 * k + s] = key_side[:, s * BLK : (s + 1) * BLK] + chain[table[s, r]]

    def piece_copy(lo, send_sem, recv_sem):
        def copy(i, j):
            peer = row_at(4 * i + j)
            piece = pl.ds(lo, FEAT)
            return remote(
                row_out.at[peer, piece], row_in.at[me_s, piece],
                send_sem, recv_sem(i), me_d, peer,
            )

        return copy

    late_copy = piece_copy(0, late_s, lambda i: late_r)
    row_copy = piece_copy(FEAT, row_s, lambda i: row_r.at[i])

    def col_copy(i, j):
        peer = peer_at(me_s, i, j, ng, 1)
        return remote(
            col_out.at[peer], col_in.at[me_s], col_s, col_r.at[i], me_d, peer
        )

    def own_piece(lo, sem):
        piece = pl.ds(lo, FEAT)
        return pltpu.make_async_copy(row_out.at[me_s, piece], row_in.at[me_s, piece], sem)

    own_late = own_piece(0, late_r)
    own_row = own_piece(FEAT, row_r.at[0])
    own_col = pltpu.make_async_copy(col_out.at[me_s], col_in.at[me_s], col_r.at[0])
    def one_step(k, p, grad=True):
        score_stage(k + 1, 1 - p)
        soft_stage(p)
        if grad:
            grad_stage(k - 1, 1 - p)

    landed(qd_in.at[pl.ds(0, 4)], qd_r.at[0])
    score_stage(0, 0)
    one_step(0, 0, grad=False)
    one_step(1, 1)
    one_step(2, 0)

    def four_rows(i, c):
        @pl.when(i > 0)
        def _():
            start_group(i - 1, own_row, row_copy)

        landed(qd_in.at[pl.ds(0, 4)], qd_r.at[i + 1])
        for u in range(4):
            one_step(3 + 4 * i + u, (1 + u) % 2)
        return c

    lax.fori_loop(0, ng - 1, four_rows, 0)
    start_group(ng - 2, own_row, row_copy)
    soft_stage(1)
    grad_stage(nb - 2, 0)
    grad_stage(nb - 1, 1)
    start_group(ng - 1, own_row, row_copy)
    own_late.start()

    def col_send(i, c):
        for j in range(4):
            peer = peer_at(me_s, i, j, ng, 1)
            total = chain[table[SLOTS, peer]]
            col_out[peer, :FEAT] = (total[:FEAT] * scale).astype(BF16)
            col_out[peer, FEAT:] = total[FEAT:].astype(BF16)
        start_group(i, own_col, col_copy)
        return c

    lax.fori_loop(0, ng, col_send, 0)
    others = nd // 2 - 1
    if others:
        landed(xt_all.at[:, pl.ds(0, others * BLK)], xt_r)
    for k in range(1, nd // 2):
        share_copy(k).start()

    def late_send(i, c):
        @pl.when(i > 0)
        def _():
            late_copy(i, 0).start()

        for j in range(1, 4):
            late_copy(i, j).start()
        return c

    lax.fori_loop(0, ng, late_send, 0)
    landed(kv_out.at[pl.ds(0, ns - 1)], kv_s)
    landed(qd_out.at[pl.ds(0, ns - 1)], qd_s)
    if others:
        landed(xt_all.at[:, pl.ds(0, others * BLK)], xt_s)
    landed(xt_all.at[:, pl.ds(0, nd // 2 * BLK)], share_s)

    def tile_own(g, m):
        t = m * ng + g
        return pltpu.make_async_copy(
            dq.at[g, pl.ds(m * BLK, BLK)], wg_in.at[lanes(t % tpd), lanes(me_d)],
            tile_r.at[t % tpd],
        )

    def tile_copy(g, m):
        t = m * ng + g
        return remote(
            dq.at[g, pl.ds(m * BLK, BLK)], wg_in.at[lanes(t % tpd), lanes(me_d)],
            tile_s, tile_r.at[t % tpd], t // tpd, me_s,
        )

    def tile_send(g, m):
        t = m * ng + g

        @pl.when(t // tpd == me_d)
        def _():
            tile_own(g, m).start()

        @pl.when(t // tpd != me_d)
        def _():
            tile_copy(g, m).start()

    def take_rows(i, c):
        g = sent_group(i)
        landed(row_in.at[pl.ds(0, 4), pl.ds(FEAT, FEAT)], row_r.at[i])
        for j in range(4):
            dq[g, j * FEAT : (j + 1) * FEAT] = row_in[4 * g + j, FEAT:]
        tile_send(g, 0)
        return c

    def take_late(g, c):
        mix = jnp.concatenate([row_in[4 * g + j, :FEAT] for j in range(4)], axis=0)
        mix_ref[:, lanes(g)] = jnp.transpose(mix.astype(F32)).astype(BF16)
        return c

    def take_cols(i, c):
        g = got_group(i)
        landed(col_in.at[pl.ds(0, 4)], col_r.at[i])
        for j in range(4):
            dq[g, BLK + j * FEAT : BLK + (j + 1) * FEAT] = col_in[4 * g + j, :FEAT]
            dq[g, 2 * BLK + j * FEAT : 2 * BLK + (j + 1) * FEAT] = col_in[4 * g + j, FEAT:]
        tile_send(g, 1)
        tile_send(g, 2)
        return c

    lax.fori_loop(0, ng, take_rows, 0)
    lax.fori_loop(0, ng, take_cols, 0)
    xt_keep.wait()
    landed(xt_all.at[:, pl.ds(0, nd // 2 * BLK)], share_r)

    chunk = nz * FEAT
    half = chunk // 2
    up, down = lax.rem(me_y + 1, ny), lax.rem(me_y + ny - 1, ny)
    across = lax.rem(me_y + 2, ny)

    def rows_of(y, which):
        return pl.ds(pl.multiple_of(y * chunk + which * half, half), half)

    def relay_copy(t, way):
        return remote(
            part.at[t, rows_of(across, way)], relay.at[t, way],
            relay_s, relay_r.at[t], me_d, (up, down)[way] * nz + me_z,
        )

    def fold_copy(t, way, which):
        return remote(
            part.at[t, rows_of((up, down)[way], which)], fold.at[t, way, which],
            fold_s, fold_r.at[t],
            me_d, (up, down)[way] * nz + me_z,
        )

    def last_copy(k):
        to = lax.rem(me_z + k, nz)
        return remote(
            mid.at[pl.ds(pl.multiple_of(to * FEAT, FEAT), FEAT)], last_in.at[k - 1],
            last_s, last_r, me_d, me_y * nz + to,
        )

    def z_copy(k):
        to = lax.rem(me_z + k, nz)
        return remote(zpart.at[:, to], z_in.at[k - 1], z_s, z_r, me_d, me_y * nz + to)

    def y_copy(k):
        to = lax.rem(me_y + k, ny)
        return remote(z_mid.at[to], y_in.at[k - 1], y_s, y_r, me_d, to * nz + me_z)

    def contract(first, last):
        for t in range(first, last):
            landed(wg_in.at[pl.ds(t * BLK, BLK)], tile_r.at[t])
        return lax.dot_general(
            xt_all[...], wg_in[first * BLK : last * BLK], (((1,), (1,)), ((), ())),
            preferred_element_type=F32,
        ).astype(BF16)

    far_first = sorted(range(1, nz), key=lambda k: -min(k, nz - k))
    pairs = tpd - 1
    zpart[...] = contract(pairs, tpd).reshape(ny, nz, FEAT, BLK)
    for k in far_first:
        z_copy(k).start()
    partial_sum = contract(0, pairs)
    for t in range(pairs):
        part[t] = partial_sum[:, t * BLK : (t + 1) * BLK]
        for way in range(2):
            relay_copy(t, way).start()
    for t in range(pairs):
        for way in range(2):
            fold_copy(t, way, 1 - way).start()

    def node_cols(n, c):
        width = 2 * BLK
        cols = pl.ds(pl.multiple_of(n * width, width), width)
        total = jnp.zeros((width, BLK), F32)
        for g in range(ng):
            total += jnp.dot(w_vm[g, cols], dq[g], preferred_element_type=F32)
        gn_ref[:, cols] = jnp.transpose(total).astype(BF16)
        return c

    steps_gn = hidden // (2 * BLK)
    lax.fori_loop(0, steps_gn // 2, node_cols, 0)
    for t in range(pairs):
        landed(relay.at[t], relay_r.at[t])
        for way in range(2):
            rows = rows_of((up, down)[way], way)
            part[t, rows] = (
                part[t, rows].astype(F32) + relay[t, way].astype(F32)
            ).astype(BF16)
            fold_copy(t, way, way).start()
    lax.fori_loop(steps_gn // 2, steps_gn, node_cols, 0)
    gn_done = pltpu.make_async_copy(gn_ref, gn_out, out_sem.at[1])
    gn_done.start()
    for t in range(pairs):
        landed(fold.at[t], fold_r.at[t])
        for which in range(2):
            total = part[t, rows_of(me_y, which)].astype(F32)
            for way in range(2):
                total += fold[t, way, which].astype(F32)
            mid[which * half : (which + 1) * half, t * BLK : (t + 1) * BLK] = total.astype(BF16)
    for k in far_first:
        last_copy(k).start()
    landed(z_in, z_r)
    total = zpart[:, me_z].astype(F32)
    for k in range(1, nz):
        total += z_in[k - 1].astype(F32)
    z_mid[...] = total.astype(BF16)
    for k in range(1, ny):
        y_copy(k).start()

    landed(row_in.at[:, pl.ds(0, FEAT)], late_r)
    lax.fori_loop(0, ng, take_late, 0)
    mix_done = pltpu.make_async_copy(mix_ref, mix_out, out_sem.at[0])
    mix_done.start()
    landed(row_out.at[pl.ds(0, ns - 1), pl.ds(FEAT, FEAT)], row_s)
    landed(row_out.at[pl.ds(0, ns - 1), pl.ds(0, FEAT)], late_s)
    landed(col_out.at[pl.ds(0, ns - 1)], col_s)
    landed(dq.at[pl.ds(0, ng - 1)], tile_s)
    landed(relay, relay_s)
    landed(fold, fold_s)
    landed(last_in, last_r)
    total = mid[pl.ds(pl.multiple_of(me_z * FEAT, FEAT), FEAT)].astype(F32)
    for k in range(1, nz):
        total += last_in[k - 1].astype(F32)
    wg_ref[:, : pairs * BLK] = total
    landed(y_in, y_r)
    total = z_mid[me_y].astype(F32)
    for k in range(1, ny):
        total += y_in[k - 1].astype(F32)
    wg_ref[:, pairs * BLK :] = total
    wg_done = pltpu.make_async_copy(wg_ref, wg_out, out_sem.at[2])
    wg_done.start()
    landed(last_in, last_s)
    landed(z_in, z_s)
    landed(y_in, y_s)
    mix_done.wait()
    gn_done.wait()
    wg_done.wait()


def settle_kernel(mix_in, gn_in, wg_in, mix_out, gn_out, wg_out, mix_vm, gn_vm, wg_vm, sem):
    triples = ((mix_in, mix_vm, mix_out), (gn_in, gn_vm, gn_out), (wg_in, wg_vm, wg_out))
    loads = [pltpu.make_async_copy(a, b, sem.at[0, n]) for n, (a, b, _) in enumerate(triples)]
    stores = [pltpu.make_async_copy(b, c, sem.at[1, n]) for n, (_, b, c) in enumerate(triples)]
    for load in loads:
        load.start()
    for load, store in zip(loads, stores):
        load.wait()
        store.start()
    for store in stores:
        store.wait()


def per_device(nd, ns, nodes, w_qkv, incoming_adjoint, block_cols, block_counts):
    rows, hidden = nodes.shape[1:]
    ny, nz = 4, ns // 4
    ng = ns // 4
    tpd = 3 * ng // nd
    chunk = nz * FEAT
    any_spec = pl.BlockSpec(memory_space=pl.ANY)
    dma = pltpu.SemaphoreType.DMA
    slots_first = jnp.swapaxes(block_cols, 1, 2)
    out_shape = (
        jax.ShapeDtypeStruct((rows, hidden), BF16),
        jax.ShapeDtypeStruct((rows, hidden), BF16),
        jax.ShapeDtypeStruct((FEAT, tpd * BLK), F32),
    )
    out_buffers = [pltpu.VMEM(out.shape, out.dtype) for out in out_shape]
    results = pl.pallas_call(
        functools.partial(whole_kernel, nd, ns, ny, nz, tpd),
        out_shape=out_shape,
        in_specs=[any_spec] * 5,
        out_specs=(any_spec,) * 3,
        scratch_shapes=[
            pltpu.SMEM((1, SLOTS, ns), jnp.int32),
            pltpu.VMEM((SLOTS, ns), jnp.int32),
            pltpu.SMEM((1, ns), jnp.int32),
            *out_buffers,
            pltpu.VMEM((rows, hidden), BF16),
            pltpu.VMEM((rows, hidden), BF16),
            pltpu.VMEM((ng, hidden, 3 * BLK), BF16),
            pltpu.VMEM((ns, 2 * FEAT, BLK), BF16),
            pltpu.VMEM((ns, 2 * FEAT, BLK), BF16),
            pltpu.VMEM((ns, 2 * FEAT, BLK), BF16),
            pltpu.VMEM((ns, 2 * FEAT, BLK), BF16),
            pltpu.VMEM((ns, BLK, 2 * FEAT), BF16),
            pltpu.VMEM((hidden, BLK), BF16),
            pltpu.VMEM((hidden, nd * BLK), BF16),
            pltpu.VMEM((SLOTS * ns + 1, 2 * FEAT, BLK), F32),
            pltpu.VMEM((ns, 2 * FEAT, BLK), BF16),
            pltpu.VMEM((ns, 2 * FEAT, BLK), BF16),
            pltpu.VMEM((ns, 2 * FEAT, BLK), BF16),
            pltpu.VMEM((ns, 2 * FEAT, BLK), BF16),
            pltpu.VMEM((SLOTS, BLK, 2 * BLK), F32),
            pltpu.VMEM((SLOTS, BLK, 2 * BLK), F32),
            pltpu.VMEM((1, BLK), F32),
            pltpu.VMEM((1, BLK), F32),
            pltpu.VMEM((SLOTS * BLK, 2 * BLK), BF16),
            pltpu.VMEM((SLOTS * BLK, 2 * BLK), BF16),
            pltpu.VMEM((8, BLK), jnp.int32),
            pltpu.SMEM((8, BLK), jnp.int32),
            pltpu.VMEM((ng, 3 * BLK, BLK), BF16),
            pltpu.VMEM((tpd * BLK, nd * BLK), BF16),
            pltpu.VMEM((tpd - 1, hidden, BLK), BF16),
            pltpu.VMEM((tpd - 1, 2, chunk // 2, BLK), BF16),
            pltpu.VMEM((tpd - 1, 2, 2, chunk // 2, BLK), BF16),
            pltpu.VMEM((chunk, (tpd - 1) * BLK), BF16),
            pltpu.VMEM((nz - 1, FEAT, (tpd - 1) * BLK), BF16),
            dma((2, ng)),
            dma((5,)),
            dma,
            dma((ng,)),
            dma,
            dma((ng,)),
            dma,
            dma,
            dma,
            dma((ng,)),
            dma,
            dma((ng,)),
            dma((2,)),
            dma,
            dma((tpd,)),
            dma,
            dma((tpd,)),
            dma,
            dma((tpd,)),
            dma,
            dma,
            dma,
            dma,
            dma,
            dma,
            dma((3,)),
            pltpu.VMEM((ny, nz, FEAT, BLK), BF16),
            pltpu.VMEM((nz - 1, ny, FEAT, BLK), BF16),
            pltpu.VMEM((ny, FEAT, BLK), BF16),
            pltpu.VMEM((ny - 1, FEAT, BLK), BF16),
            dma,
            dma,
            dma,
            dma,
        ],
        compiler_params=pltpu.CompilerParams(
            collective_id=1, has_side_effects=True, vmem_limit_bytes=VMEM_LIMIT
        ),
        name="whole",
    )(nodes, w_qkv, incoming_adjoint, slots_first, block_counts)
    mixture, grad_nodes, weight_grad = pl.pallas_call(
        settle_kernel,
        out_shape=out_shape,
        in_specs=[any_spec] * 3,
        out_specs=(any_spec,) * 3,
        scratch_shapes=[*out_buffers, dma((2, 3))],
        compiler_params=pltpu.CompilerParams(vmem_limit_bytes=VMEM_LIMIT),
        name="settle",
    )(*results)
    return (mixture[None], grad_nodes[None], jnp.transpose(weight_grad))


def solution(mesh):
    nd, ns = mesh.shape["dp"], mesh.shape["seq"]
    in_specs = (P("dp", "seq", None), P(), P("dp", "seq", None), P("dp", None, None), P("dp", None))
    out_specs = (P("dp", "seq", None), P("dp", "seq", None), P("dp", "seq"))
    return jax.shard_map(
        functools.partial(per_device, nd, ns),
        mesh=mesh,
        in_specs=in_specs,
        out_specs=out_specs,
        check_vma=False,
    )
```

```python
import functools
import math

import jax
import jax.numpy as jnp
from jax import lax
from jax.experimental import pallas as pl
from jax.experimental.pallas import tpu as pltpu
from jax.sharding import PartitionSpec as P

MESH = pl.DeviceIdType.MESH
BLK = 128
FEAT = 32
SLOTS = 4
F32 = jnp.float32
BF16 = jnp.bfloat16
VMEM_LIMIT = 62 * 1024 * 1024


def lane_ids(shape):
    return lax.broadcasted_iota(jnp.int32, shape, len(shape) - 1)


def greet(me_d, me_s, nd, ns):
    barrier = pltpu.get_barrier_semaphore()

    def seq_hello(k, c):
        pl.semaphore_signal(
            barrier, inc=1, device_id=(me_d, lax.rem(me_s + k, ns)), device_id_type=MESH
        )
        return c

    def dp_hello(k, c):
        pl.semaphore_signal(
            barrier, inc=1, device_id=(lax.rem(me_d + k, nd), me_s), device_id_type=MESH
        )
        return c

    lax.fori_loop(1, ns, seq_hello, 0)
    lax.fori_loop(1, nd, dp_hello, 0)
    return barrier


def peer_at(me_s, i, j, ng, sign):
    group = lax.rem(me_s // 4 + sign * i + ng, ng)
    return 4 * group + lax.rem(me_s % 4 + sign * j + 4, 4)


def whole_kernel(
    nd, ns, ny, nz, tpd,
    x_in, w_in, cot_in, cols_in, counts_in,
    mix_out, gn_out, wg_out,
    cols_ref, cols_vec, counts_ref, mix_ref, gn_ref, wg_ref, x_vm, cot_vm, w_vm, kv_out, kv_in, qd_out, qd_in, natural, xt_own, xt_all,
    chain, row_out, col_out, row_in, col_in,
    raw_even, raw_odd, top_even, top_odd, pair_even, pair_odd,
    table_vm, table, dq, wg_in, part, relay, fold, mid, last_in,
    w_sem, load_sem, kv_s, kv_r, qd_s, qd_r, xt_s, xt_r, row_s, row_r, col_s, col_r,
    own_sem, tile_s, tile_r, relay_s, relay_r, fold_s, fold_r, last_s, last_r, late_s, late_r, share_s, share_r, out_sem,
    zpart, z_in, z_mid, y_in, z_s, z_r, y_s, y_r,
):
    me_d, me_s = lax.axis_index("dp"), lax.axis_index("seq")
    me_y, me_z = me_s // nz, me_s % nz
    ng = ns // 4
    my_group = me_s // 4
    hidden = ng * BLK
    nb = ns
    scale = 1.0 / math.sqrt(FEAT)
    to_exp2 = scale * math.log2(math.e)

    def lanes(t):
        return pl.ds(pl.multiple_of(t * BLK, BLK), BLK)

    def sent_group(i):
        return lax.rem(my_group + i, ng)

    def got_group(i):
        return lax.rem(my_group - i + ng, ng)

    def row_at(k):
        return peer_at(me_s, k // 4, k % 4, ng, -1)

    def remote(src, dst, send_sem, recv_sem, d, s):
        return pltpu.make_async_remote_copy(
            src_ref=src, dst_ref=dst, send_sem=send_sem, recv_sem=recv_sem,
            device_id=(d, s), device_id_type=MESH,
        )

    def landed(ref, sem):
        pltpu.make_async_copy(ref, ref, sem).wait()

    barrier = greet(me_d, me_s, nd, ns)
    load_x = pltpu.make_async_copy(x_in.at[0], x_vm, load_sem.at[0])
    load_cot = pltpu.make_async_copy(cot_in.at[0], cot_vm, load_sem.at[1])
    load_x.start()

    def w_start(part, i):
        g = sent_group(i)
        for m in ((1, 2), (0,))[part]:
            pltpu.make_async_copy(
                w_in.at[:, lanes(m * ng + g)],
                w_vm.at[g, :, pl.ds(m * BLK, BLK)],
                w_sem.at[part, i],
            ).start()

    def kv_weights(i, c):
        w_start(0, i)
        return c

    def q_weights(i, c):
        w_start(1, i)
        return c

    small_loads = [
        pltpu.make_async_copy(src, dst, load_sem.at[2 + n])
        for n, (src, dst) in enumerate(
            ((cols_in, cols_ref), (cols_in.at[0], cols_vec), (counts_in, counts_ref))
        )
    ]
    lax.fori_loop(0, ng, kv_weights, 0)
    load_cot.start()
    lax.fori_loop(0, ng, q_weights, 0)
    for load in small_loads:
        load.start()
    load_x.wait()

    def pieces_copy(out, into, send_sem, recv_sem):
        def copy(i, j):
            peer = peer_at(me_s, i, j, ng, 1)
            return remote(out.at[peer], into.at[me_s], send_sem, recv_sem.at[i], me_d, peer)

        return copy, pltpu.make_async_copy(out.at[me_s], into.at[me_s], recv_sem.at[0])

    kv_copy, own_kv = pieces_copy(kv_out, kv_in, kv_s, kv_r)
    qd_copy, own_qd = pieces_copy(qd_out, qd_in, qd_s, qd_r)

    def start_group(i, own, copy):
        @pl.when(i == 0)
        def _():
            own.start()

        @pl.when(i > 0)
        def _():
            copy(i, 0).start()

        for j in range(1, 4):
            copy(i, j).start()

    def project_kv(i, c):
        g = sent_group(i)
        landed(w_vm.at[g, :, pl.ds(BLK, 2 * BLK)], w_sem.at[0, i])
        flat = jnp.dot(x_vm[...], w_vm[g, :, BLK:], preferred_element_type=F32)
        for m in range(2):
            turned = jnp.transpose(flat[:, m * BLK : (m + 1) * BLK]).astype(BF16)
            for j in range(4):
                kv_out[4 * g + j, m * FEAT : (m + 1) * FEAT] = turned[
                    j * FEAT : (j + 1) * FEAT
                ]

        @pl.when(i == 0)
        def _():
            pl.semaphore_wait(barrier, ns + nd - 2)

        start_group(i, own_kv, kv_copy)
        return c

    def project_q(i, c):
        g = sent_group(i)
        landed(w_vm.at[g, :, pl.ds(0, BLK)], w_sem.at[1, i])
        flat = jnp.dot(x_vm[...], w_vm[g, :, :BLK], preferred_element_type=F32)
        for m, piece in enumerate((flat, cot_vm[:, lanes(g)].astype(F32))):
            turned = jnp.transpose(piece).astype(BF16)
            for j in range(4):
                qd_out[4 * g + j, m * FEAT : (m + 1) * FEAT] = turned[
                    j * FEAT : (j + 1) * FEAT
                ]
        start_group(i, own_qd, qd_copy)
        return c

    lax.fori_loop(0, ng, project_kv, 0)
    load_cot.wait()
    lax.fori_loop(0, ng, project_q, 0)

    xt_own[...] = jnp.transpose(x_vm[...].astype(F32)).astype(BF16)
    xt_keep = pltpu.make_async_copy(xt_own, xt_all.at[:, lanes(me_d)], own_sem.at[0])
    xt_keep.start()

    sibling = me_d + 1 - 2 * (me_d % 2)

    def xt_copy(k):
        return remote(
            xt_own, xt_all.at[:, lanes(me_d)], xt_s, xt_r,
            lax.rem(me_d + 2 * k, nd), me_s,
        )

    def share_copy(k):
        here = lanes(lax.rem(me_d - 2 * k + nd, nd))
        return remote(
            xt_all.at[:, here] if k else xt_own, xt_all.at[:, here],
            share_s, share_r, sibling, me_s,
        )

    for k in range(1, nd // 2):
        xt_copy(k).start()
    share_copy(0).start()

    for load in small_loads:
        load.wait()
    named_now = cols_vec[...]
    row_ids = lane_ids((SLOTS, nb))
    place = 4 * lax.rem(my_group - row_ids // 4 + ng, ng) + lax.rem(
        me_s % 4 - row_ids % 4 + 4, 4
    )
    col_ids = lane_ids((1, nb))

    def link(k, carry):
        before, final = carry
        r = row_at(k)
        for s in range(SLOTS):
            name = cols_ref[0, s, r]
            before = jnp.where((named_now == name) & (place > k), 4 * k + s, before)
            final = jnp.where(col_ids == name, 4 * k + s, final)
        return before, final

    before, final = lax.fori_loop(
        0, nb, link,
        (jnp.full((SLOTS, nb), SLOTS * nb, jnp.int32), jnp.zeros((1, nb), jnp.int32)),
    )
    table_vm[...] = jnp.zeros_like(table_vm)
    table_vm[:SLOTS, :nb] = before
    table_vm[SLOTS : SLOTS + 1, :nb] = final
    table_copy = pltpu.make_async_copy(table_vm, table, own_sem.at[1])
    table_copy.start()
    chain[SLOTS * nb] = jnp.zeros((2 * FEAT, BLK), F32)

    raw, top, pair = (raw_even, raw_odd), (top_even, top_odd), (pair_even, pair_odd)

    def arrive(i, c):
        landed(kv_in.at[pl.ds(0, 4)], kv_r.at[i])
        for j in range(4):
            b = row_at(4 * i + j)
            natural[b] = jnp.transpose(kv_in[b].astype(F32)).astype(BF16)
        return c

    lax.fori_loop(0, ng, arrive, 0)
    table_copy.wait()

    def spread_pieces(r, side):
        queries, cot = qd_in[r, :FEAT], qd_in[r, FEAT:]
        empty = jnp.zeros((FEAT, BLK), BF16)
        upper, lower = [queries, empty], [empty, cot]
        if side:
            upper, lower = upper[::-1], lower[::-1]
        return jnp.concatenate(
            [jnp.concatenate(upper, axis=1), jnp.concatenate(lower, axis=1)], axis=0
        )

    def score_stage(k, p):
        r = row_at(k)
        count = counts_ref[0, r]
        keys = jnp.concatenate([natural[cols_ref[0, s, r]] for s in range(SLOTS)], axis=0)
        both = jnp.dot(keys, spread_pieces(r, 0), preferred_element_type=F32)
        best = None
        for s in range(SLOTS):
            block = both[s * BLK : (s + 1) * BLK]
            scores = block[:, :BLK]
            if s:
                scores = jnp.where(s < count, scores, -jnp.inf)
            raw[p][s, :, :BLK] = scores
            raw[p][s, :, BLK:] = block[:, BLK:]
            peak = jnp.max(scores, axis=0, keepdims=True)
            best = peak if best is None else jnp.maximum(best, peak)
        top[p][...] = best * to_exp2

    def soft_stage(p):
        peak = top[p][...]
        total = mixed = None
        for s in range(SLOTS):
            weights = jnp.exp2(raw[p][s, :, :BLK] * to_exp2 - peak)
            t = jnp.sum(weights, axis=0, keepdims=True)
            m = jnp.sum(weights * raw[p][s, :, BLK:], axis=0, keepdims=True)
            total = t if total is None else total + t
            mixed = m if mixed is None else mixed + m
            raw[p][s, :, :BLK] = weights
        inverse = 1.0 / total
        delta = mixed * inverse
        for s in range(SLOTS):
            prob = raw[p][s, :, :BLK] * inverse
            rows = slice(s * BLK, (s + 1) * BLK)
            pair[p][rows, :BLK] = prob.astype(BF16)
            pair[p][rows, BLK:] = (prob * (raw[p][s, :, BLK:] - delta)).astype(BF16)

    def grad_stage(k, p):
        r = row_at(k)
        named = [cols_ref[0, s, r] for s in range(SLOTS)]
        both = pair[p][...]
        turned = jnp.concatenate([kv_in[n] for n in named], axis=1)
        row_side = jnp.dot(turned, both, preferred_element_type=F32)
        row_out[r, :FEAT] = row_side[FEAT:, :BLK].astype(BF16)
        row_out[r, FEAT:] = (row_side[:FEAT, BLK:] * scale).astype(BF16)
        key_side = lax.dot_general(
            spread_pieces(r, 1), both, (((1,), (1,)), ((), ())), preferred_element_type=F32
        )
        for s in range(SLOTS):
            chain[4 * k + s] = key_side[:, s * BLK : (s + 1) * BLK] + chain[table[s, r]]

    def piece_copy(lo, send_sem, recv_sem):
        def copy(i, j):
            peer = row_at(4 * i + j)
            piece = pl.ds(lo, FEAT)
            return remote(
                row_out.at[peer, piece], row_in.at[me_s, piece],
                send_sem, recv_sem(i), me_d, peer,
            )

        return copy

    late_copy = piece_copy(0, late_s, lambda i: late_r)
    row_copy = piece_copy(FEAT, row_s, lambda i: row_r.at[i])

    def col_copy(i, j):
        peer = peer_at(me_s, i, j, ng, 1)
        return remote(
            col_out.at[peer], col_in.at[me_s], col_s, col_r.at[i], me_d, peer
        )

    def own_piece(lo, sem):
        piece = pl.ds(lo, FEAT)
        return pltpu.make_async_copy(row_out.at[me_s, piece], row_in.at[me_s, piece], sem)

    own_late = own_piece(0, late_r)
    own_row = own_piece(FEAT, row_r.at[0])
    own_col = pltpu.make_async_copy(col_out.at[me_s], col_in.at[me_s], col_r.at[0])
    def one_step(k, p, grad=True):
        score_stage(k + 1, 1 - p)
        soft_stage(p)
        if grad:
            grad_stage(k - 1, 1 - p)

    landed(qd_in.at[pl.ds(0, 4)], qd_r.at[0])
    score_stage(0, 0)
    one_step(0, 0, grad=False)
    one_step(1, 1)
    one_step(2, 0)

    def four_rows(i, c):
        @pl.when(i > 0)
        def _():
            start_group(i - 1, own_row, row_copy)

        landed(qd_in.at[pl.ds(0, 4)], qd_r.at[i + 1])
        for u in range(4):
            one_step(3 + 4 * i + u, (1 + u) % 2)
        return c

    lax.fori_loop(0, ng - 1, four_rows, 0)
    start_group(ng - 2, own_row, row_copy)
    soft_stage(1)
    grad_stage(nb - 2, 0)
    grad_stage(nb - 1, 1)
    start_group(ng - 1, own_row, row_copy)
    own_late.start()

    def col_send(i, c):
        for j in range(4):
            peer = peer_at(me_s, i, j, ng, 1)
            total = chain[table[SLOTS, peer]]
            col_out[peer, :FEAT] = (total[:FEAT] * scale).astype(BF16)
            col_out[peer, FEAT:] = total[FEAT:].astype(BF16)
        start_group(i, own_col, col_copy)
        return c

    lax.fori_loop(0, ng, col_send, 0)
    others = nd // 2 - 1
    if others:
        landed(xt_all.at[:, pl.ds(0, others * BLK)], xt_r)
    for k in range(1, nd // 2):
        share_copy(k).start()

    def late_send(i, c):
        @pl.when(i > 0)
        def _():
            late_copy(i, 0).start()

        for j in range(1, 4):
            late_copy(i, j).start()
        return c


    def tile_own(g, m):
        t = m * ng + g
        return pltpu.make_async_copy(
            dq.at[g, pl.ds(m * BLK, BLK)], wg_in.at[lanes(t % tpd), lanes(me_d)],
            tile_r.at[t % tpd],
        )

    def tile_copy(g, m):
        t = m * ng + g
        return remote(
            dq.at[g, pl.ds(m * BLK, BLK)], wg_in.at[lanes(t % tpd), lanes(me_d)],
            tile_s, tile_r.at[t % tpd], t // tpd, me_s,
        )

    def tile_send(g, m):
        t = m * ng + g

        @pl.when(t // tpd == me_d)
        def _():
            tile_own(g, m).start()

        @pl.when(t // tpd != me_d)
        def _():
            tile_copy(g, m).start()

    def take_rows(i, c):
        g = sent_group(i)
        landed(row_in.at[pl.ds(0, 4), pl.ds(FEAT, FEAT)], row_r.at[i])
        for j in range(4):
            dq[g, j * FEAT : (j + 1) * FEAT] = row_in[4 * g + j, FEAT:]
        tile_send(g, 0)
        return c

    def take_late(g, c):
        mix = jnp.concatenate([row_in[4 * g + j, :FEAT] for j in range(4)], axis=0)
        mix_ref[:, lanes(g)] = jnp.transpose(mix.astype(F32)).astype(BF16)
        return c

    def take_cols(i, c):
        g = got_group(i)
        landed(col_in.at[pl.ds(0, 4)], col_r.at[i])
        for j in range(4):
            dq[g, BLK + j * FEAT : BLK + (j + 1) * FEAT] = col_in[4 * g + j, :FEAT]
            dq[g, 2 * BLK + j * FEAT : 2 * BLK + (j + 1) * FEAT] = col_in[4 * g + j, FEAT:]
        tile_send(g, 1)
        tile_send(g, 2)
        return c

    def bring_home(i, c):
        late_send(i, 0)
        take_rows(i, 0)
        return take_cols(i, c)

    lax.fori_loop(0, ng, bring_home, 0)
    xt_keep.wait()
    landed(xt_all.at[:, pl.ds(0, nd // 2 * BLK)], share_r)

    chunk = nz * FEAT
    half = chunk // 2
    up, down = lax.rem(me_y + 1, ny), lax.rem(me_y + ny - 1, ny)
    across = lax.rem(me_y + 2, ny)

    def rows_of(y, which):
        return pl.ds(pl.multiple_of(y * chunk + which * half, half), half)

    def relay_copy(t, way):
        return remote(
            part.at[t, rows_of(across, way)], relay.at[t, way],
            relay_s, relay_r.at[t], me_d, (up, down)[way] * nz + me_z,
        )

    def fold_copy(t, way, which):
        return remote(
            part.at[t, rows_of((up, down)[way], which)], fold.at[t, way, which],
            fold_s, fold_r.at[t],
            me_d, (up, down)[way] * nz + me_z,
        )

    def last_copy(k):
        to = lax.rem(me_z + k, nz)
        return remote(
            mid.at[pl.ds(pl.multiple_of(to * FEAT, FEAT), FEAT)], last_in.at[k - 1],
            last_s, last_r, me_d, me_y * nz + to,
        )

    def z_copy(k):
        to = lax.rem(me_z + k, nz)
        return remote(zpart.at[:, to], z_in.at[k - 1], z_s, z_r, me_d, me_y * nz + to)

    def y_copy(k):
        to = lax.rem(me_y + k, ny)
        return remote(z_mid.at[to], y_in.at[k - 1], y_s, y_r, me_d, to * nz + me_z)

    far_first = sorted(range(1, nz), key=lambda k: -min(k, nz - k))
    pairs = tpd - 1
    for t in range(tpd):
        landed(wg_in.at[pl.ds(t * BLK, BLK)], tile_r.at[t])

    def contract(rows, first, last):
        return lax.dot_general(
            xt_all[rows, :], wg_in[first * BLK : last * BLK], (((1,), (1,)), ((), ())),
            preferred_element_type=F32,
        ).astype(BF16)

    def fill(y):
        rows = pl.ds(pl.multiple_of(y * chunk, chunk), chunk)
        value = contract(rows, 0, pairs)
        for t in range(pairs):
            part[t, rows] = value[:, t * BLK : (t + 1) * BLK]

    fill(across)
    for t in range(pairs):
        for way in range(2):
            relay_copy(t, way).start()
    zpart[...] = contract(slice(None), pairs, tpd).reshape(ny, nz, FEAT, BLK)
    for k in far_first:
        z_copy(k).start()
    fill(up)
    fill(down)
    for t in range(pairs):
        for way in range(2):
            fold_copy(t, way, 1 - way).start()
    fill(me_y)

    def node_cols(n, c):
        width = 2 * BLK
        cols = pl.ds(pl.multiple_of(n * width, width), width)
        total = jnp.zeros((width, BLK), F32)
        for g in range(ng):
            total += jnp.dot(w_vm[g, cols], dq[g], preferred_element_type=F32)
        gn_ref[:, cols] = jnp.transpose(total).astype(BF16)
        return c

    steps_gn = hidden // (2 * BLK)
    lax.fori_loop(0, steps_gn // 4, node_cols, 0)
    for t in range(pairs):
        landed(relay.at[t], relay_r.at[t])
        for way in range(2):
            rows = rows_of((up, down)[way], way)
            part[t, rows] = (
                part[t, rows].astype(F32) + relay[t, way].astype(F32)
            ).astype(BF16)
            fold_copy(t, way, way).start()
    lax.fori_loop(steps_gn // 4, steps_gn // 2, node_cols, 0)
    for t in range(pairs):
        landed(fold.at[t], fold_r.at[t])
        for which in range(2):
            total = part[t, rows_of(me_y, which)].astype(F32)
            for way in range(2):
                total += fold[t, way, which].astype(F32)
            mid[which * half : (which + 1) * half, t * BLK : (t + 1) * BLK] = total.astype(BF16)
    for k in far_first:
        last_copy(k).start()
    lax.fori_loop(steps_gn // 2, steps_gn, node_cols, 0)
    gn_done = pltpu.make_async_copy(gn_ref, gn_out, out_sem.at[1])
    gn_done.start()
    landed(z_in, z_r)
    total = zpart[:, me_z].astype(F32)
    for k in range(1, nz):
        total += z_in[k - 1].astype(F32)
    z_mid[...] = total.astype(BF16)
    for k in range(1, ny):
        y_copy(k).start()

    landed(row_in.at[:, pl.ds(0, FEAT)], late_r)
    lax.fori_loop(0, ng, take_late, 0)
    mix_done = pltpu.make_async_copy(mix_ref, mix_out, out_sem.at[0])
    mix_done.start()
    landed(kv_out.at[pl.ds(0, ns - 1)], kv_s)
    landed(qd_out.at[pl.ds(0, ns - 1)], qd_s)
    if others:
        landed(xt_all.at[:, pl.ds(0, others * BLK)], xt_s)
    landed(xt_all.at[:, pl.ds(0, nd // 2 * BLK)], share_s)
    landed(row_out.at[pl.ds(0, ns - 1), pl.ds(FEAT, FEAT)], row_s)
    landed(row_out.at[pl.ds(0, ns - 1), pl.ds(0, FEAT)], late_s)
    landed(col_out.at[pl.ds(0, ns - 1)], col_s)
    landed(dq.at[pl.ds(0, ng - 1)], tile_s)
    landed(relay, relay_s)
    landed(fold, fold_s)
    landed(last_in, last_r)
    total = mid[pl.ds(pl.multiple_of(me_z * FEAT, FEAT), FEAT)].astype(F32)
    for k in range(1, nz):
        total += last_in[k - 1].astype(F32)
    wg_ref[:, : pairs * BLK] = total
    landed(y_in, y_r)
    total = z_mid[me_y].astype(F32)
    for k in range(1, ny):
        total += y_in[k - 1].astype(F32)
    wg_ref[:, pairs * BLK :] = total
    wg_done = pltpu.make_async_copy(wg_ref, wg_out, out_sem.at[2])
    wg_done.start()
    landed(last_in, last_s)
    landed(z_in, z_s)
    landed(y_in, y_s)
    mix_done.wait()
    gn_done.wait()
    wg_done.wait()


def settle_kernel(mix_in, gn_in, wg_in, mix_out, gn_out, wg_out, mix_vm, gn_vm, wg_vm, sem):
    triples = ((mix_in, mix_vm, mix_out), (gn_in, gn_vm, gn_out), (wg_in, wg_vm, wg_out))
    loads = [pltpu.make_async_copy(a, b, sem.at[0, n]) for n, (a, b, _) in enumerate(triples)]
    stores = [pltpu.make_async_copy(b, c, sem.at[1, n]) for n, (_, b, c) in enumerate(triples)]
    for load in loads:
        load.start()
    for load, store in zip(loads, stores):
        load.wait()
        store.start()
    for store in stores:
        store.wait()


def per_device(nd, ns, nodes, w_qkv, incoming_adjoint, block_cols, block_counts):
    rows, hidden = nodes.shape[1:]
    ny, nz = 4, ns // 4
    ng = ns // 4
    tpd = 3 * ng // nd
    chunk = nz * FEAT
    any_spec = pl.BlockSpec(memory_space=pl.ANY)
    dma = pltpu.SemaphoreType.DMA
    slots_first = jnp.swapaxes(block_cols, 1, 2)
    out_shape = (
        jax.ShapeDtypeStruct((rows, hidden), BF16),
        jax.ShapeDtypeStruct((rows, hidden), BF16),
        jax.ShapeDtypeStruct((FEAT, tpd * BLK), F32),
    )
    out_buffers = [pltpu.VMEM(out.shape, out.dtype) for out in out_shape]
    results = pl.pallas_call(
        functools.partial(whole_kernel, nd, ns, ny, nz, tpd),
        out_shape=out_shape,
        in_specs=[any_spec] * 5,
        out_specs=(any_spec,) * 3,
        scratch_shapes=[
            pltpu.SMEM((1, SLOTS, ns), jnp.int32),
            pltpu.VMEM((SLOTS, ns), jnp.int32),
            pltpu.SMEM((1, ns), jnp.int32),
            *out_buffers,
            pltpu.VMEM((rows, hidden), BF16),
            pltpu.VMEM((rows, hidden), BF16),
            pltpu.VMEM((ng, hidden, 3 * BLK), BF16),
            pltpu.VMEM((ns, 2 * FEAT, BLK), BF16),
            pltpu.VMEM((ns, 2 * FEAT, BLK), BF16),
            pltpu.VMEM((ns, 2 * FEAT, BLK), BF16),
            pltpu.VMEM((ns, 2 * FEAT, BLK), BF16),
            pltpu.VMEM((ns, BLK, 2 * FEAT), BF16),
            pltpu.VMEM((hidden, BLK), BF16),
            pltpu.VMEM((hidden, nd * BLK), BF16),
            pltpu.VMEM((SLOTS * ns + 1, 2 * FEAT, BLK), F32),
            pltpu.VMEM((ns, 2 * FEAT, BLK), BF16),
            pltpu.VMEM((ns, 2 * FEAT, BLK), BF16),
            pltpu.VMEM((ns, 2 * FEAT, BLK), BF16),
            pltpu.VMEM((ns, 2 * FEAT, BLK), BF16),
            pltpu.VMEM((SLOTS, BLK, 2 * BLK), F32),
            pltpu.VMEM((SLOTS, BLK, 2 * BLK), F32),
            pltpu.VMEM((1, BLK), F32),
            pltpu.VMEM((1, BLK), F32),
            pltpu.VMEM((SLOTS * BLK, 2 * BLK), BF16),
            pltpu.VMEM((SLOTS * BLK, 2 * BLK), BF16),
            pltpu.VMEM((8, BLK), jnp.int32),
            pltpu.SMEM((8, BLK), jnp.int32),
            pltpu.VMEM((ng, 3 * BLK, BLK), BF16),
            pltpu.VMEM((tpd * BLK, nd * BLK), BF16),
            pltpu.VMEM((tpd - 1, hidden, BLK), BF16),
            pltpu.VMEM((tpd - 1, 2, chunk // 2, BLK), BF16),
            pltpu.VMEM((tpd - 1, 2, 2, chunk // 2, BLK), BF16),
            pltpu.VMEM((chunk, (tpd - 1) * BLK), BF16),
            pltpu.VMEM((nz - 1, FEAT, (tpd - 1) * BLK), BF16),
            dma((2, ng)),
            dma((5,)),
            dma,
            dma((ng,)),
            dma,
            dma((ng,)),
            dma,
            dma,
            dma,
            dma((ng,)),
            dma,
            dma((ng,)),
            dma((2,)),
            dma,
            dma((tpd,)),
            dma,
            dma((tpd,)),
            dma,
            dma((tpd,)),
            dma,
            dma,
            dma,
            dma,
            dma,
            dma,
            dma((3,)),
            pltpu.VMEM((ny, nz, FEAT, BLK), BF16),
            pltpu.VMEM((nz - 1, ny, FEAT, BLK), BF16),
            pltpu.VMEM((ny, FEAT, BLK), BF16),
            pltpu.VMEM((ny - 1, FEAT, BLK), BF16),
            dma,
            dma,
            dma,
            dma,
        ],
        compiler_params=pltpu.CompilerParams(
            collective_id=1, has_side_effects=True, vmem_limit_bytes=VMEM_LIMIT
        ),
        name="whole",
    )(nodes, w_qkv, incoming_adjoint, slots_first, block_counts)
    mixture, grad_nodes, weight_grad = pl.pallas_call(
        settle_kernel,
        out_shape=out_shape,
        in_specs=[any_spec] * 3,
        out_specs=(any_spec,) * 3,
        scratch_shapes=[*out_buffers, dma((2, 3))],
        compiler_params=pltpu.CompilerParams(vmem_limit_bytes=VMEM_LIMIT),
        name="settle",
    )(*results)
    return (mixture[None], grad_nodes[None], jnp.transpose(weight_grad))


def solution(mesh):
    nd, ns = mesh.shape["dp"], mesh.shape["seq"]
    in_specs = (P("dp", "seq", None), P(), P("dp", "seq", None), P("dp", None, None), P("dp", None))
    out_specs = (P("dp", "seq", None), P("dp", "seq", None), P("dp", "seq"))
    return jax.shard_map(
        functools.partial(per_device, nd, ns),
        mesh=mesh,
        in_specs=in_specs,
        out_specs=out_specs,
        check_vma=False,
    )
```

```python
import functools
import math

import jax
import jax.numpy as jnp
from jax import lax
from jax.experimental import pallas as pl
from jax.experimental.pallas import tpu as pltpu
from jax.sharding import PartitionSpec as P

MESH = pl.DeviceIdType.MESH
BLK = 128
FEAT = 32
SLOTS = 4
F32 = jnp.float32
BF16 = jnp.bfloat16
VMEM_LIMIT = 62 * 1024 * 1024


def lane_ids(shape):
    return lax.broadcasted_iota(jnp.int32, shape, len(shape) - 1)


def greet(me_d, me_s, nd, ns):
    barrier = pltpu.get_barrier_semaphore()

    def seq_hello(k, c):
        far = 1 + lax.rem(k + ns // 2, ns - 1)
        pl.semaphore_signal(
            barrier, inc=1, device_id=(me_d, lax.rem(me_s + far, ns)), device_id_type=MESH
        )
        return c

    def dp_hello(k, c):
        pl.semaphore_signal(
            barrier, inc=1, device_id=(lax.rem(me_d + k, nd), me_s), device_id_type=MESH
        )
        return c

    lax.fori_loop(1, ns, seq_hello, 0)
    lax.fori_loop(1, nd, dp_hello, 0)
    return barrier


def peer_at(me_s, i, j, ng, sign):
    group = lax.rem(me_s // 4 + sign * i + ng, ng)
    return 4 * group + lax.rem(me_s % 4 + sign * j + 4, 4)


def whole_kernel(
    nd, ns, ny, nz, tpd,
    x_in, w_in, cot_in, cols_in, counts_in,
    mix_out, gn_out, wg_out,
    cols_ref, cols_vec, counts_ref, mix_ref, gn_ref, wg_ref, x_vm, cot_vm, w_vm, kv_out, kv_in, qd_out, qd_in, natural, xt_own, xt_all,
    chain, row_out, col_out, row_in, col_in,
    raw_even, raw_odd, top_even, top_odd, pair_even, pair_odd,
    table_vm, table, dq, wg_in, part, relay, fold, mid, last_in,
    w_sem, load_sem, kv_s, kv_r, qd_s, qd_r, xt_s, xt_r, row_s, row_r, col_s, col_r,
    own_sem, tile_s, tile_r, relay_s, relay_r, fold_s, fold_r, last_s, last_r, late_s, late_r, share_s, share_r, out_sem,
    zpart, z_in, z_mid, y_in, z_s, z_r, y_s, y_r,
):
    me_d, me_s = lax.axis_index("dp"), lax.axis_index("seq")
    me_y, me_z = me_s // nz, me_s % nz
    ng = ns // 4
    my_group = me_s // 4
    hidden = ng * BLK
    nb = ns
    scale = 1.0 / math.sqrt(FEAT)
    to_exp2 = scale * math.log2(math.e)

    def lanes(t):
        return pl.ds(pl.multiple_of(t * BLK, BLK), BLK)

    def sent_group(i):
        return lax.rem(my_group + i, ng)

    def got_group(i):
        return lax.rem(my_group - i + ng, ng)

    def row_at(k):
        return peer_at(me_s, k // 4, k % 4, ng, -1)

    def remote(src, dst, send_sem, recv_sem, d, s):
        return pltpu.make_async_remote_copy(
            src_ref=src, dst_ref=dst, send_sem=send_sem, recv_sem=recv_sem,
            device_id=(d, s), device_id_type=MESH,
        )

    def landed(ref, sem):
        pltpu.make_async_copy(ref, ref, sem).wait()

    load_x = pltpu.make_async_copy(x_in.at[0], x_vm, load_sem.at[0])
    load_cot = pltpu.make_async_copy(cot_in.at[0], cot_vm, load_sem.at[1])
    load_x.start()

    def w_start(part, i):
        g = sent_group(i)
        for m in ((1, 2), (0,))[part]:
            pltpu.make_async_copy(
                w_in.at[:, lanes(m * ng + g)],
                w_vm.at[g, :, pl.ds(m * BLK, BLK)],
                w_sem.at[part, i],
            ).start()

    ahead = 2
    for i in range(ahead):
        w_start(0, i)
    barrier = greet(me_d, me_s, nd, ns)
    load_cot.start()
    small_loads = [
        pltpu.make_async_copy(src, dst, load_sem.at[2 + n])
        for n, (src, dst) in enumerate(
            ((cols_in, cols_ref), (cols_in.at[0], cols_vec), (counts_in, counts_ref))
        )
    ]
    load_x.wait()

    def pieces_copy(out, into, send_sem, recv_sem):
        def copy(i, j):
            peer = peer_at(me_s, i, j, ng, 1)
            return remote(out.at[peer], into.at[me_s], send_sem, recv_sem.at[i], me_d, peer)

        return copy, pltpu.make_async_copy(out.at[me_s], into.at[me_s], recv_sem.at[0])

    kv_copy, own_kv = pieces_copy(kv_out, kv_in, kv_s, kv_r)
    qd_copy, own_qd = pieces_copy(qd_out, qd_in, qd_s, qd_r)

    def start_group(i, own, copy):
        @pl.when(i == 0)
        def _():
            own.start()

        @pl.when(i > 0)
        def _():
            copy(i, 0).start()

        for j in range(1, 4):
            copy(i, j).start()

    def project_kv(i, c):
        g = sent_group(i)
        landed(w_vm.at[g, :, pl.ds(BLK, 2 * BLK)], w_sem.at[0, i])
        flat = jnp.dot(x_vm[...], w_vm[g, :, BLK:], preferred_element_type=F32)
        for m in range(2):
            turned = jnp.transpose(flat[:, m * BLK : (m + 1) * BLK]).astype(BF16)
            for j in range(4):
                kv_out[4 * g + j, m * FEAT : (m + 1) * FEAT] = turned[
                    j * FEAT : (j + 1) * FEAT
                ]

        @pl.when(i == 0)
        def _():
            pl.semaphore_wait(barrier, ns + nd - 2)

        start_group(i, own_kv, kv_copy)

        @pl.when(i + ahead < ng)
        def _():
            w_start(0, i + ahead)

        w_start(1, i)
        return c

    def project_q(i, c):
        g = sent_group(i)
        landed(w_vm.at[g, :, pl.ds(0, BLK)], w_sem.at[1, i])
        flat = jnp.dot(x_vm[...], w_vm[g, :, :BLK], preferred_element_type=F32)
        for m, piece in enumerate((flat, cot_vm[:, lanes(g)].astype(F32))):
            turned = jnp.transpose(piece).astype(BF16)
            for j in range(4):
                qd_out[4 * g + j, m * FEAT : (m + 1) * FEAT] = turned[
                    j * FEAT : (j + 1) * FEAT
                ]
        start_group(i, own_qd, qd_copy)
        return c

    lax.fori_loop(0, ng, project_kv, 0)
    for load in small_loads:
        load.start()
    load_cot.wait()
    lax.fori_loop(0, ng, project_q, 0)

    xt_own[...] = jnp.transpose(x_vm[...].astype(F32)).astype(BF16)
    xt_keep = pltpu.make_async_copy(xt_own, xt_all.at[:, lanes(me_d)], own_sem.at[0])
    xt_keep.start()

    sibling = me_d + 1 - 2 * (me_d % 2)

    def xt_copy(k):
        return remote(
            xt_own, xt_all.at[:, lanes(me_d)], xt_s, xt_r,
            lax.rem(me_d + 2 * k, nd), me_s,
        )

    def share_copy(k):
        here = lanes(lax.rem(me_d - 2 * k + nd, nd))
        return remote(
            xt_all.at[:, here] if k else xt_own, xt_all.at[:, here],
            share_s, share_r, sibling, me_s,
        )

    for k in range(1, nd // 2):
        xt_copy(k).start()
    share_copy(0).start()

    for load in small_loads:
        load.wait()
    named_now = cols_vec[...]
    row_ids = lane_ids((SLOTS, nb))
    place = 4 * lax.rem(my_group - row_ids // 4 + ng, ng) + lax.rem(
        me_s % 4 - row_ids % 4 + 4, 4
    )
    col_ids = lane_ids((1, nb))

    def link(k, carry):
        before, final = carry
        r = row_at(k)
        for s in range(SLOTS):
            name = cols_ref[0, s, r]
            before = jnp.where((named_now == name) & (place > k), 4 * k + s, before)
            final = jnp.where(col_ids == name, 4 * k + s, final)
        return before, final

    before, final = lax.fori_loop(
        0, nb, link,
        (jnp.full((SLOTS, nb), SLOTS * nb, jnp.int32), jnp.zeros((1, nb), jnp.int32)),
    )
    table_vm[...] = jnp.zeros_like(table_vm)
    table_vm[:SLOTS, :nb] = before
    table_vm[SLOTS : SLOTS + 1, :nb] = final
    table_copy = pltpu.make_async_copy(table_vm, table, own_sem.at[1])
    table_copy.start()
    chain[SLOTS * nb] = jnp.zeros((2 * FEAT, BLK), F32)

    raw, top, pair = (raw_even, raw_odd), (top_even, top_odd), (pair_even, pair_odd)

    def arrive(i, c):
        landed(kv_in.at[pl.ds(0, 4)], kv_r.at[i])
        for j in range(4):
            b = row_at(4 * i + j)
            natural[b] = jnp.transpose(kv_in[b].astype(F32)).astype(BF16)
        return c

    lax.fori_loop(0, ng, arrive, 0)
    table_copy.wait()

    def spread_pieces(r, side):
        queries, cot = qd_in[r, :FEAT], qd_in[r, FEAT:]
        empty = jnp.zeros((FEAT, BLK), BF16)
        upper, lower = [queries, empty], [empty, cot]
        if side:
            upper, lower = upper[::-1], lower[::-1]
        return jnp.concatenate(
            [jnp.concatenate(upper, axis=1), jnp.concatenate(lower, axis=1)], axis=0
        )

    def score_stage(k, p):
        r = row_at(k)
        count = counts_ref[0, r]
        keys = jnp.concatenate([natural[cols_ref[0, s, r]] for s in range(SLOTS)], axis=0)
        both = jnp.dot(keys, spread_pieces(r, 0), preferred_element_type=F32)
        best = None
        for s in range(SLOTS):
            block = both[s * BLK : (s + 1) * BLK]
            scores = block[:, :BLK]
            if s:
                scores = jnp.where(s < count, scores, -jnp.inf)
            raw[p][s, :, :BLK] = scores
            raw[p][s, :, BLK:] = block[:, BLK:]
            peak = jnp.max(scores, axis=0, keepdims=True)
            best = peak if best is None else jnp.maximum(best, peak)
        top[p][...] = best * to_exp2

    def soft_stage(p):
        peak = top[p][...]
        total = mixed = None
        for s in range(SLOTS):
            weights = jnp.exp2(raw[p][s, :, :BLK] * to_exp2 - peak)
            t = jnp.sum(weights, axis=0, keepdims=True)
            m = jnp.sum(weights * raw[p][s, :, BLK:], axis=0, keepdims=True)
            total = t if total is None else total + t
            mixed = m if mixed is None else mixed + m
            raw[p][s, :, :BLK] = weights
        inverse = 1.0 / total
        delta = mixed * inverse
        for s in range(SLOTS):
            prob = raw[p][s, :, :BLK] * inverse
            rows = slice(s * BLK, (s + 1) * BLK)
            pair[p][rows, :BLK] = prob.astype(BF16)
            pair[p][rows, BLK:] = (prob * (raw[p][s, :, BLK:] - delta)).astype(BF16)

    def grad_stage(k, p):
        r = row_at(k)
        named = [cols_ref[0, s, r] for s in range(SLOTS)]
        both = pair[p][...]
        turned = jnp.concatenate([kv_in[n] for n in named], axis=1)
        row_side = jnp.dot(turned, both, preferred_element_type=F32)
        row_out[r, :FEAT] = row_side[FEAT:, :BLK].astype(BF16)
        row_out[r, FEAT:] = (row_side[:FEAT, BLK:] * scale).astype(BF16)
        key_side = lax.dot_general(
            spread_pieces(r, 1), both, (((1,), (1,)), ((), ())), preferred_element_type=F32
        )
        for s in range(SLOTS):
            chain[4 * k + s] = key_side[:, s * BLK : (s + 1) * BLK] + chain[table[s, r]]

    def piece_copy(lo, send_sem, recv_sem):
        def copy(i, j):
            peer = peer_at(me_s, i, j, ng, -1)
            piece = pl.ds(lo, FEAT)
            return remote(
                row_out.at[peer, piece], row_in.at[me_s, piece],
                send_sem, recv_sem(i), me_d, peer,
            )

        return copy

    late_copy = piece_copy(0, late_s, lambda i: late_r)
    row_copy = piece_copy(FEAT, row_s, lambda i: row_r.at[i])

    def col_copy(i, j):
        peer = peer_at(me_s, i, j, ng, 1)
        return remote(
            col_out.at[peer], col_in.at[me_s], col_s, col_r.at[i], me_d, peer
        )

    def own_piece(lo, sem):
        piece = pl.ds(lo, FEAT)
        return pltpu.make_async_copy(row_out.at[me_s, piece], row_in.at[me_s, piece], sem)

    own_late = own_piece(0, late_r)
    own_row = own_piece(FEAT, row_r.at[0])
    own_col = pltpu.make_async_copy(col_out.at[me_s], col_in.at[me_s], col_r.at[0])
    def one_step(k, p, grad=True):
        score_stage(k + 1, 1 - p)
        soft_stage(p)
        if grad:
            grad_stage(k - 1, 1 - p)

    landed(qd_in.at[pl.ds(0, 4)], qd_r.at[0])
    score_stage(0, 0)
    one_step(0, 0, grad=False)
    one_step(1, 1)
    one_step(2, 0)

    def four_rows(i, c):
        @pl.when(i > 0)
        def _():
            start_group(i - 1, own_row, row_copy)

        landed(qd_in.at[pl.ds(0, 4)], qd_r.at[i + 1])
        for u in range(4):
            one_step(3 + 4 * i + u, (1 + u) % 2)
        return c

    lax.fori_loop(0, ng - 1, four_rows, 0)
    start_group(ng - 2, own_row, row_copy)
    soft_stage(1)
    grad_stage(nb - 2, 0)
    grad_stage(nb - 1, 1)
    start_group(ng - 1, own_row, row_copy)
    own_late.start()

    def col_send(i, c):
        for j in range(4):
            peer = peer_at(me_s, i, j, ng, 1)
            total = chain[table[SLOTS, peer]]
            col_out[peer, :FEAT] = (total[:FEAT] * scale).astype(BF16)
            col_out[peer, FEAT:] = total[FEAT:].astype(BF16)
        start_group(i, own_col, col_copy)
        return c

    lax.fori_loop(0, ng, col_send, 0)
    others = nd // 2 - 1
    if others:
        landed(xt_all.at[:, pl.ds(0, others * BLK)], xt_r)
    for k in range(1, nd // 2):
        share_copy(k).start()

    def late_send(i, c):
        @pl.when(i > 0)
        def _():
            late_copy(i, 0).start()

        for j in range(1, 4):
            late_copy(i, j).start()
        return c


    def tile_own(g, m):
        t = m * ng + g
        return pltpu.make_async_copy(
            dq.at[g, pl.ds(m * BLK, BLK)], wg_in.at[lanes(t % tpd), lanes(me_d)],
            tile_r.at[t % tpd],
        )

    def tile_copy(g, m):
        t = m * ng + g
        return remote(
            dq.at[g, pl.ds(m * BLK, BLK)], wg_in.at[lanes(t % tpd), lanes(me_d)],
            tile_s, tile_r.at[t % tpd], t // tpd, me_s,
        )

    def tile_send(g, m):
        t = m * ng + g

        @pl.when(t // tpd == me_d)
        def _():
            tile_own(g, m).start()

        @pl.when(t // tpd != me_d)
        def _():
            tile_copy(g, m).start()

    def take_rows(i, c):
        g = sent_group(i)
        landed(row_in.at[pl.ds(0, 4), pl.ds(FEAT, FEAT)], row_r.at[i])
        for j in range(4):
            dq[g, j * FEAT : (j + 1) * FEAT] = row_in[4 * g + j, FEAT:]
        tile_send(g, 0)
        return c

    def take_late(g, c):
        mix = jnp.concatenate([row_in[4 * g + j, :FEAT] for j in range(4)], axis=0)
        mix_ref[:, lanes(g)] = jnp.transpose(mix.astype(F32)).astype(BF16)
        return c

    def take_cols(i, c):
        g = got_group(i)
        landed(col_in.at[pl.ds(0, 4)], col_r.at[i])
        for j in range(4):
            dq[g, BLK + j * FEAT : BLK + (j + 1) * FEAT] = col_in[4 * g + j, :FEAT]
            dq[g, 2 * BLK + j * FEAT : 2 * BLK + (j + 1) * FEAT] = col_in[4 * g + j, FEAT:]
        tile_send(g, 1)
        tile_send(g, 2)
        return c

    def bring_home(i, c):
        late_send(i, 0)
        take_rows(i, 0)
        return take_cols(i, c)

    lax.fori_loop(0, ng, bring_home, 0)
    xt_keep.wait()
    landed(xt_all.at[:, pl.ds(0, nd // 2 * BLK)], share_r)

    chunk = nz * FEAT
    half = chunk // 2
    up, down = lax.rem(me_y + 1, ny), lax.rem(me_y + ny - 1, ny)
    across = lax.rem(me_y + 2, ny)

    def rows_of(y, which):
        return pl.ds(pl.multiple_of(y * chunk + which * half, half), half)

    def relay_copy(t, way):
        return remote(
            part.at[t, rows_of(across, way)], relay.at[t, way],
            relay_s, relay_r.at[t], me_d, (up, down)[way] * nz + me_z,
        )

    def fold_copy(t, way, which):
        return remote(
            part.at[t, rows_of((up, down)[way], which)], fold.at[t, way, which],
            fold_s, fold_r.at[t],
            me_d, (up, down)[way] * nz + me_z,
        )

    def last_copy(k):
        to = lax.rem(me_z + k, nz)
        return remote(
            mid.at[pl.ds(pl.multiple_of(to * FEAT, FEAT), FEAT)], last_in.at[k - 1],
            last_s, last_r, me_d, me_y * nz + to,
        )

    def z_copy(k):
        to = lax.rem(me_z + k, nz)
        return remote(zpart.at[:, to], z_in.at[k - 1], z_s, z_r, me_d, me_y * nz + to)

    def y_copy(k):
        to = lax.rem(me_y + k, ny)
        return remote(z_mid.at[to], y_in.at[k - 1], y_s, y_r, me_d, to * nz + me_z)

    far_first = sorted(range(1, nz), key=lambda k: -min(k, nz - k))
    pairs = tpd - 1
    for t in range(tpd):
        landed(wg_in.at[pl.ds(t * BLK, BLK)], tile_r.at[t])

    def contract(rows, first, last):
        return lax.dot_general(
            xt_all[rows, :], wg_in[first * BLK : last * BLK], (((1,), (1,)), ((), ())),
            preferred_element_type=F32,
        ).astype(BF16)

    def fill(y):
        rows = pl.ds(pl.multiple_of(y * chunk, chunk), chunk)
        value = contract(rows, 0, pairs)
        for t in range(pairs):
            part[t, rows] = value[:, t * BLK : (t + 1) * BLK]

    fill(across)
    for t in range(pairs):
        for way in range(2):
            relay_copy(t, way).start()
    zpart[...] = contract(slice(None), pairs, tpd).reshape(ny, nz, FEAT, BLK)
    for k in far_first:
        z_copy(k).start()
    fill(up)
    fill(down)
    for t in range(pairs):
        for way in range(2):
            fold_copy(t, way, 1 - way).start()
    fill(me_y)

    def node_cols(n, c):
        width = 2 * BLK
        cols = pl.ds(pl.multiple_of(n * width, width), width)
        total = jnp.zeros((width, BLK), F32)
        for g in range(ng):
            total += jnp.dot(w_vm[g, cols], dq[g], preferred_element_type=F32)
        gn_ref[:, cols] = jnp.transpose(total).astype(BF16)
        return c

    steps_gn = hidden // (2 * BLK)
    lax.fori_loop(0, steps_gn // 4, node_cols, 0)
    for t in range(pairs):
        landed(relay.at[t], relay_r.at[t])
        for way in range(2):
            rows = rows_of((up, down)[way], way)
            part[t, rows] = (
                part[t, rows].astype(F32) + relay[t, way].astype(F32)
            ).astype(BF16)
            fold_copy(t, way, way).start()
    lax.fori_loop(steps_gn // 4, steps_gn // 2, node_cols, 0)
    for t in range(pairs):
        landed(fold.at[t], fold_r.at[t])
        for which in range(2):
            total = part[t, rows_of(me_y, which)].astype(F32)
            for way in range(2):
                total += fold[t, way, which].astype(F32)
            mid[which * half : (which + 1) * half, t * BLK : (t + 1) * BLK] = total.astype(BF16)
    for k in far_first:
        last_copy(k).start()
    lax.fori_loop(steps_gn // 2, steps_gn, node_cols, 0)
    gn_done = pltpu.make_async_copy(gn_ref, gn_out, out_sem.at[1])
    gn_done.start()
    landed(z_in, z_r)
    total = zpart[:, me_z].astype(F32)
    for k in range(1, nz):
        total += z_in[k - 1].astype(F32)
    z_mid[...] = total.astype(BF16)
    for k in range(1, ny):
        y_copy(k).start()

    landed(row_in.at[:, pl.ds(0, FEAT)], late_r)
    lax.fori_loop(0, ng, take_late, 0)
    mix_done = pltpu.make_async_copy(mix_ref, mix_out, out_sem.at[0])
    mix_done.start()
    landed(kv_out.at[pl.ds(0, ns - 1)], kv_s)
    landed(qd_out.at[pl.ds(0, ns - 1)], qd_s)
    if others:
        landed(xt_all.at[:, pl.ds(0, others * BLK)], xt_s)
    landed(xt_all.at[:, pl.ds(0, nd // 2 * BLK)], share_s)
    landed(row_out.at[pl.ds(0, ns - 1), pl.ds(FEAT, FEAT)], row_s)
    landed(row_out.at[pl.ds(0, ns - 1), pl.ds(0, FEAT)], late_s)
    landed(col_out.at[pl.ds(0, ns - 1)], col_s)
    landed(dq.at[pl.ds(0, ng - 1)], tile_s)
    landed(relay, relay_s)
    landed(fold, fold_s)
    landed(last_in, last_r)
    total = mid[pl.ds(pl.multiple_of(me_z * FEAT, FEAT), FEAT)].astype(F32)
    for k in range(1, nz):
        total += last_in[k - 1].astype(F32)
    wg_ref[:, : pairs * BLK] = total
    landed(y_in, y_r)
    total = z_mid[me_y].astype(F32)
    for k in range(1, ny):
        total += y_in[k - 1].astype(F32)
    wg_ref[:, pairs * BLK :] = total
    wg_done = pltpu.make_async_copy(wg_ref, wg_out, out_sem.at[2])
    wg_done.start()
    landed(last_in, last_s)
    landed(z_in, z_s)
    landed(y_in, y_s)
    mix_done.wait()
    gn_done.wait()
    wg_done.wait()


def settle_kernel(mix_in, gn_in, wg_in, mix_out, gn_out, wg_out, mix_vm, gn_vm, wg_vm, sem):
    triples = ((mix_in, mix_vm, mix_out), (gn_in, gn_vm, gn_out), (wg_in, wg_vm, wg_out))
    loads = [pltpu.make_async_copy(a, b, sem.at[0, n]) for n, (a, b, _) in enumerate(triples)]
    stores = [pltpu.make_async_copy(b, c, sem.at[1, n]) for n, (_, b, c) in enumerate(triples)]
    for load in loads:
        load.start()
    for load, store in zip(loads, stores):
        load.wait()
        store.start()
    for store in stores:
        store.wait()


def per_device(nd, ns, nodes, w_qkv, incoming_adjoint, block_cols, block_counts):
    rows, hidden = nodes.shape[1:]
    ny, nz = 4, ns // 4
    ng = ns // 4
    tpd = 3 * ng // nd
    chunk = nz * FEAT
    any_spec = pl.BlockSpec(memory_space=pl.ANY)
    dma = pltpu.SemaphoreType.DMA
    slots_first = jnp.swapaxes(block_cols, 1, 2)
    out_shape = (
        jax.ShapeDtypeStruct((rows, hidden), BF16),
        jax.ShapeDtypeStruct((rows, hidden), BF16),
        jax.ShapeDtypeStruct((FEAT, tpd * BLK), F32),
    )
    out_buffers = [pltpu.VMEM(out.shape, out.dtype) for out in out_shape]
    results = pl.pallas_call(
        functools.partial(whole_kernel, nd, ns, ny, nz, tpd),
        out_shape=out_shape,
        in_specs=[any_spec] * 5,
        out_specs=(any_spec,) * 3,
        scratch_shapes=[
            pltpu.SMEM((1, SLOTS, ns), jnp.int32),
            pltpu.VMEM((SLOTS, ns), jnp.int32),
            pltpu.SMEM((1, ns), jnp.int32),
            *out_buffers,
            pltpu.VMEM((rows, hidden), BF16),
            pltpu.VMEM((rows, hidden), BF16),
            pltpu.VMEM((ng, hidden, 3 * BLK), BF16),
            pltpu.VMEM((ns, 2 * FEAT, BLK), BF16),
            pltpu.VMEM((ns, 2 * FEAT, BLK), BF16),
            pltpu.VMEM((ns, 2 * FEAT, BLK), BF16),
            pltpu.VMEM((ns, 2 * FEAT, BLK), BF16),
            pltpu.VMEM((ns, BLK, 2 * FEAT), BF16),
            pltpu.VMEM((hidden, BLK), BF16),
            pltpu.VMEM((hidden, nd * BLK), BF16),
            pltpu.VMEM((SLOTS * ns + 1, 2 * FEAT, BLK), F32),
            pltpu.VMEM((ns, 2 * FEAT, BLK), BF16),
            pltpu.VMEM((ns, 2 * FEAT, BLK), BF16),
            pltpu.VMEM((ns, 2 * FEAT, BLK), BF16),
            pltpu.VMEM((ns, 2 * FEAT, BLK), BF16),
            pltpu.VMEM((SLOTS, BLK, 2 * BLK), F32),
            pltpu.VMEM((SLOTS, BLK, 2 * BLK), F32),
            pltpu.VMEM((1, BLK), F32),
            pltpu.VMEM((1, BLK), F32),
            pltpu.VMEM((SLOTS * BLK, 2 * BLK), BF16),
            pltpu.VMEM((SLOTS * BLK, 2 * BLK), BF16),
            pltpu.VMEM((8, BLK), jnp.int32),
            pltpu.SMEM((8, BLK), jnp.int32),
            pltpu.VMEM((ng, 3 * BLK, BLK), BF16),
            pltpu.VMEM((tpd * BLK, nd * BLK), BF16),
            pltpu.VMEM((tpd - 1, hidden, BLK), BF16),
            pltpu.VMEM((tpd - 1, 2, chunk // 2, BLK), BF16),
            pltpu.VMEM((tpd - 1, 2, 2, chunk // 2, BLK), BF16),
            pltpu.VMEM((chunk, (tpd - 1) * BLK), BF16),
            pltpu.VMEM((nz - 1, FEAT, (tpd - 1) * BLK), BF16),
            dma((2, ng)),
            dma((5,)),
            dma,
            dma((ng,)),
            dma,
            dma((ng,)),
            dma,
            dma,
            dma,
            dma((ng,)),
            dma,
            dma((ng,)),
            dma((2,)),
            dma,
            dma((tpd,)),
            dma,
            dma((tpd,)),
            dma,
            dma((tpd,)),
            dma,
            dma,
            dma,
            dma,
            dma,
            dma,
            dma((3,)),
            pltpu.VMEM((ny, nz, FEAT, BLK), BF16),
            pltpu.VMEM((nz - 1, ny, FEAT, BLK), BF16),
            pltpu.VMEM((ny, FEAT, BLK), BF16),
            pltpu.VMEM((ny - 1, FEAT, BLK), BF16),
            dma,
            dma,
            dma,
            dma,
        ],
        compiler_params=pltpu.CompilerParams(
            collective_id=1, has_side_effects=True, vmem_limit_bytes=VMEM_LIMIT
        ),
        name="whole",
    )(nodes, w_qkv, incoming_adjoint, slots_first, block_counts)
    mixture, grad_nodes, weight_grad = pl.pallas_call(
        settle_kernel,
        out_shape=out_shape,
        in_specs=[any_spec] * 3,
        out_specs=(any_spec,) * 3,
        scratch_shapes=[*out_buffers, dma((2, 3))],
        compiler_params=pltpu.CompilerParams(vmem_limit_bytes=VMEM_LIMIT),
        name="settle",
    )(*results)
    return (mixture[None], grad_nodes[None], jnp.transpose(weight_grad))


def solution(mesh):
    nd, ns = mesh.shape["dp"], mesh.shape["seq"]
    in_specs = (P("dp", "seq", None), P(), P("dp", "seq", None), P("dp", None, None), P("dp", None))
    out_specs = (P("dp", "seq", None), P("dp", "seq", None), P("dp", "seq"))
    return jax.shard_map(
        functools.partial(per_device, nd, ns),
        mesh=mesh,
        in_specs=in_specs,
        out_specs=out_specs,
        check_vma=False,
    )
```

```python
import functools
import math

import jax
import jax.numpy as jnp
from jax import lax
from jax.experimental import pallas as pl
from jax.experimental.pallas import tpu as pltpu
from jax.sharding import PartitionSpec as P

MESH = pl.DeviceIdType.MESH
BLK = 128
FEAT = 32
SLOTS = 4
F32 = jnp.float32
BF16 = jnp.bfloat16
VMEM_LIMIT = 62 * 1024 * 1024


def lane_ids(shape):
    return lax.broadcasted_iota(jnp.int32, shape, len(shape) - 1)


def greet(me_d, me_s, nd, ns):
    barrier = pltpu.get_barrier_semaphore()

    def seq_hello(k, c):
        far = 1 + lax.rem(k + ns // 2, ns - 1)
        pl.semaphore_signal(
            barrier, inc=1, device_id=(me_d, lax.rem(me_s + far, ns)), device_id_type=MESH
        )
        return c

    def dp_hello(k, c):
        pl.semaphore_signal(
            barrier, inc=1, device_id=(lax.rem(me_d + k, nd), me_s), device_id_type=MESH
        )
        return c

    lax.fori_loop(1, ns, seq_hello, 0)
    lax.fori_loop(1, nd, dp_hello, 0)
    return barrier


def peer_at(me_s, i, j, ng, sign):
    group = lax.rem(me_s // 4 + sign * i + ng, ng)
    return 4 * group + lax.rem(me_s % 4 + sign * j + 4, 4)


def whole_kernel(
    nd, ns, ny, nz, tpd,
    x_in, w_in, cot_in, cols_in, counts_in,
    mix_out, gn_out, wg_out,
    cols_ref, cols_vec, counts_ref, mix_ref, gn_ref, wg_ref, x_vm, cot_vm, w_vm, kv_out, kv_in, qd_out, qd_in, natural, xt_own, xt_all,
    chain, row_out, col_out, row_in, col_in,
    raw_even, raw_odd, top_even, top_odd, pair_even, pair_odd,
    table_vm, table, dq, wg_in, part, relay, fold, mid, last_in,
    w_sem, load_sem, kv_s, kv_r, qd_s, qd_r, xt_s, xt_r, row_s, row_r, col_s, col_r,
    own_sem, tile_s, tile_r, relay_s, relay_r, fold_s, fold_r, last_s, last_r, late_s, late_r, share_s, share_r, out_sem,
    zpart, z_in, z_mid, y_in, z_s, z_r, y_s, y_r,
):
    me_d, me_s = lax.axis_index("dp"), lax.axis_index("seq")
    me_y, me_z = me_s // nz, me_s % nz
    ng = ns // 4
    my_group = me_s // 4
    hidden = ng * BLK
    nb = ns
    scale = 1.0 / math.sqrt(FEAT)
    to_exp2 = scale * math.log2(math.e)

    def lanes(t):
        return pl.ds(pl.multiple_of(t * BLK, BLK), BLK)

    def sent_group(i):
        return lax.rem(my_group + i, ng)

    def got_group(i):
        return lax.rem(my_group - i + ng, ng)

    def row_at(k):
        return peer_at(me_s, k // 4, k % 4, ng, -1)

    def remote(src, dst, send_sem, recv_sem, d, s):
        return pltpu.make_async_remote_copy(
            src_ref=src, dst_ref=dst, send_sem=send_sem, recv_sem=recv_sem,
            device_id=(d, s), device_id_type=MESH,
        )

    def landed(ref, sem):
        pltpu.make_async_copy(ref, ref, sem).wait()

    load_x = pltpu.make_async_copy(x_in.at[0], x_vm, load_sem.at[0])
    load_cot = pltpu.make_async_copy(cot_in.at[0], cot_vm, load_sem.at[1])
    load_x.start()

    def w_start(part, i):
        g = sent_group(i)
        for m in ((1, 2), (0,))[part]:
            pltpu.make_async_copy(
                w_in.at[:, lanes(m * ng + g)],
                w_vm.at[g, :, pl.ds(m * BLK, BLK)],
                w_sem.at[part, i],
            ).start()

    ahead = 2
    for i in range(ahead):
        w_start(0, i)
    barrier = greet(me_d, me_s, nd, ns)
    load_cot.start()
    small_loads = [
        pltpu.make_async_copy(src, dst, load_sem.at[2 + n])
        for n, (src, dst) in enumerate(
            ((cols_in, cols_ref), (cols_in.at[0], cols_vec), (counts_in, counts_ref))
        )
    ]
    load_x.wait()

    def pieces_copy(out, into, send_sem, recv_sem):
        def copy(i, j):
            peer = peer_at(me_s, i, j, ng, 1)
            return remote(out.at[peer], into.at[me_s], send_sem, recv_sem.at[i], me_d, peer)

        return copy, pltpu.make_async_copy(out.at[me_s], into.at[me_s], recv_sem.at[0])

    kv_copy, own_kv = pieces_copy(kv_out, kv_in, kv_s, kv_r)
    qd_copy, own_qd = pieces_copy(qd_out, qd_in, qd_s, qd_r)

    def start_group(i, own, copy):
        @pl.when(i == 0)
        def _():
            own.start()

        @pl.when(i > 0)
        def _():
            copy(i, 0).start()

        for j in range(1, 4):
            copy(i, j).start()

    def project_kv(i, c):
        g = sent_group(i)
        landed(w_vm.at[g, :, pl.ds(BLK, 2 * BLK)], w_sem.at[0, i])
        flat = jnp.dot(x_vm[...], w_vm[g, :, BLK:], preferred_element_type=F32)
        for m in range(2):
            turned = jnp.transpose(flat[:, m * BLK : (m + 1) * BLK]).astype(BF16)
            for j in range(4):
                kv_out[4 * g + j, m * FEAT : (m + 1) * FEAT] = turned[
                    j * FEAT : (j + 1) * FEAT
                ]

        @pl.when(i == 0)
        def _():
            pl.semaphore_wait(barrier, ns + nd - 2)

        start_group(i, own_kv, kv_copy)

        @pl.when(i + ahead < ng)
        def _():
            w_start(0, i + ahead)

        w_start(1, i)
        return c

    def project_q(i, c):
        g = sent_group(i)
        landed(w_vm.at[g, :, pl.ds(0, BLK)], w_sem.at[1, i])
        flat = jnp.dot(x_vm[...], w_vm[g, :, :BLK], preferred_element_type=F32)
        for m, piece in enumerate((flat, cot_vm[:, lanes(g)].astype(F32))):
            turned = jnp.transpose(piece).astype(BF16)
            for j in range(4):
                qd_out[4 * g + j, m * FEAT : (m + 1) * FEAT] = turned[
                    j * FEAT : (j + 1) * FEAT
                ]
        start_group(i, own_qd, qd_copy)
        return c

    lax.fori_loop(0, ng, project_kv, 0)
    for load in small_loads:
        load.start()
    load_cot.wait()
    lax.fori_loop(0, ng, project_q, 0)

    xt_own[...] = jnp.transpose(x_vm[...].astype(F32)).astype(BF16)
    xt_keep = pltpu.make_async_copy(xt_own, xt_all.at[:, lanes(me_d)], own_sem.at[0])
    xt_keep.start()

    sibling = me_d + 1 - 2 * (me_d % 2)

    def xt_copy(k):
        return remote(
            xt_own, xt_all.at[:, lanes(me_d)], xt_s, xt_r,
            lax.rem(me_d + 2 * k, nd), me_s,
        )

    def share_copy(k):
        here = lanes(lax.rem(me_d - 2 * k + nd, nd))
        return remote(
            xt_all.at[:, here] if k else xt_own, xt_all.at[:, here],
            share_s, share_r, sibling, me_s,
        )

    for k in range(1, nd // 2):
        xt_copy(k).start()
    share_copy(0).start()

    for load in small_loads:
        load.wait()
    named_now = cols_vec[...]
    row_ids = lane_ids((SLOTS, nb))
    place = 4 * lax.rem(my_group - row_ids // 4 + ng, ng) + lax.rem(
        me_s % 4 - row_ids % 4 + 4, 4
    )
    col_ids = lane_ids((1, nb))

    def link(k, carry):
        before, final = carry
        r = row_at(k)
        for s in range(SLOTS):
            name = cols_ref[0, s, r]
            before = jnp.where((named_now == name) & (place > k), 4 * k + s, before)
            final = jnp.where(col_ids == name, 4 * k + s, final)
        return before, final

    before, final = lax.fori_loop(
        0, nb, link,
        (jnp.full((SLOTS, nb), SLOTS * nb, jnp.int32), jnp.zeros((1, nb), jnp.int32)),
    )
    table_vm[...] = jnp.zeros_like(table_vm)
    table_vm[:SLOTS, :nb] = before
    table_vm[SLOTS : SLOTS + 1, :nb] = final
    table_copy = pltpu.make_async_copy(table_vm, table, own_sem.at[1])
    table_copy.start()
    chain[SLOTS * nb] = jnp.zeros((2 * FEAT, BLK), F32)

    raw, top, pair = (raw_even, raw_odd), (top_even, top_odd), (pair_even, pair_odd)

    def arrive(i, c):
        landed(kv_in.at[pl.ds(0, 4)], kv_r.at[i])
        for j in range(4):
            b = row_at(4 * i + j)
            natural[b] = jnp.transpose(kv_in[b].astype(F32)).astype(BF16)
        return c

    lax.fori_loop(0, ng, arrive, 0)
    table_copy.wait()

    def spread_pieces(r, side):
        queries, cot = qd_in[r, :FEAT], qd_in[r, FEAT:]
        empty = jnp.zeros((FEAT, BLK), BF16)
        upper, lower = [queries, empty], [empty, cot]
        if side:
            upper, lower = upper[::-1], lower[::-1]
        return jnp.concatenate(
            [jnp.concatenate(upper, axis=1), jnp.concatenate(lower, axis=1)], axis=0
        )

    def score_stage(k, p):
        r = row_at(k)
        count = counts_ref[0, r]
        keys = jnp.concatenate([natural[cols_ref[0, s, r]] for s in range(SLOTS)], axis=0)
        both = jnp.dot(keys, spread_pieces(r, 0), preferred_element_type=F32)
        best = None
        for s in range(SLOTS):
            block = both[s * BLK : (s + 1) * BLK]
            scores = block[:, :BLK]
            if s:
                scores = jnp.where(s < count, scores, -jnp.inf)
            raw[p][s, :, :BLK] = scores
            raw[p][s, :, BLK:] = block[:, BLK:]
            peak = jnp.max(scores, axis=0, keepdims=True)
            best = peak if best is None else jnp.maximum(best, peak)
        top[p][...] = best * to_exp2

    def soft_stage(p):
        peak = top[p][...]
        total = mixed = None
        for s in range(SLOTS):
            weights = jnp.exp2(raw[p][s, :, :BLK] * to_exp2 - peak)
            t = jnp.sum(weights, axis=0, keepdims=True)
            m = jnp.sum(weights * raw[p][s, :, BLK:], axis=0, keepdims=True)
            total = t if total is None else total + t
            mixed = m if mixed is None else mixed + m
            raw[p][s, :, :BLK] = weights
        inverse = 1.0 / total
        delta = mixed * inverse
        for s in range(SLOTS):
            prob = raw[p][s, :, :BLK] * inverse
            rows = slice(s * BLK, (s + 1) * BLK)
            pair[p][rows, :BLK] = prob.astype(BF16)
            pair[p][rows, BLK:] = (prob * (raw[p][s, :, BLK:] - delta)).astype(BF16)

    def grad_stage(k, p):
        r = row_at(k)
        named = [cols_ref[0, s, r] for s in range(SLOTS)]
        both = pair[p][...]
        turned = jnp.concatenate([kv_in[n] for n in named], axis=1)
        row_side = jnp.dot(turned, both, preferred_element_type=F32)
        row_out[r, :FEAT] = row_side[FEAT:, :BLK].astype(BF16)
        row_out[r, FEAT:] = (row_side[:FEAT, BLK:] * scale).astype(BF16)
        key_side = lax.dot_general(
            spread_pieces(r, 1), both, (((1,), (1,)), ((), ())), preferred_element_type=F32
        )
        for s in range(SLOTS):
            chain[4 * k + s] = key_side[:, s * BLK : (s + 1) * BLK] + chain[table[s, r]]

    def piece_copy(lo, send_sem, recv_sem):
        def copy(i, j):
            peer = peer_at(me_s, i, j, ng, -1)
            piece = pl.ds(lo, FEAT)
            return remote(
                row_out.at[peer, piece], row_in.at[me_s, piece],
                send_sem, recv_sem(i), me_d, peer,
            )

        return copy

    late_copy = piece_copy(0, late_s, lambda i: late_r)
    row_copy = piece_copy(FEAT, row_s, lambda i: row_r.at[i])

    def col_copy(i, j):
        peer = peer_at(me_s, i, j, ng, 1)
        return remote(
            col_out.at[peer], col_in.at[me_s], col_s, col_r.at[i], me_d, peer
        )

    def own_piece(lo, sem):
        piece = pl.ds(lo, FEAT)
        return pltpu.make_async_copy(row_out.at[me_s, piece], row_in.at[me_s, piece], sem)

    own_late = own_piece(0, late_r)
    own_row = own_piece(FEAT, row_r.at[0])
    own_col = pltpu.make_async_copy(col_out.at[me_s], col_in.at[me_s], col_r.at[0])
    def one_step(k, p, grad=True):
        score_stage(k + 1, 1 - p)
        soft_stage(p)
        if grad:
            grad_stage(k - 1, 1 - p)

    landed(qd_in.at[pl.ds(0, 4)], qd_r.at[0])
    score_stage(0, 0)
    one_step(0, 0, grad=False)
    one_step(1, 1)
    one_step(2, 0)

    def four_rows(i, c):
        @pl.when(i > 1)
        def _():
            start_group(i - 2, own_row, row_copy)

        landed(qd_in.at[pl.ds(0, 4)], qd_r.at[i + 1])
        for u in range(4):
            one_step(3 + 4 * i + u, (1 + u) % 2)
        return c

    lax.fori_loop(0, ng - 1, four_rows, 0)
    for i in range(max(ng - 3, 0), ng - 1):
        start_group(i, own_row, row_copy)
    soft_stage(1)
    grad_stage(nb - 2, 0)
    grad_stage(nb - 1, 1)
    start_group(ng - 1, own_row, row_copy)
    own_late.start()

    def col_send(i, c):
        for j in range(4):
            peer = peer_at(me_s, i, j, ng, 1)
            total = chain[table[SLOTS, peer]]
            col_out[peer, :FEAT] = (total[:FEAT] * scale).astype(BF16)
            col_out[peer, FEAT:] = total[FEAT:].astype(BF16)
        start_group(i, own_col, col_copy)
        return c

    lax.fori_loop(0, ng, col_send, 0)
    others = nd // 2 - 1
    if others:
        landed(xt_all.at[:, pl.ds(0, others * BLK)], xt_r)
    for k in range(1, nd // 2):
        share_copy(k).start()

    def late_send(i, c):
        @pl.when(i > 0)
        def _():
            late_copy(i, 0).start()

        for j in range(1, 4):
            late_copy(i, j).start()
        return c


    def tile_own(g, m):
        t = m * ng + g
        return pltpu.make_async_copy(
            dq.at[g, pl.ds(m * BLK, BLK)], wg_in.at[lanes(t % tpd), lanes(me_d)],
            tile_r.at[t % tpd],
        )

    def tile_copy(g, m):
        t = m * ng + g
        return remote(
            dq.at[g, pl.ds(m * BLK, BLK)], wg_in.at[lanes(t % tpd), lanes(me_d)],
            tile_s, tile_r.at[t % tpd], t // tpd, me_s,
        )

    def tile_send(g, m):
        t = m * ng + g

        @pl.when(t // tpd == me_d)
        def _():
            tile_own(g, m).start()

        @pl.when(t // tpd != me_d)
        def _():
            tile_copy(g, m).start()

    def take_rows(i, c):
        g = sent_group(i)
        landed(row_in.at[pl.ds(0, 4), pl.ds(FEAT, FEAT)], row_r.at[i])
        for j in range(4):
            dq[g, j * FEAT : (j + 1) * FEAT] = row_in[4 * g + j, FEAT:]
        tile_send(g, 0)
        return c

    def take_late(g, c):
        mix = jnp.concatenate([row_in[4 * g + j, :FEAT] for j in range(4)], axis=0)
        mix_ref[:, lanes(g)] = jnp.transpose(mix.astype(F32)).astype(BF16)
        return c

    def take_cols(i, c):
        g = got_group(i)
        landed(col_in.at[pl.ds(0, 4)], col_r.at[i])
        for j in range(4):
            dq[g, BLK + j * FEAT : BLK + (j + 1) * FEAT] = col_in[4 * g + j, :FEAT]
            dq[g, 2 * BLK + j * FEAT : 2 * BLK + (j + 1) * FEAT] = col_in[4 * g + j, FEAT:]
        tile_send(g, 1)
        tile_send(g, 2)
        return c

    def bring_home(i, c):
        late_send(i, 0)
        take_rows(i, 0)
        return take_cols(i, c)

    lax.fori_loop(0, ng, bring_home, 0)
    xt_keep.wait()
    landed(xt_all.at[:, pl.ds(0, nd // 2 * BLK)], share_r)

    chunk = nz * FEAT
    half = chunk // 2
    up, down = lax.rem(me_y + 1, ny), lax.rem(me_y + ny - 1, ny)
    across = lax.rem(me_y + 2, ny)

    def rows_of(y, which):
        return pl.ds(pl.multiple_of(y * chunk + which * half, half), half)

    def relay_copy(t, way):
        return remote(
            part.at[t, rows_of(across, way)], relay.at[t, way],
            relay_s, relay_r.at[t], me_d, (up, down)[way] * nz + me_z,
        )

    def fold_copy(t, way, which):
        return remote(
            part.at[t, rows_of((up, down)[way], which)], fold.at[t, way, which],
            fold_s, fold_r.at[t],
            me_d, (up, down)[way] * nz + me_z,
        )

    def last_copy(k):
        to = lax.rem(me_z + k, nz)
        return remote(
            mid.at[pl.ds(pl.multiple_of(to * FEAT, FEAT), FEAT)], last_in.at[k - 1],
            last_s, last_r, me_d, me_y * nz + to,
        )

    def z_copy(k):
        to = lax.rem(me_z + k, nz)
        return remote(zpart.at[:, to], z_in.at[k - 1], z_s, z_r, me_d, me_y * nz + to)

    def y_copy(k):
        to = lax.rem(me_y + k, ny)
        return remote(z_mid.at[to], y_in.at[k - 1], y_s, y_r, me_d, to * nz + me_z)

    far_first = sorted(range(1, nz), key=lambda k: -min(k, nz - k))
    pairs = tpd - 1
    for t in range(tpd):
        landed(wg_in.at[pl.ds(t * BLK, BLK)], tile_r.at[t])

    def contract(rows, first, last):
        return lax.dot_general(
            xt_all[rows, :], wg_in[first * BLK : last * BLK], (((1,), (1,)), ((), ())),
            preferred_element_type=F32,
        ).astype(BF16)

    def fill(y):
        rows = pl.ds(pl.multiple_of(y * chunk, chunk), chunk)
        value = contract(rows, 0, pairs)
        for t in range(pairs):
            part[t, rows] = value[:, t * BLK : (t + 1) * BLK]

    fill(across)
    for t in range(pairs):
        for way in range(2):
            relay_copy(t, way).start()
    zpart[...] = contract(slice(None), pairs, tpd).reshape(ny, nz, FEAT, BLK)
    for k in far_first:
        z_copy(k).start()
    fill(up)
    fill(down)
    for t in range(pairs):
        for way in range(2):
            fold_copy(t, way, 1 - way).start()
    fill(me_y)

    def node_cols(n, c):
        width = 2 * BLK
        cols = pl.ds(pl.multiple_of(n * width, width), width)
        total = jnp.zeros((width, BLK), F32)
        for g in range(ng):
            total += jnp.dot(w_vm[g, cols], dq[g], preferred_element_type=F32)
        gn_ref[:, cols] = jnp.transpose(total).astype(BF16)
        return c

    steps_gn = hidden // (2 * BLK)
    lax.fori_loop(0, steps_gn // 4, node_cols, 0)
    for t in range(pairs):
        landed(relay.at[t], relay_r.at[t])
        for way in range(2):
            rows = rows_of((up, down)[way], way)
            part[t, rows] = (
                part[t, rows].astype(F32) + relay[t, way].astype(F32)
            ).astype(BF16)
            fold_copy(t, way, way).start()
    lax.fori_loop(steps_gn // 4, steps_gn // 2, node_cols, 0)
    for t in range(pairs):
        landed(fold.at[t], fold_r.at[t])
        for which in range(2):
            total = part[t, rows_of(me_y, which)].astype(F32)
            for way in range(2):
                total += fold[t, way, which].astype(F32)
            mid[which * half : (which + 1) * half, t * BLK : (t + 1) * BLK] = total.astype(BF16)
    for k in far_first:
        last_copy(k).start()
    lax.fori_loop(steps_gn // 2, 3 * steps_gn // 4, node_cols, 0)
    landed(z_in, z_r)
    total = zpart[:, me_z].astype(F32)
    for k in range(1, nz):
        total += z_in[k - 1].astype(F32)
    z_mid[...] = total.astype(BF16)
    for k in range(1, ny):
        y_copy(k).start()
    lax.fori_loop(3 * steps_gn // 4, steps_gn, node_cols, 0)
    gn_done = pltpu.make_async_copy(gn_ref, gn_out, out_sem.at[1])
    gn_done.start()

    landed(row_in.at[:, pl.ds(0, FEAT)], late_r)
    lax.fori_loop(0, ng, take_late, 0)
    mix_done = pltpu.make_async_copy(mix_ref, mix_out, out_sem.at[0])
    mix_done.start()
    landed(kv_out.at[pl.ds(0, ns - 1)], kv_s)
    landed(qd_out.at[pl.ds(0, ns - 1)], qd_s)
    if others:
        landed(xt_all.at[:, pl.ds(0, others * BLK)], xt_s)
    landed(xt_all.at[:, pl.ds(0, nd // 2 * BLK)], share_s)
    landed(row_out.at[pl.ds(0, ns - 1), pl.ds(FEAT, FEAT)], row_s)
    landed(row_out.at[pl.ds(0, ns - 1), pl.ds(0, FEAT)], late_s)
    landed(col_out.at[pl.ds(0, ns - 1)], col_s)
    landed(dq.at[pl.ds(0, ng - 1)], tile_s)
    landed(relay, relay_s)
    landed(fold, fold_s)
    landed(last_in, last_r)
    total = mid[pl.ds(pl.multiple_of(me_z * FEAT, FEAT), FEAT)].astype(F32)
    for k in range(1, nz):
        total += last_in[k - 1].astype(F32)
    wg_ref[:, : pairs * BLK] = total
    landed(y_in, y_r)
    total = z_mid[me_y].astype(F32)
    for k in range(1, ny):
        total += y_in[k - 1].astype(F32)
    wg_ref[:, pairs * BLK :] = total
    wg_done = pltpu.make_async_copy(wg_ref, wg_out, out_sem.at[2])
    wg_done.start()
    landed(last_in, last_s)
    landed(z_in, z_s)
    landed(y_in, y_s)
    mix_done.wait()
    gn_done.wait()
    wg_done.wait()


def settle_kernel(mix_in, gn_in, wg_in, mix_out, gn_out, wg_out, mix_vm, gn_vm, wg_vm, sem):
    triples = ((mix_in, mix_vm, mix_out), (gn_in, gn_vm, gn_out), (wg_in, wg_vm, wg_out))
    loads = [pltpu.make_async_copy(a, b, sem.at[0, n]) for n, (a, b, _) in enumerate(triples)]
    stores = [pltpu.make_async_copy(b, c, sem.at[1, n]) for n, (_, b, c) in enumerate(triples)]
    for load in loads:
        load.start()
    for load, store in zip(loads, stores):
        load.wait()
        store.start()
    for store in stores:
        store.wait()


def per_device(nd, ns, nodes, w_qkv, incoming_adjoint, block_cols, block_counts):
    rows, hidden = nodes.shape[1:]
    ny, nz = 4, ns // 4
    ng = ns // 4
    tpd = 3 * ng // nd
    chunk = nz * FEAT
    any_spec = pl.BlockSpec(memory_space=pl.ANY)
    dma = pltpu.SemaphoreType.DMA
    slots_first = jnp.swapaxes(block_cols, 1, 2)
    out_shape = (
        jax.ShapeDtypeStruct((rows, hidden), BF16),
        jax.ShapeDtypeStruct((rows, hidden), BF16),
        jax.ShapeDtypeStruct((FEAT, tpd * BLK), F32),
    )
    out_buffers = [pltpu.VMEM(out.shape, out.dtype) for out in out_shape]
    results = pl.pallas_call(
        functools.partial(whole_kernel, nd, ns, ny, nz, tpd),
        out_shape=out_shape,
        in_specs=[any_spec] * 5,
        out_specs=(any_spec,) * 3,
        scratch_shapes=[
            pltpu.SMEM((1, SLOTS, ns), jnp.int32),
            pltpu.VMEM((SLOTS, ns), jnp.int32),
            pltpu.SMEM((1, ns), jnp.int32),
            *out_buffers,
            pltpu.VMEM((rows, hidden), BF16),
            pltpu.VMEM((rows, hidden), BF16),
            pltpu.VMEM((ng, hidden, 3 * BLK), BF16),
            pltpu.VMEM((ns, 2 * FEAT, BLK), BF16),
            pltpu.VMEM((ns, 2 * FEAT, BLK), BF16),
            pltpu.VMEM((ns, 2 * FEAT, BLK), BF16),
            pltpu.VMEM((ns, 2 * FEAT, BLK), BF16),
            pltpu.VMEM((ns, BLK, 2 * FEAT), BF16),
            pltpu.VMEM((hidden, BLK), BF16),
            pltpu.VMEM((hidden, nd * BLK), BF16),
            pltpu.VMEM((SLOTS * ns + 1, 2 * FEAT, BLK), F32),
            pltpu.VMEM((ns, 2 * FEAT, BLK), BF16),
            pltpu.VMEM((ns, 2 * FEAT, BLK), BF16),
            pltpu.VMEM((ns, 2 * FEAT, BLK), BF16),
            pltpu.VMEM((ns, 2 * FEAT, BLK), BF16),
            pltpu.VMEM((SLOTS, BLK, 2 * BLK), F32),
            pltpu.VMEM((SLOTS, BLK, 2 * BLK), F32),
            pltpu.VMEM((1, BLK), F32),
            pltpu.VMEM((1, BLK), F32),
            pltpu.VMEM((SLOTS * BLK, 2 * BLK), BF16),
            pltpu.VMEM((SLOTS * BLK, 2 * BLK), BF16),
            pltpu.VMEM((8, BLK), jnp.int32),
            pltpu.SMEM((8, BLK), jnp.int32),
            pltpu.VMEM((ng, 3 * BLK, BLK), BF16),
            pltpu.VMEM((tpd * BLK, nd * BLK), BF16),
            pltpu.VMEM((tpd - 1, hidden, BLK), BF16),
            pltpu.VMEM((tpd - 1, 2, chunk // 2, BLK), BF16),
            pltpu.VMEM((tpd - 1, 2, 2, chunk // 2, BLK), BF16),
            pltpu.VMEM((chunk, (tpd - 1) * BLK), BF16),
            pltpu.VMEM((nz - 1, FEAT, (tpd - 1) * BLK), BF16),
            dma((2, ng)),
            dma((5,)),
            dma,
            dma((ng,)),
            dma,
            dma((ng,)),
            dma,
            dma,
            dma,
            dma((ng,)),
            dma,
            dma((ng,)),
            dma((2,)),
            dma,
            dma((tpd,)),
            dma,
            dma((tpd,)),
            dma,
            dma((tpd,)),
            dma,
            dma,
            dma,
            dma,
            dma,
            dma,
            dma((3,)),
            pltpu.VMEM((ny, nz, FEAT, BLK), BF16),
            pltpu.VMEM((nz - 1, ny, FEAT, BLK), BF16),
            pltpu.VMEM((ny, FEAT, BLK), BF16),
            pltpu.VMEM((ny - 1, FEAT, BLK), BF16),
            dma,
            dma,
            dma,
            dma,
        ],
        compiler_params=pltpu.CompilerParams(
            collective_id=1, has_side_effects=True, vmem_limit_bytes=VMEM_LIMIT
        ),
        name="whole",
    )(nodes, w_qkv, incoming_adjoint, slots_first, block_counts)
    mixture, grad_nodes, weight_grad = pl.pallas_call(
        settle_kernel,
        out_shape=out_shape,
        in_specs=[any_spec] * 3,
        out_specs=(any_spec,) * 3,
        scratch_shapes=[*out_buffers, dma((2, 3))],
        compiler_params=pltpu.CompilerParams(vmem_limit_bytes=VMEM_LIMIT),
        name="settle",
    )(*results)
    return (mixture[None], grad_nodes[None], jnp.transpose(weight_grad))


def solution(mesh):
    nd, ns = mesh.shape["dp"], mesh.shape["seq"]
    in_specs = (P("dp", "seq", None), P(), P("dp", "seq", None), P("dp", None, None), P("dp", None))
    out_specs = (P("dp", "seq", None), P("dp", "seq", None), P("dp", "seq"))
    return jax.shard_map(
        functools.partial(per_device, nd, ns),
        mesh=mesh,
        in_specs=in_specs,
        out_specs=out_specs,
        check_vma=False,
    )
```

```python
import functools
import math

import jax
import jax.numpy as jnp
from jax import lax
from jax.experimental import pallas as pl
from jax.experimental.pallas import tpu as pltpu
from jax.sharding import PartitionSpec as P

MESH = pl.DeviceIdType.MESH
BLK = 128
FEAT = 32
SLOTS = 4
F32 = jnp.float32
BF16 = jnp.bfloat16
VMEM_LIMIT = 62 * 1024 * 1024


def lane_ids(shape):
    return lax.broadcasted_iota(jnp.int32, shape, len(shape) - 1)


def greet(me_d, me_s, nd, ns):
    barrier = pltpu.get_barrier_semaphore()

    def seq_hello(k, c):
        pl.semaphore_signal(
            barrier, inc=1, device_id=(me_d, lax.rem(me_s + k, ns)), device_id_type=MESH
        )
        return c

    def dp_hello(k, c):
        pl.semaphore_signal(
            barrier, inc=1, device_id=(lax.rem(me_d + k, nd), me_s), device_id_type=MESH
        )
        return c

    lax.fori_loop(1, ns, seq_hello, 0)
    lax.fori_loop(1, nd, dp_hello, 0)
    return barrier


def peer_at(me_s, i, j, ng, sign):
    group = lax.rem(me_s // 4 + sign * i + ng, ng)
    return 4 * group + lax.rem(me_s % 4 + sign * j + 4, 4)


def whole_kernel(
    nd, ns, ny, nz, tpd,
    x_in, w_in, cot_in, cols_in, counts_in,
    mix_out, gn_out, wg_out,
    cols_ref, cols_vec, counts_ref, mix_ref, gn_ref, wg_ref, x_vm, cot_vm, w_vm, kv_out, kv_in, qd_out, qd_in, natural, xt_own, xt_all,
    chain, row_out, col_out, row_in, col_in,
    raw_even, raw_odd, top_even, top_odd, pair_even, pair_odd,
    table_vm, table, dq, wg_in, part, relay, fold, mid, last_in,
    w_sem, load_sem, kv_s, kv_r, qd_s, qd_r, xt_s, xt_r, row_s, row_r, col_s, col_r,
    own_sem, tile_s, tile_r, relay_s, relay_r, fold_s, fold_r, last_s, last_r, late_s, late_r, share_s, share_r, out_sem,
    zpart, z_in, z_mid, y_in, z_s, z_r, y_s, y_r,
):
    me_d, me_s = lax.axis_index("dp"), lax.axis_index("seq")
    me_y, me_z = me_s // nz, me_s % nz
    ng = ns // 4
    my_group = me_s // 4
    hidden = ng * BLK
    nb = ns
    scale = 1.0 / math.sqrt(FEAT)
    to_exp2 = scale * math.log2(math.e)

    def lanes(t):
        return pl.ds(pl.multiple_of(t * BLK, BLK), BLK)

    def sent_group(i):
        return lax.rem(my_group + i, ng)

    def got_group(i):
        return lax.rem(my_group - i + ng, ng)

    def row_at(k):
        return peer_at(me_s, k // 4, k % 4, ng, -1)

    def remote(src, dst, send_sem, recv_sem, d, s):
        return pltpu.make_async_remote_copy(
            src_ref=src, dst_ref=dst, send_sem=send_sem, recv_sem=recv_sem,
            device_id=(d, s), device_id_type=MESH,
        )

    def landed(ref, sem):
        pltpu.make_async_copy(ref, ref, sem).wait()

    barrier = greet(me_d, me_s, nd, ns)
    load_x = pltpu.make_async_copy(x_in.at[0], x_vm, load_sem.at[0])
    load_cot = pltpu.make_async_copy(cot_in.at[0], cot_vm, load_sem.at[1])
    load_x.start()

    def w_start(part, i):
        g = sent_group(i)
        for m in ((1, 2), (0,))[part]:
            pltpu.make_async_copy(
                w_in.at[:, lanes(m * ng + g)],
                w_vm.at[g, :, pl.ds(m * BLK, BLK)],
                w_sem.at[part, i],
            ).start()

    def kv_weights(i, c):
        w_start(0, i)
        return c

    def q_weights(i, c):
        w_start(1, i)
        return c

    small_loads = [
        pltpu.make_async_copy(src, dst, load_sem.at[2 + n])
        for n, (src, dst) in enumerate(
            ((cols_in, cols_ref), (cols_in.at[0], cols_vec), (counts_in, counts_ref))
        )
    ]
    lax.fori_loop(0, ng, kv_weights, 0)
    load_cot.start()
    lax.fori_loop(0, ng, q_weights, 0)
    for load in small_loads:
        load.start()
    load_x.wait()

    def pieces_copy(out, into, send_sem, recv_sem):
        def copy(i, j):
            peer = peer_at(me_s, i, j, ng, 1)
            return remote(out.at[peer], into.at[me_s], send_sem, recv_sem.at[i], me_d, peer)

        return copy, pltpu.make_async_copy(out.at[me_s], into.at[me_s], recv_sem.at[0])

    kv_copy, own_kv = pieces_copy(kv_out, kv_in, kv_s, kv_r)
    qd_copy, own_qd = pieces_copy(qd_out, qd_in, qd_s, qd_r)

    def start_group(i, own, copy):
        @pl.when(i == 0)
        def _():
            own.start()

        @pl.when(i > 0)
        def _():
            copy(i, 0).start()

        for j in range(1, 4):
            copy(i, j).start()

    def project_kv(i, c):
        g = sent_group(i)
        landed(w_vm.at[g, :, pl.ds(BLK, 2 * BLK)], w_sem.at[0, i])
        flat = jnp.dot(x_vm[...], w_vm[g, :, BLK:], preferred_element_type=F32)
        for m in range(2):
            turned = jnp.transpose(flat[:, m * BLK : (m + 1) * BLK]).astype(BF16)
            for j in range(4):
                kv_out[4 * g + j, m * FEAT : (m + 1) * FEAT] = turned[
                    j * FEAT : (j + 1) * FEAT
                ]

        @pl.when(i == 0)
        def _():
            pl.semaphore_wait(barrier, ns + nd - 2)

        start_group(i, own_kv, kv_copy)
        return c

    def project_q(i, c):
        g = sent_group(i)
        landed(w_vm.at[g, :, pl.ds(0, BLK)], w_sem.at[1, i])
        flat = jnp.dot(x_vm[...], w_vm[g, :, :BLK], preferred_element_type=F32)
        for m, piece in enumerate((flat, cot_vm[:, lanes(g)].astype(F32))):
            turned = jnp.transpose(piece).astype(BF16)
            for j in range(4):
                qd_out[4 * g + j, m * FEAT : (m + 1) * FEAT] = turned[
                    j * FEAT : (j + 1) * FEAT
                ]
        start_group(i, own_qd, qd_copy)
        return c

    lax.fori_loop(0, ng, project_kv, 0)
    load_cot.wait()
    lax.fori_loop(0, ng, project_q, 0)

    xt_own[...] = jnp.transpose(x_vm[...].astype(F32)).astype(BF16)
    xt_keep = pltpu.make_async_copy(xt_own, xt_all.at[:, lanes(me_d)], own_sem.at[0])
    xt_keep.start()

    sibling = me_d + 1 - 2 * (me_d % 2)

    def xt_copy(k):
        return remote(
            xt_own, xt_all.at[:, lanes(me_d)], xt_s, xt_r,
            lax.rem(me_d + 2 * k, nd), me_s,
        )

    def share_copy(k):
        here = lanes(lax.rem(me_d - 2 * k + nd, nd))
        return remote(
            xt_all.at[:, here] if k else xt_own, xt_all.at[:, here],
            share_s, share_r, sibling, me_s,
        )

    for k in range(1, nd // 2):
        xt_copy(k).start()
    share_copy(0).start()

    for load in small_loads:
        load.wait()
    named_now = cols_vec[...]
    row_ids = lane_ids((SLOTS, nb))
    place = 4 * lax.rem(my_group - row_ids // 4 + ng, ng) + lax.rem(
        me_s % 4 - row_ids % 4 + 4, 4
    )
    col_ids = lane_ids((1, nb))

    def link(k, carry):
        before, final = carry
        r = row_at(k)
        for s in range(SLOTS):
            name = cols_ref[0, s, r]
            before = jnp.where((named_now == name) & (place > k), 4 * k + s, before)
            final = jnp.where(col_ids == name, 4 * k + s, final)
        return before, final

    before, final = lax.fori_loop(
        0, nb, link,
        (jnp.full((SLOTS, nb), SLOTS * nb, jnp.int32), jnp.zeros((1, nb), jnp.int32)),
    )
    table_vm[...] = jnp.zeros_like(table_vm)
    table_vm[:SLOTS, :nb] = before
    table_vm[SLOTS : SLOTS + 1, :nb] = final
    table_copy = pltpu.make_async_copy(table_vm, table, own_sem.at[1])
    table_copy.start()
    chain[SLOTS * nb] = jnp.zeros((2 * FEAT, BLK), F32)

    raw, top, pair = (raw_even, raw_odd), (top_even, top_odd), (pair_even, pair_odd)

    def arrive(i, c):
        landed(kv_in.at[pl.ds(0, 4)], kv_r.at[i])
        for j in range(4):
            b = row_at(4 * i + j)
            natural[b] = jnp.transpose(kv_in[b].astype(F32)).astype(BF16)
        return c

    lax.fori_loop(0, ng, arrive, 0)
    table_copy.wait()

    def spread_pieces(r, side):
        queries, cot = qd_in[r, :FEAT], qd_in[r, FEAT:]
        empty = jnp.zeros((FEAT, BLK), BF16)
        upper, lower = [queries, empty], [empty, cot]
        if side:
            upper, lower = upper[::-1], lower[::-1]
        return jnp.concatenate(
            [jnp.concatenate(upper, axis=1), jnp.concatenate(lower, axis=1)], axis=0
        )

    def score_stage(k, p):
        r = row_at(k)
        count = counts_ref[0, r]
        keys = jnp.concatenate([natural[cols_ref[0, s, r]] for s in range(SLOTS)], axis=0)
        both = jnp.dot(keys, spread_pieces(r, 0), preferred_element_type=F32)
        best = None
        for s in range(SLOTS):
            block = both[s * BLK : (s + 1) * BLK]
            scores = block[:, :BLK]
            if s:
                scores = jnp.where(s < count, scores, -jnp.inf)
            raw[p][s, :, :BLK] = scores
            raw[p][s, :, BLK:] = block[:, BLK:]
            peak = jnp.max(scores, axis=0, keepdims=True)
            best = peak if best is None else jnp.maximum(best, peak)
        top[p][...] = best * to_exp2

    def soft_stage(p):
        peak = top[p][...]
        total = mixed = None
        for s in range(SLOTS):
            weights = jnp.exp2(raw[p][s, :, :BLK] * to_exp2 - peak)
            t = jnp.sum(weights, axis=0, keepdims=True)
            m = jnp.sum(weights * raw[p][s, :, BLK:], axis=0, keepdims=True)
            total = t if total is None else total + t
            mixed = m if mixed is None else mixed + m
            raw[p][s, :, :BLK] = weights
        inverse = 1.0 / total
        delta = mixed * inverse
        for s in range(SLOTS):
            prob = raw[p][s, :, :BLK] * inverse
            rows = slice(s * BLK, (s + 1) * BLK)
            pair[p][rows, :BLK] = prob.astype(BF16)
            pair[p][rows, BLK:] = (prob * (raw[p][s, :, BLK:] - delta)).astype(BF16)

    def grad_stage(k, p):
        r = row_at(k)
        named = [cols_ref[0, s, r] for s in range(SLOTS)]
        both = pair[p][...]
        turned = jnp.concatenate([kv_in[n] for n in named], axis=1)
        row_side = jnp.dot(turned, both, preferred_element_type=F32)
        row_out[r, :FEAT] = row_side[FEAT:, :BLK].astype(BF16)
        row_out[r, FEAT:] = (row_side[:FEAT, BLK:] * scale).astype(BF16)
        key_side = lax.dot_general(
            spread_pieces(r, 1), both, (((1,), (1,)), ((), ())), preferred_element_type=F32
        )
        for s in range(SLOTS):
            chain[4 * k + s] = key_side[:, s * BLK : (s + 1) * BLK] + chain[table[s, r]]

    def piece_copy(lo, send_sem, recv_sem):
        def copy(i, j):
            peer = row_at(4 * i + j)
            piece = pl.ds(lo, FEAT)
            return remote(
                row_out.at[peer, piece], row_in.at[me_s, piece],
                send_sem, recv_sem(i), me_d, peer,
            )

        return copy

    late_copy = piece_copy(0, late_s, lambda i: late_r)
    row_copy = piece_copy(FEAT, row_s, lambda i: row_r.at[i])

    def col_copy(i, j):
        peer = peer_at(me_s, i, j, ng, 1)
        return remote(
            col_out.at[peer], col_in.at[me_s], col_s, col_r.at[i], me_d, peer
        )

    def own_piece(lo, sem):
        piece = pl.ds(lo, FEAT)
        return pltpu.make_async_copy(row_out.at[me_s, piece], row_in.at[me_s, piece], sem)

    own_late = own_piece(0, late_r)
    own_row = own_piece(FEAT, row_r.at[0])
    own_col = pltpu.make_async_copy(col_out.at[me_s], col_in.at[me_s], col_r.at[0])
    def one_step(k, p, grad=True):
        score_stage(k + 1, 1 - p)
        soft_stage(p)
        if grad:
            grad_stage(k - 1, 1 - p)

    landed(qd_in.at[pl.ds(0, 4)], qd_r.at[0])
    score_stage(0, 0)
    one_step(0, 0, grad=False)
    one_step(1, 1)
    one_step(2, 0)

    def four_rows(i, c):
        @pl.when(i > 0)
        def _():
            start_group(i - 1, own_row, row_copy)

        landed(qd_in.at[pl.ds(0, 4)], qd_r.at[i + 1])
        for u in range(4):
            one_step(3 + 4 * i + u, (1 + u) % 2)
        return c

    lax.fori_loop(0, ng - 1, four_rows, 0)
    start_group(ng - 2, own_row, row_copy)
    soft_stage(1)
    grad_stage(nb - 2, 0)
    grad_stage(nb - 1, 1)
    start_group(ng - 1, own_row, row_copy)

    def col_send(i, c):
        for j in range(4):
            peer = peer_at(me_s, i, j, ng, 1)
            total = chain[table[SLOTS, peer]]
            col_out[peer, :FEAT] = (total[:FEAT] * scale).astype(BF16)
            col_out[peer, FEAT:] = total[FEAT:].astype(BF16)
        start_group(i, own_col, col_copy)
        return c

    lax.fori_loop(0, ng, col_send, 0)
    own_late.start()
    others = nd // 2 - 1
    if others:
        landed(xt_all.at[:, pl.ds(0, others * BLK)], xt_r)
    for k in range(1, nd // 2):
        share_copy(k).start()

    def late_send(i, c):
        @pl.when(i > 0)
        def _():
            late_copy(i, 0).start()

        for j in range(1, 4):
            late_copy(i, j).start()
        return c


    def tile_own(g, m):
        t = m * ng + g
        return pltpu.make_async_copy(
            dq.at[g, pl.ds(m * BLK, BLK)], wg_in.at[lanes(t % tpd), lanes(me_d)],
            tile_r.at[t % tpd],
        )

    def tile_copy(g, m):
        t = m * ng + g
        return remote(
            dq.at[g, pl.ds(m * BLK, BLK)], wg_in.at[lanes(t % tpd), lanes(me_d)],
            tile_s, tile_r.at[t % tpd], t // tpd, me_s,
        )

    def tile_send(g, m):
        t = m * ng + g

        @pl.when(t // tpd == me_d)
        def _():
            tile_own(g, m).start()

        @pl.when(t // tpd != me_d)
        def _():
            tile_copy(g, m).start()

    def take_rows(i, c):
        g = sent_group(i)
        landed(row_in.at[pl.ds(0, 4), pl.ds(FEAT, FEAT)], row_r.at[i])
        for j in range(4):
            dq[g, j * FEAT : (j + 1) * FEAT] = row_in[4 * g + j, FEAT:]
        tile_send(g, 0)
        return c

    def take_late(g, c):
        mix = jnp.concatenate([row_in[4 * g + j, :FEAT] for j in range(4)], axis=0)
        mix_ref[:, lanes(g)] = jnp.transpose(mix.astype(F32)).astype(BF16)
        return c

    def take_cols(i, c):
        g = got_group(i)
        landed(col_in.at[pl.ds(0, 4)], col_r.at[i])
        for j in range(4):
            dq[g, BLK + j * FEAT : BLK + (j + 1) * FEAT] = col_in[4 * g + j, :FEAT]
            dq[g, 2 * BLK + j * FEAT : 2 * BLK + (j + 1) * FEAT] = col_in[4 * g + j, FEAT:]
        tile_send(g, 1)
        tile_send(g, 2)
        return c

    def bring_home(i, c):
        late_send(i, 0)
        take_rows(i, 0)
        return take_cols(i, c)

    lax.fori_loop(0, ng, bring_home, 0)
    xt_keep.wait()
    landed(xt_all.at[:, pl.ds(0, nd // 2 * BLK)], share_r)

    chunk = nz * FEAT
    half = chunk // 2
    up, down = lax.rem(me_y + 1, ny), lax.rem(me_y + ny - 1, ny)
    across = lax.rem(me_y + 2, ny)

    def rows_of(y, which):
        return pl.ds(pl.multiple_of(y * chunk + which * half, half), half)

    def relay_copy(t, way):
        return remote(
            part.at[t, rows_of(across, way)], relay.at[t, way],
            relay_s, relay_r.at[t], me_d, (up, down)[way] * nz + me_z,
        )

    def fold_copy(t, way, which):
        return remote(
            part.at[t, rows_of((up, down)[way], which)], fold.at[t, way, which],
            fold_s, fold_r.at[t],
            me_d, (up, down)[way] * nz + me_z,
        )

    def last_copy(k):
        to = lax.rem(me_z + k, nz)
        return remote(
            mid.at[pl.ds(pl.multiple_of(to * FEAT, FEAT), FEAT)], last_in.at[k - 1],
            last_s, last_r, me_d, me_y * nz + to,
        )

    def z_copy(k):
        to = lax.rem(me_z + k, nz)
        return remote(zpart.at[:, to], z_in.at[k - 1], z_s, z_r, me_d, me_y * nz + to)

    def y_copy(k):
        to = lax.rem(me_y + k, ny)
        return remote(z_mid.at[to], y_in.at[k - 1], y_s, y_r, me_d, to * nz + me_z)

    far_first = sorted(range(1, nz), key=lambda k: -min(k, nz - k))
    pairs = tpd - 1
    for t in range(tpd):
        landed(wg_in.at[pl.ds(t * BLK, BLK)], tile_r.at[t])

    def contract(rows, first, last):
        return lax.dot_general(
            xt_all[rows, :], wg_in[first * BLK : last * BLK], (((1,), (1,)), ((), ())),
            preferred_element_type=F32,
        ).astype(BF16)

    def fill(y):
        rows = pl.ds(pl.multiple_of(y * chunk, chunk), chunk)
        value = contract(rows, 0, pairs)
        for t in range(pairs):
            part[t, rows] = value[:, t * BLK : (t + 1) * BLK]

    fill(across)
    for t in range(pairs):
        for way in range(2):
            relay_copy(t, way).start()
    zpart[...] = contract(slice(None), pairs, tpd).reshape(ny, nz, FEAT, BLK)
    for k in far_first:
        z_copy(k).start()
    fill(up)
    fill(down)
    for t in range(pairs):
        for way in range(2):
            fold_copy(t, way, 1 - way).start()
    fill(me_y)

    def node_cols(n, c):
        width = 2 * BLK
        cols = pl.ds(pl.multiple_of(n * width, width), width)
        total = jnp.zeros((width, BLK), F32)
        for g in range(ng):
            total += jnp.dot(w_vm[g, cols], dq[g], preferred_element_type=F32)
        gn_ref[:, cols] = jnp.transpose(total).astype(BF16)
        return c

    steps_gn = hidden // (2 * BLK)
    lax.fori_loop(0, steps_gn // 4, node_cols, 0)
    for t in range(pairs):
        landed(relay.at[t], relay_r.at[t])
        for way in range(2):
            rows = rows_of((up, down)[way], way)
            part[t, rows] = (
                part[t, rows].astype(F32) + relay[t, way].astype(F32)
            ).astype(BF16)
            fold_copy(t, way, way).start()
    lax.fori_loop(steps_gn // 4, steps_gn // 2, node_cols, 0)
    for t in range(pairs):
        landed(fold.at[t], fold_r.at[t])
        for which in range(2):
            total = part[t, rows_of(me_y, which)].astype(F32)
            for way in range(2):
                total += fold[t, way, which].astype(F32)
            mid[which * half : (which + 1) * half, t * BLK : (t + 1) * BLK] = total.astype(BF16)
    for k in far_first:
        last_copy(k).start()
    lax.fori_loop(steps_gn // 2, 3 * steps_gn // 4, node_cols, 0)
    landed(z_in, z_r)
    total = zpart[:, me_z].astype(F32)
    for k in range(1, nz):
        total += z_in[k - 1].astype(F32)
    z_mid[...] = total.astype(BF16)
    for k in range(1, ny):
        y_copy(k).start()
    lax.fori_loop(3 * steps_gn // 4, steps_gn, node_cols, 0)
    gn_done = pltpu.make_async_copy(gn_ref, gn_out, out_sem.at[1])
    gn_done.start()

    landed(row_in.at[:, pl.ds(0, FEAT)], late_r)
    lax.fori_loop(0, ng, take_late, 0)
    mix_done = pltpu.make_async_copy(mix_ref, mix_out, out_sem.at[0])
    mix_done.start()
    landed(kv_out.at[pl.ds(0, ns - 1)], kv_s)
    landed(qd_out.at[pl.ds(0, ns - 1)], qd_s)
    if others:
        landed(xt_all.at[:, pl.ds(0, others * BLK)], xt_s)
    landed(xt_all.at[:, pl.ds(0, nd // 2 * BLK)], share_s)
    landed(row_out.at[pl.ds(0, ns - 1), pl.ds(FEAT, FEAT)], row_s)
    landed(row_out.at[pl.ds(0, ns - 1), pl.ds(0, FEAT)], late_s)
    landed(col_out.at[pl.ds(0, ns - 1)], col_s)
    landed(dq.at[pl.ds(0, ng - 1)], tile_s)
    landed(relay, relay_s)
    landed(fold, fold_s)
    landed(last_in, last_r)
    total = mid[pl.ds(pl.multiple_of(me_z * FEAT, FEAT), FEAT)].astype(F32)
    for k in range(1, nz):
        total += last_in[k - 1].astype(F32)
    wg_ref[:, : pairs * BLK] = total
    landed(y_in, y_r)
    total = z_mid[me_y].astype(F32)
    for k in range(1, ny):
        total += y_in[k - 1].astype(F32)
    wg_ref[:, pairs * BLK :] = total
    wg_done = pltpu.make_async_copy(wg_ref, wg_out, out_sem.at[2])
    wg_done.start()
    landed(last_in, last_s)
    landed(z_in, z_s)
    landed(y_in, y_s)
    mix_done.wait()
    gn_done.wait()
    wg_done.wait()


def settle_kernel(mix_in, gn_in, wg_in, mix_out, gn_out, wg_out, mix_vm, gn_vm, wg_vm, sem):
    triples = ((mix_in, mix_vm, mix_out), (gn_in, gn_vm, gn_out), (wg_in, wg_vm, wg_out))
    loads = [pltpu.make_async_copy(a, b, sem.at[0, n]) for n, (a, b, _) in enumerate(triples)]
    stores = [pltpu.make_async_copy(b, c, sem.at[1, n]) for n, (_, b, c) in enumerate(triples)]
    for load in loads:
        load.start()
    for load, store in zip(loads, stores):
        load.wait()
        store.start()
    for store in stores:
        store.wait()


def per_device(nd, ns, nodes, w_qkv, incoming_adjoint, block_cols, block_counts):
    rows, hidden = nodes.shape[1:]
    ny, nz = 4, ns // 4
    ng = ns // 4
    tpd = 3 * ng // nd
    chunk = nz * FEAT
    any_spec = pl.BlockSpec(memory_space=pl.ANY)
    dma = pltpu.SemaphoreType.DMA
    slots_first = jnp.swapaxes(block_cols, 1, 2)
    out_shape = (
        jax.ShapeDtypeStruct((rows, hidden), BF16),
        jax.ShapeDtypeStruct((rows, hidden), BF16),
        jax.ShapeDtypeStruct((FEAT, tpd * BLK), F32),
    )
    out_buffers = [pltpu.VMEM(out.shape, out.dtype) for out in out_shape]
    results = pl.pallas_call(
        functools.partial(whole_kernel, nd, ns, ny, nz, tpd),
        out_shape=out_shape,
        in_specs=[any_spec] * 5,
        out_specs=(any_spec,) * 3,
        scratch_shapes=[
            pltpu.SMEM((1, SLOTS, ns), jnp.int32),
            pltpu.VMEM((SLOTS, ns), jnp.int32),
            pltpu.SMEM((1, ns), jnp.int32),
            *out_buffers,
            pltpu.VMEM((rows, hidden), BF16),
            pltpu.VMEM((rows, hidden), BF16),
            pltpu.VMEM((ng, hidden, 3 * BLK), BF16),
            pltpu.VMEM((ns, 2 * FEAT, BLK), BF16),
            pltpu.VMEM((ns, 2 * FEAT, BLK), BF16),
            pltpu.VMEM((ns, 2 * FEAT, BLK), BF16),
            pltpu.VMEM((ns, 2 * FEAT, BLK), BF16),
            pltpu.VMEM((ns, BLK, 2 * FEAT), BF16),
            pltpu.VMEM((hidden, BLK), BF16),
            pltpu.VMEM((hidden, nd * BLK), BF16),
            pltpu.VMEM((SLOTS * ns + 1, 2 * FEAT, BLK), F32),
            pltpu.VMEM((ns, 2 * FEAT, BLK), BF16),
            pltpu.VMEM((ns, 2 * FEAT, BLK), BF16),
            pltpu.VMEM((ns, 2 * FEAT, BLK), BF16),
            pltpu.VMEM((ns, 2 * FEAT, BLK), BF16),
            pltpu.VMEM((SLOTS, BLK, 2 * BLK), F32),
            pltpu.VMEM((SLOTS, BLK, 2 * BLK), F32),
            pltpu.VMEM((1, BLK), F32),
            pltpu.VMEM((1, BLK), F32),
            pltpu.VMEM((SLOTS * BLK, 2 * BLK), BF16),
            pltpu.VMEM((SLOTS * BLK, 2 * BLK), BF16),
            pltpu.VMEM((8, BLK), jnp.int32),
            pltpu.SMEM((8, BLK), jnp.int32),
            pltpu.VMEM((ng, 3 * BLK, BLK), BF16),
            pltpu.VMEM((tpd * BLK, nd * BLK), BF16),
            pltpu.VMEM((tpd - 1, hidden, BLK), BF16),
            pltpu.VMEM((tpd - 1, 2, chunk // 2, BLK), BF16),
            pltpu.VMEM((tpd - 1, 2, 2, chunk // 2, BLK), BF16),
            pltpu.VMEM((chunk, (tpd - 1) * BLK), BF16),
            pltpu.VMEM((nz - 1, FEAT, (tpd - 1) * BLK), BF16),
            dma((2, ng)),
            dma((5,)),
            dma,
            dma((ng,)),
            dma,
            dma((ng,)),
            dma,
            dma,
            dma,
            dma((ng,)),
            dma,
            dma((ng,)),
            dma((2,)),
            dma,
            dma((tpd,)),
            dma,
            dma((tpd,)),
            dma,
            dma((tpd,)),
            dma,
            dma,
            dma,
            dma,
            dma,
            dma,
            dma((3,)),
            pltpu.VMEM((ny, nz, FEAT, BLK), BF16),
            pltpu.VMEM((nz - 1, ny, FEAT, BLK), BF16),
            pltpu.VMEM((ny, FEAT, BLK), BF16),
            pltpu.VMEM((ny - 1, FEAT, BLK), BF16),
            dma,
            dma,
            dma,
            dma,
        ],
        compiler_params=pltpu.CompilerParams(
            collective_id=1, has_side_effects=True, vmem_limit_bytes=VMEM_LIMIT
        ),
        name="whole",
    )(nodes, w_qkv, incoming_adjoint, slots_first, block_counts)
    mixture, grad_nodes, weight_grad = pl.pallas_call(
        settle_kernel,
        out_shape=out_shape,
        in_specs=[any_spec] * 3,
        out_specs=(any_spec,) * 3,
        scratch_shapes=[*out_buffers, dma((2, 3))],
        compiler_params=pltpu.CompilerParams(vmem_limit_bytes=VMEM_LIMIT),
        name="settle",
    )(*results)
    return (mixture[None], grad_nodes[None], jnp.transpose(weight_grad))


def solution(mesh):
    nd, ns = mesh.shape["dp"], mesh.shape["seq"]
    in_specs = (P("dp", "seq", None), P(), P("dp", "seq", None), P("dp", None, None), P("dp", None))
    out_specs = (P("dp", "seq", None), P("dp", "seq", None), P("dp", "seq"))
    return jax.shard_map(
        functools.partial(per_device, nd, ns),
        mesh=mesh,
        in_specs=in_specs,
        out_specs=out_specs,
        check_vma=False,
    )
```

```python
import functools
import math

import jax
import jax.numpy as jnp
from jax import lax
from jax.experimental import pallas as pl
from jax.experimental.pallas import tpu as pltpu
from jax.sharding import PartitionSpec as P

MESH = pl.DeviceIdType.MESH
BLK = 128
FEAT = 32
SLOTS = 4
F32 = jnp.float32
BF16 = jnp.bfloat16
VMEM_LIMIT = 62 * 1024 * 1024


def lane_ids(shape):
    return lax.broadcasted_iota(jnp.int32, shape, len(shape) - 1)


def greet(me_d, me_s, nd, ns):
    barrier = pltpu.get_barrier_semaphore()

    def seq_hello(k, c):
        pl.semaphore_signal(
            barrier, inc=1, device_id=(me_d, lax.rem(me_s + k, ns)), device_id_type=MESH
        )
        return c

    def dp_hello(k, c):
        pl.semaphore_signal(
            barrier, inc=1, device_id=(lax.rem(me_d + k, nd), me_s), device_id_type=MESH
        )
        return c

    lax.fori_loop(1, ns, seq_hello, 0)
    lax.fori_loop(1, nd, dp_hello, 0)
    return barrier


def peer_at(me_s, i, j, ng, sign):
    group = lax.rem(me_s // 4 + sign * i + ng, ng)
    return 4 * group + lax.rem(me_s % 4 + sign * j + 4, 4)


def whole_kernel(
    nd, ns, ny, nz, tpd,
    x_in, w_in, cot_in, cols_in, counts_in,
    mix_out, gn_out, wg_out,
    cols_ref, cols_vec, counts_ref, mix_ref, gn_ref, wg_ref, x_vm, cot_vm, w_vm, kv_out, kv_in, qd_out, qd_in, natural, xt_own, xt_all,
    chain, row_out, col_out, row_in, col_in,
    raw_even, raw_odd, top_even, top_odd, pair_even, pair_odd,
    table_vm, table, dq, wg_in, part, relay, fold, mid, last_in,
    w_sem, load_sem, kv_s, kv_r, qd_s, qd_r, xt_s, xt_r, row_s, row_r, col_s, col_r,
    own_sem, tile_s, tile_r, relay_s, relay_r, fold_s, fold_r, last_s, last_r, late_s, late_r, share_s, share_r, out_sem,
    zpart, z_in, z_mid, y_in, z_s, z_r, y_s, y_r,
):
    me_d, me_s = lax.axis_index("dp"), lax.axis_index("seq")
    me_y, me_z = me_s // nz, me_s % nz
    ng = ns // 4
    my_group = me_s // 4
    hidden = ng * BLK
    nb = ns
    scale = 1.0 / math.sqrt(FEAT)
    to_exp2 = scale * math.log2(math.e)

    def lanes(t):
        return pl.ds(pl.multiple_of(t * BLK, BLK), BLK)

    def sent_group(i):
        return lax.rem(my_group + i, ng)

    def got_group(i):
        return lax.rem(my_group - i + ng, ng)

    def row_at(k):
        return peer_at(me_s, k // 4, k % 4, ng, -1)

    def remote(src, dst, send_sem, recv_sem, d, s):
        return pltpu.make_async_remote_copy(
            src_ref=src, dst_ref=dst, send_sem=send_sem, recv_sem=recv_sem,
            device_id=(d, s), device_id_type=MESH,
        )

    def landed(ref, sem):
        pltpu.make_async_copy(ref, ref, sem).wait()

    barrier = greet(me_d, me_s, nd, ns)
    load_x = pltpu.make_async_copy(x_in.at[0], x_vm, load_sem.at[0])
    load_cot = pltpu.make_async_copy(cot_in.at[0], cot_vm, load_sem.at[1])
    load_x.start()

    def w_start(part, i):
        g = sent_group(i)
        for m in ((1, 2), (0,))[part]:
            pltpu.make_async_copy(
                w_in.at[:, lanes(m * ng + g)],
                w_vm.at[g, :, pl.ds(m * BLK, BLK)],
                w_sem.at[part, i],
            ).start()

    def kv_weights(i, c):
        w_start(0, i)
        return c

    def q_weights(i, c):
        w_start(1, i)
        return c

    small_loads = [
        pltpu.make_async_copy(src, dst, load_sem.at[2 + n])
        for n, (src, dst) in enumerate(
            ((cols_in, cols_ref), (cols_in.at[0], cols_vec), (counts_in, counts_ref))
        )
    ]
    lax.fori_loop(0, ng, kv_weights, 0)
    load_cot.start()
    lax.fori_loop(0, ng, q_weights, 0)
    for load in small_loads:
        load.start()
    load_x.wait()

    def pieces_copy(out, into, send_sem, recv_sem):
        def copy(i, j):
            peer = peer_at(me_s, i, j, ng, 1)
            return remote(out.at[peer], into.at[me_s], send_sem, recv_sem.at[i], me_d, peer)

        return copy, pltpu.make_async_copy(out.at[me_s], into.at[me_s], recv_sem.at[0])

    kv_copy, own_kv = pieces_copy(kv_out, kv_in, kv_s, kv_r)
    qd_copy, own_qd = pieces_copy(qd_out, qd_in, qd_s, qd_r)

    def start_group(i, own, copy):
        @pl.when(i == 0)
        def _():
            own.start()

        @pl.when(i > 0)
        def _():
            copy(i, 0).start()

        for j in range(1, 4):
            copy(i, j).start()

    def project_kv(i, c):
        g = sent_group(i)
        landed(w_vm.at[g, :, pl.ds(BLK, 2 * BLK)], w_sem.at[0, i])
        flat = jnp.dot(x_vm[...], w_vm[g, :, BLK:], preferred_element_type=F32)
        for m in range(2):
            turned = jnp.transpose(flat[:, m * BLK : (m + 1) * BLK]).astype(BF16)
            for j in range(4):
                kv_out[4 * g + j, m * FEAT : (m + 1) * FEAT] = turned[
                    j * FEAT : (j + 1) * FEAT
                ]

        @pl.when(i == 0)
        def _():
            pl.semaphore_wait(barrier, ns + nd - 2)

        start_group(i, own_kv, kv_copy)
        return c

    def project_q(i, c):
        g = sent_group(i)
        landed(w_vm.at[g, :, pl.ds(0, BLK)], w_sem.at[1, i])
        flat = jnp.dot(x_vm[...], w_vm[g, :, :BLK], preferred_element_type=F32)
        for m, piece in enumerate((flat, cot_vm[:, lanes(g)].astype(F32))):
            turned = jnp.transpose(piece).astype(BF16)
            for j in range(4):
                qd_out[4 * g + j, m * FEAT : (m + 1) * FEAT] = turned[
                    j * FEAT : (j + 1) * FEAT
                ]
        start_group(i, own_qd, qd_copy)
        return c

    lax.fori_loop(0, ng, project_kv, 0)
    load_cot.wait()
    lax.fori_loop(0, ng, project_q, 0)

    xt_own[...] = jnp.transpose(x_vm[...].astype(F32)).astype(BF16)
    xt_keep = pltpu.make_async_copy(xt_own, xt_all.at[:, lanes(me_d)], own_sem.at[0])
    xt_keep.start()

    sibling = me_d + 1 - 2 * (me_d % 2)

    def xt_copy(k):
        return remote(
            xt_own, xt_all.at[:, lanes(me_d)], xt_s, xt_r,
            lax.rem(me_d + 2 * k, nd), me_s,
        )

    def share_copy(k):
        here = lanes(lax.rem(me_d - 2 * k + nd, nd))
        return remote(
            xt_all.at[:, here] if k else xt_own, xt_all.at[:, here],
            share_s, share_r, sibling, me_s,
        )

    for k in range(1, nd // 2):
        xt_copy(k).start()
    share_copy(0).start()

    for load in small_loads:
        load.wait()
    named_now = cols_vec[...]
    row_ids = lane_ids((SLOTS, nb))
    place = 4 * lax.rem(my_group - row_ids // 4 + ng, ng) + lax.rem(
        me_s % 4 - row_ids % 4 + 4, 4
    )
    col_ids = lane_ids((1, nb))

    def link(k, carry):
        before, final = carry
        r = row_at(k)
        for s in range(SLOTS):
            name = cols_ref[0, s, r]
            before = jnp.where((named_now == name) & (place > k), 4 * k + s, before)
            final = jnp.where(col_ids == name, 4 * k + s, final)
        return before, final

    before, final = lax.fori_loop(
        0, nb, link,
        (jnp.full((SLOTS, nb), SLOTS * nb, jnp.int32), jnp.zeros((1, nb), jnp.int32)),
    )
    table_vm[...] = jnp.zeros_like(table_vm)
    table_vm[:SLOTS, :nb] = before
    table_vm[SLOTS : SLOTS + 1, :nb] = final
    table_copy = pltpu.make_async_copy(table_vm, table, own_sem.at[1])
    table_copy.start()
    chain[SLOTS * nb] = jnp.zeros((2 * FEAT, BLK), F32)

    raw, top, pair = (raw_even, raw_odd), (top_even, top_odd), (pair_even, pair_odd)

    def arrive(i, c):
        landed(kv_in.at[pl.ds(0, 4)], kv_r.at[i])
        for j in range(4):
            b = row_at(4 * i + j)
            natural[b] = jnp.transpose(kv_in[b].astype(F32)).astype(BF16)
        return c

    lax.fori_loop(0, ng, arrive, 0)
    table_copy.wait()

    def spread_pieces(r, side):
        queries, cot = qd_in[r, :FEAT], qd_in[r, FEAT:]
        empty = jnp.zeros((FEAT, BLK), BF16)
        upper, lower = [queries, empty], [empty, cot]
        if side:
            upper, lower = upper[::-1], lower[::-1]
        return jnp.concatenate(
            [jnp.concatenate(upper, axis=1), jnp.concatenate(lower, axis=1)], axis=0
        )

    def score_stage(k, p):
        r = row_at(k)
        count = counts_ref[0, r]
        keys = jnp.concatenate([natural[cols_ref[0, s, r]] for s in range(SLOTS)], axis=0)
        both = jnp.dot(keys, spread_pieces(r, 0), preferred_element_type=F32)
        best = None
        for s in range(SLOTS):
            block = both[s * BLK : (s + 1) * BLK]
            scores = block[:, :BLK]
            if s:
                scores = jnp.where(s < count, scores, -jnp.inf)
            raw[p][s, :, :BLK] = scores
            raw[p][s, :, BLK:] = block[:, BLK:]
            peak = jnp.max(scores, axis=0, keepdims=True)
            best = peak if best is None else jnp.maximum(best, peak)
        top[p][...] = best * to_exp2

    def soft_stage(p):
        peak = top[p][...]
        total = mixed = None
        for s in range(SLOTS):
            weights = jnp.exp2(raw[p][s, :, :BLK] * to_exp2 - peak)
            t = jnp.sum(weights, axis=0, keepdims=True)
            m = jnp.sum(weights * raw[p][s, :, BLK:], axis=0, keepdims=True)
            total = t if total is None else total + t
            mixed = m if mixed is None else mixed + m
            raw[p][s, :, :BLK] = weights
        inverse = 1.0 / total
        delta = mixed * inverse
        for s in range(SLOTS):
            prob = raw[p][s, :, :BLK] * inverse
            rows = slice(s * BLK, (s + 1) * BLK)
            pair[p][rows, :BLK] = prob.astype(BF16)
            pair[p][rows, BLK:] = (prob * (raw[p][s, :, BLK:] - delta)).astype(BF16)

    def grad_stage(k, p):
        r = row_at(k)
        named = [cols_ref[0, s, r] for s in range(SLOTS)]
        both = pair[p][...]
        turned = jnp.concatenate([kv_in[n] for n in named], axis=1)
        row_side = jnp.dot(turned, both, preferred_element_type=F32)
        row_out[r, :FEAT] = row_side[FEAT:, :BLK].astype(BF16)
        row_out[r, FEAT:] = (row_side[:FEAT, BLK:] * scale).astype(BF16)
        key_side = lax.dot_general(
            spread_pieces(r, 1), both, (((1,), (1,)), ((), ())), preferred_element_type=F32
        )
        for s in range(SLOTS):
            chain[4 * k + s] = key_side[:, s * BLK : (s + 1) * BLK] + chain[table[s, r]]

    def piece_copy(lo, send_sem, recv_sem):
        def copy(i, j):
            peer = row_at(4 * i + j)
            piece = pl.ds(lo, FEAT)
            return remote(
                row_out.at[peer, piece], row_in.at[me_s, piece],
                send_sem, recv_sem(i), me_d, peer,
            )

        return copy

    late_copy = piece_copy(0, late_s, lambda i: late_r)
    row_copy = piece_copy(FEAT, row_s, lambda i: row_r.at[i])

    def col_copy(i, j):
        peer = peer_at(me_s, i, j, ng, 1)
        return remote(
            col_out.at[peer], col_in.at[me_s], col_s, col_r.at[i], me_d, peer
        )

    def own_piece(lo, sem):
        piece = pl.ds(lo, FEAT)
        return pltpu.make_async_copy(row_out.at[me_s, piece], row_in.at[me_s, piece], sem)

    own_late = own_piece(0, late_r)
    own_row = own_piece(FEAT, row_r.at[0])
    own_col = pltpu.make_async_copy(col_out.at[me_s], col_in.at[me_s], col_r.at[0])
    def one_step(k, p, grad=True):
        score_stage(k + 1, 1 - p)
        soft_stage(p)
        if grad:
            grad_stage(k - 1, 1 - p)

    landed(qd_in.at[pl.ds(0, 4)], qd_r.at[0])
    score_stage(0, 0)
    one_step(0, 0, grad=False)
    one_step(1, 1)
    one_step(2, 0)

    def four_rows(i, c):
        @pl.when(i > 0)
        def _():
            start_group(i - 1, own_row, row_copy)

        landed(qd_in.at[pl.ds(0, 4)], qd_r.at[i + 1])
        for u in range(4):
            one_step(3 + 4 * i + u, (1 + u) % 2)
        return c

    lax.fori_loop(0, ng - 1, four_rows, 0)
    soft_stage(1)
    grad_stage(nb - 2, 0)
    grad_stage(nb - 1, 1)

    def col_send(i, c):
        for j in range(4):
            peer = peer_at(me_s, i, j, ng, 1)
            total = chain[table[SLOTS, peer]]
            col_out[peer, :FEAT] = (total[:FEAT] * scale).astype(BF16)
            col_out[peer, FEAT:] = total[FEAT:].astype(BF16)
        start_group(i, own_col, col_copy)
        return c

    lax.fori_loop(0, ng // 2, col_send, 0)
    start_group(ng - 2, own_row, row_copy)
    start_group(ng - 1, own_row, row_copy)
    lax.fori_loop(ng // 2, ng, col_send, 0)
    own_late.start()
    others = nd // 2 - 1
    if others:
        landed(xt_all.at[:, pl.ds(0, others * BLK)], xt_r)
    for k in range(1, nd // 2):
        share_copy(k).start()

    def late_send(i, c):
        @pl.when(i > 0)
        def _():
            late_copy(i, 0).start()

        for j in range(1, 4):
            late_copy(i, j).start()
        return c


    def tile_own(g, m):
        t = m * ng + g
        return pltpu.make_async_copy(
            dq.at[g, pl.ds(m * BLK, BLK)], wg_in.at[lanes(t % tpd), lanes(me_d)],
            tile_r.at[t % tpd],
        )

    def tile_copy(g, m):
        t = m * ng + g
        return remote(
            dq.at[g, pl.ds(m * BLK, BLK)], wg_in.at[lanes(t % tpd), lanes(me_d)],
            tile_s, tile_r.at[t % tpd], t // tpd, me_s,
        )

    def tile_send(g, m):
        t = m * ng + g

        @pl.when(t // tpd == me_d)
        def _():
            tile_own(g, m).start()

        @pl.when(t // tpd != me_d)
        def _():
            tile_copy(g, m).start()

    def take_rows(i, c):
        g = sent_group(i)
        landed(row_in.at[pl.ds(0, 4), pl.ds(FEAT, FEAT)], row_r.at[i])
        for j in range(4):
            dq[g, j * FEAT : (j + 1) * FEAT] = row_in[4 * g + j, FEAT:]
        tile_send(g, 0)
        return c

    def take_late(g, c):
        mix = jnp.concatenate([row_in[4 * g + j, :FEAT] for j in range(4)], axis=0)
        mix_ref[:, lanes(g)] = jnp.transpose(mix.astype(F32)).astype(BF16)
        return c

    def take_cols(i, c):
        g = got_group(i)
        landed(col_in.at[pl.ds(0, 4)], col_r.at[i])
        for j in range(4):
            dq[g, BLK + j * FEAT : BLK + (j + 1) * FEAT] = col_in[4 * g + j, :FEAT]
            dq[g, 2 * BLK + j * FEAT : 2 * BLK + (j + 1) * FEAT] = col_in[4 * g + j, FEAT:]
        tile_send(g, 1)
        tile_send(g, 2)
        return c

    def bring_home(i, c):
        late_send(i, 0)
        take_rows(i, 0)
        return take_cols(i, c)

    lax.fori_loop(0, ng, bring_home, 0)
    xt_keep.wait()
    landed(xt_all.at[:, pl.ds(0, nd // 2 * BLK)], share_r)

    chunk = nz * FEAT
    half = chunk // 2
    up, down = lax.rem(me_y + 1, ny), lax.rem(me_y + ny - 1, ny)
    across = lax.rem(me_y + 2, ny)

    def rows_of(y, which):
        return pl.ds(pl.multiple_of(y * chunk + which * half, half), half)

    def relay_copy(t, way):
        return remote(
            part.at[t, rows_of(across, way)], relay.at[t, way],
            relay_s, relay_r.at[t], me_d, (up, down)[way] * nz + me_z,
        )

    def fold_copy(t, way, which):
        return remote(
            part.at[t, rows_of((up, down)[way], which)], fold.at[t, way, which],
            fold_s, fold_r.at[t],
            me_d, (up, down)[way] * nz + me_z,
        )

    def last_copy(k):
        to = lax.rem(me_z + k, nz)
        return remote(
            mid.at[pl.ds(pl.multiple_of(to * FEAT, FEAT), FEAT)], last_in.at[k - 1],
            last_s, last_r, me_d, me_y * nz + to,
        )

    def z_copy(k):
        to = lax.rem(me_z + k, nz)
        return remote(zpart.at[:, to], z_in.at[k - 1], z_s, z_r, me_d, me_y * nz + to)

    def y_copy(k):
        to = lax.rem(me_y + k, ny)
        return remote(z_mid.at[to], y_in.at[k - 1], y_s, y_r, me_d, to * nz + me_z)

    far_first = sorted(range(1, nz), key=lambda k: -min(k, nz - k))
    pairs = tpd - 1
    for t in range(tpd):
        landed(wg_in.at[pl.ds(t * BLK, BLK)], tile_r.at[t])

    def contract(rows, first, last):
        return lax.dot_general(
            xt_all[rows, :], wg_in[first * BLK : last * BLK], (((1,), (1,)), ((), ())),
            preferred_element_type=F32,
        ).astype(BF16)

    def fill(y):
        rows = pl.ds(pl.multiple_of(y * chunk, chunk), chunk)
        value = contract(rows, 0, pairs)
        for t in range(pairs):
            part[t, rows] = value[:, t * BLK : (t + 1) * BLK]

    fill(across)
    for t in range(pairs):
        for way in range(2):
            relay_copy(t, way).start()
    zpart[...] = contract(slice(None), pairs, tpd).reshape(ny, nz, FEAT, BLK)
    for k in far_first:
        z_copy(k).start()
    fill(up)
    fill(down)
    for t in range(pairs):
        for way in range(2):
            fold_copy(t, way, 1 - way).start()
    fill(me_y)

    def node_cols(n, c):
        width = 2 * BLK
        cols = pl.ds(pl.multiple_of(n * width, width), width)
        total = jnp.zeros((width, BLK), F32)
        for g in range(ng):
            total += jnp.dot(w_vm[g, cols], dq[g], preferred_element_type=F32)
        gn_ref[:, cols] = jnp.transpose(total).astype(BF16)
        return c

    steps_gn = hidden // (2 * BLK)
    lax.fori_loop(0, steps_gn // 4, node_cols, 0)
    for t in range(pairs):
        landed(relay.at[t], relay_r.at[t])
        for way in range(2):
            rows = rows_of((up, down)[way], way)
            part[t, rows] = (
                part[t, rows].astype(F32) + relay[t, way].astype(F32)
            ).astype(BF16)
            fold_copy(t, way, way).start()
    lax.fori_loop(steps_gn // 4, steps_gn // 2, node_cols, 0)
    for t in range(pairs):
        landed(fold.at[t], fold_r.at[t])
        for which in range(2):
            total = part[t, rows_of(me_y, which)].astype(F32)
            for way in range(2):
                total += fold[t, way, which].astype(F32)
            mid[which * half : (which + 1) * half, t * BLK : (t + 1) * BLK] = total.astype(BF16)
    for k in far_first:
        last_copy(k).start()
    lax.fori_loop(steps_gn // 2, 3 * steps_gn // 4, node_cols, 0)
    landed(z_in, z_r)
    total = zpart[:, me_z].astype(F32)
    for k in range(1, nz):
        total += z_in[k - 1].astype(F32)
    z_mid[...] = total.astype(BF16)
    for k in range(1, ny):
        y_copy(k).start()
    lax.fori_loop(3 * steps_gn // 4, steps_gn, node_cols, 0)
    gn_done = pltpu.make_async_copy(gn_ref, gn_out, out_sem.at[1])
    gn_done.start()

    landed(row_in.at[:, pl.ds(0, FEAT)], late_r)
    lax.fori_loop(0, ng, take_late, 0)
    mix_done = pltpu.make_async_copy(mix_ref, mix_out, out_sem.at[0])
    mix_done.start()
    landed(kv_out.at[pl.ds(0, ns - 1)], kv_s)
    landed(qd_out.at[pl.ds(0, ns - 1)], qd_s)
    if others:
        landed(xt_all.at[:, pl.ds(0, others * BLK)], xt_s)
    landed(xt_all.at[:, pl.ds(0, nd // 2 * BLK)], share_s)
    landed(row_out.at[pl.ds(0, ns - 1), pl.ds(FEAT, FEAT)], row_s)
    landed(row_out.at[pl.ds(0, ns - 1), pl.ds(0, FEAT)], late_s)
    landed(col_out.at[pl.ds(0, ns - 1)], col_s)
    landed(dq.at[pl.ds(0, ng - 1)], tile_s)
    landed(relay, relay_s)
    landed(fold, fold_s)
    landed(last_in, last_r)
    total = mid[pl.ds(pl.multiple_of(me_z * FEAT, FEAT), FEAT)].astype(F32)
    for k in range(1, nz):
        total += last_in[k - 1].astype(F32)
    wg_ref[:, : pairs * BLK] = total
    landed(y_in, y_r)
    total = z_mid[me_y].astype(F32)
    for k in range(1, ny):
        total += y_in[k - 1].astype(F32)
    wg_ref[:, pairs * BLK :] = total
    wg_done = pltpu.make_async_copy(wg_ref, wg_out, out_sem.at[2])
    wg_done.start()
    landed(last_in, last_s)
    landed(z_in, z_s)
    landed(y_in, y_s)
    mix_done.wait()
    gn_done.wait()
    wg_done.wait()


def settle_kernel(mix_in, gn_in, wg_in, mix_out, gn_out, wg_out, mix_vm, gn_vm, wg_vm, sem):
    triples = ((mix_in, mix_vm, mix_out), (gn_in, gn_vm, gn_out), (wg_in, wg_vm, wg_out))
    loads = [pltpu.make_async_copy(a, b, sem.at[0, n]) for n, (a, b, _) in enumerate(triples)]
    stores = [pltpu.make_async_copy(b, c, sem.at[1, n]) for n, (_, b, c) in enumerate(triples)]
    for load in loads:
        load.start()
    for load, store in zip(loads, stores):
        load.wait()
        store.start()
    for store in stores:
        store.wait()


def per_device(nd, ns, nodes, w_qkv, incoming_adjoint, block_cols, block_counts):
    rows, hidden = nodes.shape[1:]
    ny, nz = 4, ns // 4
    ng = ns // 4
    tpd = 3 * ng // nd
    chunk = nz * FEAT
    any_spec = pl.BlockSpec(memory_space=pl.ANY)
    dma = pltpu.SemaphoreType.DMA
    slots_first = jnp.swapaxes(block_cols, 1, 2)
    out_shape = (
        jax.ShapeDtypeStruct((rows, hidden), BF16),
        jax.ShapeDtypeStruct((rows, hidden), BF16),
        jax.ShapeDtypeStruct((FEAT, tpd * BLK), F32),
    )
    out_buffers = [pltpu.VMEM(out.shape, out.dtype) for out in out_shape]
    results = pl.pallas_call(
        functools.partial(whole_kernel, nd, ns, ny, nz, tpd),
        out_shape=out_shape,
        in_specs=[any_spec] * 5,
        out_specs=(any_spec,) * 3,
        scratch_shapes=[
            pltpu.SMEM((1, SLOTS, ns), jnp.int32),
            pltpu.VMEM((SLOTS, ns), jnp.int32),
            pltpu.SMEM((1, ns), jnp.int32),
            *out_buffers,
            pltpu.VMEM((rows, hidden), BF16),
            pltpu.VMEM((rows, hidden), BF16),
            pltpu.VMEM((ng, hidden, 3 * BLK), BF16),
            pltpu.VMEM((ns, 2 * FEAT, BLK), BF16),
            pltpu.VMEM((ns, 2 * FEAT, BLK), BF16),
            pltpu.VMEM((ns, 2 * FEAT, BLK), BF16),
            pltpu.VMEM((ns, 2 * FEAT, BLK), BF16),
            pltpu.VMEM((ns, BLK, 2 * FEAT), BF16),
            pltpu.VMEM((hidden, BLK), BF16),
            pltpu.VMEM((hidden, nd * BLK), BF16),
            pltpu.VMEM((SLOTS * ns + 1, 2 * FEAT, BLK), F32),
            pltpu.VMEM((ns, 2 * FEAT, BLK), BF16),
            pltpu.VMEM((ns, 2 * FEAT, BLK), BF16),
            pltpu.VMEM((ns, 2 * FEAT, BLK), BF16),
            pltpu.VMEM((ns, 2 * FEAT, BLK), BF16),
            pltpu.VMEM((SLOTS, BLK, 2 * BLK), F32),
            pltpu.VMEM((SLOTS, BLK, 2 * BLK), F32),
            pltpu.VMEM((1, BLK), F32),
            pltpu.VMEM((1, BLK), F32),
            pltpu.VMEM((SLOTS * BLK, 2 * BLK), BF16),
            pltpu.VMEM((SLOTS * BLK, 2 * BLK), BF16),
            pltpu.VMEM((8, BLK), jnp.int32),
            pltpu.SMEM((8, BLK), jnp.int32),
            pltpu.VMEM((ng, 3 * BLK, BLK), BF16),
            pltpu.VMEM((tpd * BLK, nd * BLK), BF16),
            pltpu.VMEM((tpd - 1, hidden, BLK), BF16),
            pltpu.VMEM((tpd - 1, 2, chunk // 2, BLK), BF16),
            pltpu.VMEM((tpd - 1, 2, 2, chunk // 2, BLK), BF16),
            pltpu.VMEM((chunk, (tpd - 1) * BLK), BF16),
            pltpu.VMEM((nz - 1, FEAT, (tpd - 1) * BLK), BF16),
            dma((2, ng)),
            dma((5,)),
            dma,
            dma((ng,)),
            dma,
            dma((ng,)),
            dma,
            dma,
            dma,
            dma((ng,)),
            dma,
            dma((ng,)),
            dma((2,)),
            dma,
            dma((tpd,)),
            dma,
            dma((tpd,)),
            dma,
            dma((tpd,)),
            dma,
            dma,
            dma,
            dma,
            dma,
            dma,
            dma((3,)),
            pltpu.VMEM((ny, nz, FEAT, BLK), BF16),
            pltpu.VMEM((nz - 1, ny, FEAT, BLK), BF16),
            pltpu.VMEM((ny, FEAT, BLK), BF16),
            pltpu.VMEM((ny - 1, FEAT, BLK), BF16),
            dma,
            dma,
            dma,
            dma,
        ],
        compiler_params=pltpu.CompilerParams(
            collective_id=1, has_side_effects=True, vmem_limit_bytes=VMEM_LIMIT
        ),
        name="whole",
    )(nodes, w_qkv, incoming_adjoint, slots_first, block_counts)
    mixture, grad_nodes, weight_grad = pl.pallas_call(
        settle_kernel,
        out_shape=out_shape,
        in_specs=[any_spec] * 3,
        out_specs=(any_spec,) * 3,
        scratch_shapes=[*out_buffers, dma((2, 3))],
        compiler_params=pltpu.CompilerParams(vmem_limit_bytes=VMEM_LIMIT),
        name="settle",
    )(*results)
    return (mixture[None], grad_nodes[None], jnp.transpose(weight_grad))


def solution(mesh):
    nd, ns = mesh.shape["dp"], mesh.shape["seq"]
    in_specs = (P("dp", "seq", None), P(), P("dp", "seq", None), P("dp", None, None), P("dp", None))
    out_specs = (P("dp", "seq", None), P("dp", "seq", None), P("dp", "seq"))
    return jax.shard_map(
        functools.partial(per_device, nd, ns),
        mesh=mesh,
        in_specs=in_specs,
        out_specs=out_specs,
        check_vma=False,
    )
```
